512 devices in a mesh: grp: 8 (over z), seg: 64 (over x, y, core).
Axes of the slice: x: 4, y: 8, z: 8, core: 2. Of those that a mesh axis runs over, the one named last changes fastest.
Arguments:
- bricks: bfloat16 [28, 3072, 512], P(None, 'seg'), may hold values from -6 to 6
- requests: int32 [64, 8, 64, 2], P('seg', 'grp'), may hold values from 0 to 47
- seg_owner: int32 [64, 1024, 1], P('seg', 'grp'), may hold values from 0 to 63; in each aligned block of 128 rows (0 to 127, 128 to 255, ..., all dimensions but the last counted through in order) at most 4 rows name the same one
- seg_slot: int32 [64, 1024], P('seg', 'grp'), may hold values from 0 to 1
- sample_cells: int32 [16, 64, 1024], P(None, 'seg', 'grp'), may hold values from 0 to 342
- sample_fracs: float32 [3, 16, 64, 1024], P(None, None, 'seg', 'grp'), may hold values from 0 to 1
- ray_angles: float32 [2, 1024], P(None, 'grp'), may hold values from -3.140625 to 3.140625
- ray_step: float32 [1024], P('grp'), may hold values from 0.0003 to 0.003
- pixel_target: float32 [3, 1024], P(None, 'grp'), may hold values from 0 to 1
Outputs:
- gradients: float32 [28, 3072, 512], P(None, 'seg')
- colour: float32 [3, 1024], P(None, 'grp')
The draws below stay inside these ranges and needn't reach their ends.
Inputs may be any that keep to these rules, and one draw needn't show every extreme that they name: `seg_owner`: among the rays of one device, at most 4 segments name the same owner, a bound that some block reaches of them. `requests`: indices may repeat.
All inputs are finite; a program needn't handle non-finite values.
Results may differ from the reference program's by a relative error of at most 0.0003.
Values may be sent and summed in bfloat16 or wider, within the bound.
A program may use at most 128 MiB of HBM per device.

```python
import math
import jax
import jax.numpy as jnp
import numpy as np
from jax import lax

COEF = 28
VOXELS = 512
SAMP = 16
CAP = 2
B_DEV = 48
RAYS_DEV = 128
SEGS = 64
RAYS = 1024
BRICKS = 3072
SEGCAP = 4
N_GRP = 8


def touch_ends(values, key, least, largest):
    shape = values.shape
    index_at = [jax.random.randint(jax.random.fold_in(key, axis), (), 0, shape[axis]) for axis in range(len(shape))]
    values = values.at[tuple(index_at)].set(least)
    longest = shape.index(max(shape))
    index_at[longest] = (index_at[longest] + 1) % shape[longest]
    return values.at[tuple(index_at)].set(largest)


def shard_levels(rng, dims, split, smallest, top_value):
    gain, own = 1.0, jax.random.fold_in(rng, 6)
    for dim, shards_of in split:
        draws = jnp.exp(jax.random.uniform(jax.random.fold_in(own, dim), (shards_of,), jnp.float32, smallest / len(split), top_value / len(split)))
        gain = gain * jnp.repeat(draws, dims[dim] // shards_of).reshape([-1 if axis == dim else 1 for axis in range(len(dims))])
    return gain


def deal_out(stream_key, own, number, rows, amount, top, limit, slope):
    order = jax.random.permutation(stream_key, amount)
    heavy_load, ordinary = portions_of(amount, rows * top, limit, slope, True), portions_of(amount, rows * top, limit, slope, False)
    places = jnp.arange(amount)

    def named(tallies, turn):
        used = int((tallies > 0).sum())
        fixed = max(1, used // 4)
        moved = fixed + (places - fixed + turn * (used - fixed)) % max(1, amount - fixed)
        return jnp.zeros((amount,), jnp.int32).at[order[jnp.where(places < fixed, places, moved)]].set(jnp.asarray(tallies, jnp.int32))

    tallies = jnp.where(number % 4 == 0, named(heavy_load, number // 4), named(ordinary, number - number // 4 - 1))
    mixed = jax.random.permutation(jax.random.fold_in(own, 3), amount)
    giver, sink = mixed[0:amount // 2 * 2:2], mixed[1:amount // 2 * 2:2]
    margin = jnp.minimum(tallies[giver] - 1, limit - tallies[sink]) // 2
    margin = jnp.where((giver == order[0]) | (sink == order[0]) | (tallies[sink] == 0), 0, jnp.maximum(margin, 0))
    moved = jax.random.randint(jax.random.fold_in(own, 4), (amount // 2,), 0, 1 << 20) % (margin + 1)
    tallies = tallies.at[giver].add(-moved).at[sink].add(moved)
    labels = jnp.searchsorted(jnp.cumsum(tallies), jnp.arange(rows * top), side="right").astype(jnp.int32)
    table = labels.reshape(top, rows).T
    table = table[jax.random.permutation(jax.random.fold_in(own, 1), rows)]
    turn = jax.random.randint(jax.random.fold_in(own, 2), (rows, 1), 0, top)
    return jnp.take_along_axis(table, (jnp.arange(top)[None, :] + turn) % top, axis=1)


def portions_of(number_of, total, most, skew, full):
    portions = [(1 << 20) // math.isqrt(grade ** skew) + 1 for grade in range(1, number_of + 1)]
    largest = most if full else min(most, max(-(-total // number_of), total * portions[0] // sum(portions)))
    least = 1 if total - largest >= number_of - 1 else 0
    counts, spare = [largest] + [least] * (number_of - 1), total - largest - least * (number_of - 1)
    while spare > 0:
        free = [i for i in range(1, number_of) if counts[i] < largest] or [i for i in range(1, number_of) if counts[i] < most]
        whole, remaining = sum([portions[i] for i in free]), spare
        for i in free:
            more = min(most - counts[i], max(1, remaining * portions[i] // whole), spare)
            counts[i] = counts[i] + more
            spare = spare - more
    return np.array(counts)


def scatter_about(stream_key, dims, width, reach, shards=(), kind=jnp.bfloat16):
    drawn = width * jax.random.normal(stream_key, dims, jnp.float32)
    if shards:
        drawn = drawn * shard_levels(stream_key, dims, shards, -0.22, 0.18)
    return jnp.clip(drawn, -reach, reach).astype(kind)


def setup_inputs(seed: int = 0) -> dict:
    seeds = jax.random.split(jax.random.key(seed), 10)
    bricks = scatter_about(seeds[0], (COEF, BRICKS, VOXELS), 1.0, 6.0, ((1, 64),))
    requests = touch_ends(jax.random.randint(seeds[1], (SEGS, N_GRP, SEGS, CAP), 0, B_DEV), jax.random.fold_in(seeds[1], 1), 0, B_DEV - 1).astype(jnp.int32)
    seg_owner_keys = jax.random.split(jax.random.fold_in(seeds[2], 1), SEGS * RAYS // RAYS_DEV)
    seg_owner_turns = jax.random.permutation(jax.random.fold_in(seeds[2], 3), SEGS * RAYS // RAYS_DEV)
    seg_owner = jax.vmap(lambda own, number: deal_out(jax.random.fold_in(seeds[2], 2), own, number, RAYS_DEV, SEGS, 1, SEGCAP, 2))(seg_owner_keys, seg_owner_turns).reshape((SEGS, RAYS, 1))
    seg_slot = touch_ends(jax.random.randint(seeds[3], (SEGS, RAYS), 0, CAP), jax.random.fold_in(seeds[3], 1), 0, CAP - 1).astype(jnp.int32)
    sample_cells = touch_ends(jax.random.randint(seeds[4], (SAMP, SEGS, RAYS), 0, 343), jax.random.fold_in(seeds[4], 1), 0, 342).astype(jnp.int32)
    sample_fracs = jnp.clip(1.0 * jax.random.uniform(seeds[5], (3, SAMP, SEGS, RAYS), jnp.float32) ** shard_levels(seeds[5], (3, SAMP, SEGS, RAYS), ((2, 64), (3, 8)), -0.2, 0.2), 0.0, 1.0)
    ray_angles = jnp.clip(jax.random.uniform(seeds[6], (2, RAYS), jnp.float32, -3.140625, 3.140625), -3.140625, 3.140625)
    ray_step = jnp.clip(jnp.exp(math.log(0.003) - 2.3025851 * jax.random.uniform(seeds[7], (RAYS,), jnp.float32) ** shard_levels(seeds[7], (RAYS,), ((0, 8),), -0.2, 0.2)), 0.0003, 0.003)
    pixel_target = jnp.clip(1.0 * jax.random.uniform(seeds[8], (3, RAYS), jnp.float32) ** shard_levels(seeds[8], (3, RAYS), ((1, 8),), -0.2, 0.2), 0.0, 1.0)
    return dict(bricks=bricks, requests=requests, seg_owner=seg_owner, seg_slot=seg_slot, sample_cells=sample_cells, sample_fracs=sample_fracs, ray_angles=ray_angles, ray_step=ray_step, pixel_target=pixel_target)


loss_scale = 1024.0

def harmonics(ray_angles):
    polar = ray_angles[0]
    azimuth = ray_angles[1]
    coord_x = jnp.sin(polar) * jnp.cos(azimuth)
    coord_y = jnp.sin(polar) * jnp.sin(azimuth)
    coord_z = jnp.cos(polar)
    return jnp.stack([0.28209479 * jnp.ones_like(coord_x), -0.48860251 * coord_y, 0.48860251 * coord_z, -0.48860251 * coord_x, 1.09254843 * coord_x * coord_y, -1.09254843 * coord_y * coord_z, 0.31539157 * (2.0 * coord_z * coord_z - coord_x * coord_x - coord_y * coord_y), -1.09254843 * coord_x * coord_z, 0.54627422 * (coord_x * coord_x - coord_y * coord_y)])

def corners(brick_ids, cell_ids, fraction):
    cell_x = cell_ids // 49
    cell_y = cell_ids // 7 % 7
    cell_z = cell_ids % 7
    base = brick_ids[None, :] * 512 + cell_x * 64 + cell_y * 8 + cell_z
    corner_ids = []
    weights = []
    for corner in range(8):
        along_x = corner // 4
        along_y = corner // 2 % 2
        along_z = corner % 2
        corner_ids.append(base + (along_x * 64 + along_y * 8 + along_z))
        weight_x = fraction[0] if along_x else 1.0 - fraction[0]
        weight_y = fraction[1] if along_y else 1.0 - fraction[1]
        weight_z = fraction[2] if along_z else 1.0 - fraction[2]
        weights.append(weight_x * weight_y * weight_z)
    return (jnp.stack(corner_ids).astype(jnp.int32), jnp.stack(weights))

def shade(corner_vals, weights, basis_rows, step_len):
    coefficient = lax.optimization_barrier(jnp.sum(corner_vals * weights[None], axis=1))
    optical = jax.nn.softplus(coefficient[0]) * step_len[None]
    shaped = coefficient[1:].reshape(3, 9, coefficient.shape[1], coefficient.shape[2])
    logits = lax.optimization_barrier(jnp.sum(shaped * basis_rows[None, :, None, :], axis=1))
    radiance = jax.nn.sigmoid(logits)
    before = jnp.cumsum(optical, axis=0) - optical
    seg_colour = lax.optimization_barrier(jnp.sum(jnp.exp(-before)[None] * (1.0 - jnp.exp(-optical))[None] * radiance, axis=1))
    depth_total = lax.optimization_barrier(jnp.sum(optical, axis=0))
    return (seg_colour, depth_total)

def reference(bricks, requests, seg_owner, seg_slot, sample_cells, sample_fracs, ray_angles, ray_step, pixel_target):
    brick_table = bricks.reshape(COEF, BRICKS * VOXELS)
    basis_rows = harmonics(ray_angles)
    ray_group = (jnp.arange(RAYS, dtype=jnp.int32) // RAYS_DEV).astype(jnp.int32)

    def sampled(depth_index):
        owners = seg_owner[depth_index, :, 0]
        chosen = seg_slot[depth_index]
        local_brick = requests[depth_index][ray_group, owners, chosen]
        brick_ids = (owners * B_DEV + local_brick).astype(jnp.int32)
        corner_ids, weights = corners(brick_ids, sample_cells[:, depth_index], sample_fracs[:, :, depth_index])
        corner_vals = brick_table[:, corner_ids].astype(jnp.float32)
        return (corner_ids, corner_vals, weights)

    def forward(depth_index):
        corner_ids, corner_vals, weights = sampled(depth_index)
        return shade(corner_vals, weights, basis_rows, ray_step)
    depth_ids = jnp.arange(SEGS, dtype=jnp.int32)
    seg_colour, seg_tau = lax.map(forward, depth_ids)
    prefix = jnp.cumsum(seg_tau, axis=0) - seg_tau
    attenuation = jnp.exp(-prefix)
    contrib = attenuation[:, None] * seg_colour
    colour = lax.optimization_barrier(jnp.sum(contrib, axis=0))
    suffix = jnp.flip(jnp.cumsum(jnp.flip(contrib, 0), axis=0), 0) - contrib
    misfit = loss_scale * (colour - pixel_target)
    grad_colour = attenuation[:, None] * misfit[None]
    grad_tau = -lax.optimization_barrier(jnp.sum(misfit[None] * suffix, axis=1))

    def backward(total, depth_index):
        corner_ids, corner_vals, weights = sampled(depth_index)

        def local_shade(values):
            return shade(values, weights, basis_rows, ray_step)
        unused, pullback = jax.vjp(local_shade, corner_vals)
        grad_vals, = pullback((grad_colour[depth_index], grad_tau[depth_index]))
        return (total.at[:, corner_ids].add(grad_vals), None)
    gradients, unused = lax.scan(backward, jnp.zeros((COEF, BRICKS * VOXELS), jnp.float32), depth_ids)
    return (gradients.reshape(COEF, BRICKS, VOXELS), colour)
```

```python
import functools

import jax
import jax.numpy as jnp
from jax import lax
from jax.experimental import pallas as pl
from jax.experimental.pallas import tpu as pltpu
from jax.sharding import PartitionSpec as P

COEF = 28
VOXELS = 512
SAMP = 16
OWNERS = 64
GROUPS = 8
SLOTS = 4
BRICKS = 48
RAYS = 128
CHUNKS = OWNERS * SLOTS // 8
ALL_CHUNKS = GROUPS * CHUNKS
TABLE = 384
UNROLL = 4
LOSS_SCALE = 1024.0
F32 = jnp.float32
BF16 = jnp.bfloat16
I32 = jnp.int32
VMEM = pl.BlockSpec(memory_space=pltpu.VMEM)
ANY = pl.BlockSpec(memory_space=pl.ANY)
MESH = pl.DeviceIdType.MESH
NN = (((1,), (0,)), ((), ()))
NT = (((1,), (1,)), ((), ()))


def iota(shape, dim):
    return lax.broadcasted_iota(I32, shape, dim)


def exact_dot(a, b, dims=NN):
    return lax.dot_general(
        a, b, dims, precision=lax.Precision.HIGHEST, preferred_element_type=F32
    )


def fast_dot(a, b, dims=NN):
    return lax.dot_general(a, b, dims, preferred_element_type=F32)


def split(value):
    high = value.astype(BF16)
    return high, (value - high.astype(F32)).astype(BF16)


def hat(place):
    return jnp.maximum(1.0 - jnp.abs(place - iota((8, 128), 0).astype(F32)), 0.0)


def softplus(value):
    return jnp.maximum(value, 0.0) + jnp.log1p(jnp.exp(-jnp.abs(value)))


def sigmoid(value):
    return 1.0 / (1.0 + jnp.exp(-value))


def ray_basis(angles):
    polar = angles[0:1]
    azimuth = angles[1:2]
    x = jnp.sin(polar) * jnp.cos(azimuth)
    y = jnp.sin(polar) * jnp.sin(azimuth)
    z = jnp.cos(polar)
    return [
        0.28209479 * jnp.ones_like(x),
        -0.48860251 * y,
        0.48860251 * z,
        -0.48860251 * x,
        1.09254843 * x * y,
        -1.09254843 * y * z,
        0.31539157 * (2.0 * z * z - x * x - y * y),
        -1.09254843 * x * z,
        0.54627422 * (x * x - y * y),
    ]


def pack(owner, slot, wanted, cells, fracs, basis, step):
    mine = owner == iota((OWNERS, RAYS), 0)
    ones = jnp.where(mine, 1.0, 0.0)
    upper = jnp.where(iota((RAYS, RAYS), 0) < iota((RAYS, RAYS), 1), 1.0, 0.0)
    earlier = fast_dot(ones.astype(BF16), upper.astype(BF16))
    rank = jnp.sum(ones * earlier, axis=0, keepdims=True)
    named = wanted.astype(F32)
    brick = jnp.sum(
        ones * jnp.where(slot == 0, named[:, 0:1], named[:, 1:2]), axis=0, keepdims=True
    )
    choice = jnp.concatenate(
        [jnp.where(rank == float(j), ones, 0.0) for j in range(SLOTS)], axis=1
    )
    cell_x = (cells * 1338) >> 16
    rest = cells - cell_x * 49
    cell_y = (rest * 9363) >> 16
    cell_z = rest - cell_y * 7
    place_x = cell_x.astype(F32) + fracs[0:16]
    place_y = cell_y.astype(F32) + fracs[16:32]
    place_z = cell_z.astype(F32) + fracs[32:48]
    row = iota((SAMP, RAYS), 0)
    extra = jnp.where(row == 11, 1.0, 0.0)
    for k, value in enumerate(basis + [step, brick + 1.0]):
        extra = jnp.where(row == k, value, extra)
    none = jnp.zeros((SAMP, RAYS), F32)

    def placed(first, second):
        parts = []
        for j in range(SLOTS):
            rows = [none] * 8
            rows[j] = first
            rows[4 + j] = second
            parts.append(jnp.concatenate(rows, axis=0))
        return jnp.concatenate(parts, axis=1)

    return (
        choice,
        exact_dot(choice, placed(place_x, place_y), NT),
        exact_dot(choice, placed(place_z, extra), NT),
    )


def greet(axes):
    barrier = pltpu.get_barrier_semaphore()
    total = 0
    for axis, count in axes:
        me = lax.axis_index(axis)

        def hail(turn, carry, axis=axis, count=count, me=me):
            pl.semaphore_signal(
                barrier,
                inc=1,
                device_id={axis: lax.rem(me + turn, count)},
                device_id_type=MESH,
            )
            return carry

        lax.fori_loop(1, count, hail, 0)
        total += count - 1
    pl.semaphore_wait(barrier, total)


def send_all(axis, count, source, target, send_sem, recv_sem):
    me = lax.axis_index(axis)

    def one(turn, carry):
        peer = lax.rem(me + turn, count)
        pltpu.make_async_remote_copy(
            src_ref=source(peer),
            dst_ref=target.at[me],
            send_sem=send_sem,
            recv_sem=recv_sem,
            device_id={axis: peer},
            device_id_type=MESH,
        ).start()
        return carry

    lax.fori_loop(1, count, one, 0)


def wait_all(target, count, sem):
    part = target.at[pl.ds(0, count - 1)]
    pltpu.make_async_copy(part, part, sem).wait()


def dispatch_kernel(
    owner_ref, slot_ref, wanted_ref, cells_ref, fracs_ref, angles_ref, step_ref,
    got_ref, choice_ref, out_ref, send_sem, recv_sem,
):
    greet([("seg", OWNERS)])
    choice, first, second = pack(
        owner_ref[...], slot_ref[...], wanted_ref[...], cells_ref[...], fracs_ref[...],
        ray_basis(angles_ref[...]), step_ref[...],
    )
    choice_ref[...] = choice
    out_ref[:, 0, :] = first
    out_ref[:, 1, :] = second
    me = lax.axis_index("seg")
    send_all("seg", OWNERS, lambda peer: out_ref.at[peer], got_ref, send_sem, recv_sem)
    got_ref[me] = out_ref[me]
    wait_all(got_ref, OWNERS, recv_sem)
    wait_all(out_ref, OWNERS, send_sem)


def dispatch(owner, slot, wanted, cells, fracs, angles, step):
    return pl.pallas_call(
        dispatch_kernel,
        out_shape=(
            jax.ShapeDtypeStruct((OWNERS, 2, 128), F32),
            jax.ShapeDtypeStruct((OWNERS, SLOTS * RAYS), F32),
        ),
        in_specs=[VMEM] * 7,
        out_specs=(VMEM, VMEM),
        scratch_shapes=[
            pltpu.VMEM((OWNERS, 2, 128), F32),
            pltpu.SemaphoreType.DMA,
            pltpu.SemaphoreType.DMA,
        ],
        compiler_params=pltpu.CompilerParams(
            collective_id=0, has_side_effects=True, vmem_limit_bytes=32 << 20
        ),
        name="dispatch",
    )(owner, slot, wanted, cells, fracs, angles, step)


def lane_group_sum():
    return jnp.where(iota((128, 128), 0) // 16 == iota((128, 128), 1) // 16, 1.0, 0.0)


def basis_rows(extra_row, group_sum):
    c = iota((32, 128), 0)
    k = lax.rem(c - 1 + 9, 9)
    wanted = jnp.where(c == 0, 11, jnp.where(c < COEF, k, 15))
    chosen = jnp.where(iota((32, 128), 1) % 16 == wanted, extra_row, 0.0)
    high, low = split(chosen)
    both = fast_dot(jnp.concatenate([high, low], axis=0), group_sum)
    return both[0:32] + both[32:64]


def forward_kernel(
    bricks_ref, got_ref, tiles_ref, sums_ref,
    wide_ref, brick_ref, half_ref, id_vmem, id_smem, place_ref, raw_ref, sem,
):
    wide_ref[...] = jnp.zeros_like(wide_ref)
    for c in range(COEF):
        for x in range(4):
            wide_ref[x, pl.ds(c, BRICKS, stride=32), :] = bricks_ref[
                c, :, x * 128 : x * 128 + 128
            ].astype(F32)

    def narrow(b, carry):
        rows = pl.ds(pl.multiple_of(b * 32, 32), 32)
        for x in range(4):
            brick_ref[rows, x * 128 : x * 128 + 128] = wide_ref[x, rows, :].astype(BF16)
        return carry

    lax.fori_loop(0, BRICKS, narrow, 0)

    left = iota((CHUNKS, 128), 1) < 64
    for half in range(2):
        half_ref[...] = got_ref[:, half, :]
        even = half_ref[pl.ds(0, CHUNKS, stride=2), :]
        odd = half_ref[pl.ds(1, CHUNKS, stride=2), :]
        place_ref[2 * half] = jnp.where(left, even, pltpu.roll(odd, 64, 1))
        place_ref[2 * half + 1] = jnp.where(left, pltpu.roll(even, 64, 1), odd)
    extra = place_ref[3]
    id_vmem[...] = jnp.maximum(extra - 1.0, 0.0).astype(I32)
    copy = pltpu.make_async_copy(id_vmem, id_smem, sem)
    copy.start()
    copy.wait()
    group_sum = lane_group_sum().astype(BF16)
    lane_group = iota((32, 128), 1) // 16
    c32 = iota((32, 128), 0)

    def one(chunk):
        hat_x = hat(place_ref[0, pl.ds(chunk, 1), :])
        hat_y = hat(place_ref[1, pl.ds(chunk, 1), :])
        hat_z = hat(place_ref[2, pl.ds(chunk, 1), :])
        plane = jnp.concatenate([hat_y[y : y + 1] * hat_z for y in range(8)], axis=0)
        weights = jnp.concatenate([hat_x[x : x + 1] * plane for x in range(8)], axis=0)
        high, low = split(weights)
        rows = []
        for seg in range(8):
            b = id_smem[chunk, seg * 16 + 10]
            rows.append(brick_ref[pl.ds(pl.multiple_of(b * 32, 32), 32), :])
        values = fast_dot(
            jnp.concatenate(rows, axis=0), jnp.concatenate([high, low], axis=1)
        )
        coef = jnp.zeros((32, 128), F32)
        for seg in range(8):
            part = values[seg * 32 : seg * 32 + 32]
            coef = jnp.where(lane_group == seg, part[:, 0:128] + part[:, 128:256], coef)
        shaped = coef * basis_rows(place_ref[3, pl.ds(chunk, 1), :], group_sum)
        raw_ref[0, pl.ds(chunk, 1), :] = coef[0:1]
        for ch in range(3):
            inside = (c32 >= 1 + 9 * ch) & (c32 < 10 + 9 * ch)
            raw_ref[1 + ch, pl.ds(chunk, 1), :] = jnp.sum(
                jnp.where(inside, shaped, 0.0), axis=0, keepdims=True
            )

    def several(turn, carry):
        for k in range(2):
            one(turn * 2 + k)
        return carry

    lax.fori_loop(0, CHUNKS // 2, several, 0)

    for q in range(3):
        tiles_ref[pl.ds(q, CHUNKS, stride=8), :] = place_ref[q]
    for q in range(4):
        tiles_ref[pl.ds(3 + q, CHUNKS, stride=8), :] = raw_ref[q]
    tiles_ref[pl.ds(7, CHUNKS, stride=8), :] = extra

    optical, through, opaque, _ = march(raw_ref[0], extra)
    light = through * opaque
    total = jnp.zeros((CHUNKS, 128), F32)
    row, lane = iota((128, 128), 0), iota((128, 128), 1)
    for v in range(4):
        part = optical if v == 3 else light * sigmoid(raw_ref[1 + v])
        total += exact_dot(part, jnp.where(lane == (row // 16) * 8 + v, 1.0, 0.0))
    sums_ref[:, 0, :] = total


def march(density, extra):
    row, lane = iota((128, 128), 0), iota((128, 128), 1)
    same = row // 16 == lane // 16
    step = exact_dot(extra, jnp.where(same & (row % 16 == 9), 1.0, 0.0))
    optical = softplus(density) * step
    before = exact_dot(optical, jnp.where(same & (row < lane), 1.0, 0.0))
    through = jnp.exp(-before)
    remains = jnp.exp(-optical)
    return optical, through, 1.0 - remains, (step, remains)


def forward(bricks, got):
    return pl.pallas_call(
        forward_kernel,
        out_shape=(
            jax.ShapeDtypeStruct((CHUNKS * 8, 128), F32),
            jax.ShapeDtypeStruct((CHUNKS, 1, 128), F32),
        ),
        in_specs=[VMEM, VMEM],
        out_specs=(VMEM, VMEM),
        scratch_shapes=[
            pltpu.VMEM((4, BRICKS * 32, 128), F32),
            pltpu.VMEM((BRICKS * 32, VOXELS), BF16),
            pltpu.VMEM((OWNERS, 128), F32),
            pltpu.VMEM((CHUNKS, 128), I32),
            pltpu.SMEM((CHUNKS, 128), I32),
            pltpu.VMEM((4, CHUNKS, 128), F32),
            pltpu.VMEM((4, CHUNKS, 128), F32),
            pltpu.SemaphoreType.DMA,
        ],
        compiler_params=pltpu.CompilerParams(vmem_limit_bytes=40 << 20),
        name="interpolate",
    )(bricks, got)


def to_rays(sums, choice):
    half = lax.rem(lax.axis_index("seg"), 2)
    turned = pltpu.roll(sums, lax.rem(128 - half * 32, 128), 1)
    found = exact_dot(jnp.transpose(turned)[0:32], choice)
    total = jnp.zeros((8, RAYS), F32)
    for j in range(SLOTS):
        total += found[8 * j : 8 * j + 8, RAYS * j : RAYS * j + RAYS]
    return total


def composite(colours, taus, target):
    me = lax.axis_index("seg")
    lower = jnp.where(iota((OWNERS, OWNERS), 1) < iota((OWNERS, OWNERS), 0), 1.0, 0.0)
    through = jnp.exp(-exact_dot(lower, taus))
    depth = iota((OWNERS, RAYS), 0)
    here = jnp.sum(jnp.where(depth == me, through, 0.0), axis=0, keepdims=True)
    colour, grad_colour = [], []
    grad_tau = jnp.zeros((1, RAYS), F32)
    for v in range(3):
        contrib = through * colours[v]
        colour.append(jnp.sum(contrib, axis=0, keepdims=True))
        behind = jnp.sum(jnp.where(depth > me, contrib, 0.0), axis=0, keepdims=True)
        misfit = LOSS_SCALE * (colour[v] - target[v : v + 1])
        grad_colour.append(here * misfit)
        grad_tau -= misfit * behind
    return colour, grad_colour + [grad_tau]


def to_slots(grads, choice):
    me = lax.axis_index("seg")
    row = iota((SLOTS * 4, RAYS), 0)
    block = jnp.zeros((SLOTS * 4, RAYS), F32)
    for v in range(4):
        block = jnp.where(row % 4 == v, grads[v], block)
    wide = jnp.concatenate(
        [jnp.where(row // 4 == j, block, 0.0) for j in range(SLOTS)], axis=1
    )
    wide = jnp.concatenate([wide, jnp.zeros((112, SLOTS * RAYS), F32)], axis=0)
    placed = exact_dot(choice, wide, NT)
    return pltpu.roll(placed, (me // 16) * 32 + lax.rem(me, 2) * 16, 1)


def composite_kernel(
    sums_ref, tiles_ref, choice_ref, target_ref,
    colour_ref, all_tiles_ref, all_grads_ref,
    back_ref, ray_ref, rays_ref, slot_ref, slots_ref, grads_ref,
    send_sems, recv_sems, own_sem,
):
    greet([("seg", OWNERS), ("grp", GROUPS)])
    me = lax.axis_index("seg")
    group = lax.axis_index("grp")
    send_all(
        "grp", GROUPS, lambda peer: tiles_ref, all_tiles_ref, send_sems.at[0], recv_sems.at[0]
    )
    own = pltpu.make_async_copy(tiles_ref, all_tiles_ref.at[group], own_sem)
    own.start()

    send_all(
        "seg", OWNERS, lambda peer: sums_ref.at[peer // 2], back_ref,
        send_sems.at[1], recv_sems.at[1],
    )
    back_ref[me] = sums_ref[me // 2]
    wait_all(back_ref, OWNERS, recv_sems.at[1])
    choice = choice_ref[...]
    ray_ref[...] = to_rays(back_ref[:, 0, :], choice)[0:4]

    send_all("seg", OWNERS, lambda peer: ray_ref, rays_ref, send_sems.at[2], recv_sems.at[2])
    rays_ref[me] = ray_ref[...]
    wait_all(rays_ref, OWNERS, recv_sems.at[2])
    colour, grads = composite(
        [rays_ref[:, v, :] for v in range(3)], rays_ref[:, 3, :], target_ref[...]
    )
    for v in range(3):
        colour_ref[v : v + 1, :] = colour[v]
    slot_ref[:, 0, :] = to_slots(grads, choice)

    send_all(
        "seg", OWNERS, lambda peer: slot_ref.at[peer], slots_ref, send_sems.at[3], recv_sems.at[3]
    )
    slots_ref[me] = slot_ref[me]
    wait_all(slots_ref, OWNERS, recv_sems.at[3])
    pick = jnp.where((iota((8, OWNERS), 1) // 2) % 8 == iota((8, OWNERS), 0), 1.0, 0.0)
    grads_ref[...] = exact_dot(pick, slots_ref[:, 0, :])

    send_all(
        "grp", GROUPS, lambda peer: grads_ref, all_grads_ref, send_sems.at[4], recv_sems.at[4]
    )
    all_grads_ref[group] = grads_ref[...]
    wait_all(all_grads_ref, GROUPS, recv_sems.at[4])
    own.wait()
    wait_all(all_tiles_ref, GROUPS, recv_sems.at[0])
    wait_all(all_tiles_ref, GROUPS, send_sems.at[0])
    wait_all(back_ref, OWNERS, send_sems.at[1])
    wait_all(rays_ref, OWNERS, send_sems.at[2])
    wait_all(slots_ref, OWNERS, send_sems.at[3])
    wait_all(all_grads_ref, GROUPS, send_sems.at[4])


def exchange(sums, tiles, choice, target):
    return pl.pallas_call(
        composite_kernel,
        out_shape=(
            jax.ShapeDtypeStruct((3, RAYS), F32),
            jax.ShapeDtypeStruct((GROUPS, CHUNKS * 8, 128), F32),
            jax.ShapeDtypeStruct((GROUPS, 8, 128), F32),
        ),
        in_specs=[VMEM] * 4,
        out_specs=(VMEM, VMEM, VMEM),
        scratch_shapes=[
            pltpu.VMEM((OWNERS, 1, 128), F32),
            pltpu.VMEM((4, RAYS), F32),
            pltpu.VMEM((OWNERS, 4, RAYS), F32),
            pltpu.VMEM((OWNERS, 1, 128), F32),
            pltpu.VMEM((OWNERS, 1, 128), F32),
            pltpu.VMEM((8, 128), F32),
            pltpu.SemaphoreType.DMA((5,)),
            pltpu.SemaphoreType.DMA((5,)),
            pltpu.SemaphoreType.DMA,
        ],
        compiler_params=pltpu.CompilerParams(
            collective_id=1, has_side_effects=True, vmem_limit_bytes=32 << 20
        ),
        name="composite",
    )(sums, tiles, choice, target)


def plan_chunks(extra):
    across = jnp.transpose(extra)
    named = iota((64, ALL_CHUNKS), 0).astype(F32) + 1.0
    hits = [
        jnp.where(across[seg * 16 + 10 : seg * 16 + 11] == named, 1.0, 0.0) for seg in range(8)
    ]
    earlier = jnp.where(
        iota((ALL_CHUNKS, ALL_CHUNKS), 0) < iota((ALL_CHUNKS, ALL_CHUNKS), 1), 1.0, 0.0
    ).astype(BF16)
    counts = fast_dot(jnp.concatenate(hits, axis=0).astype(BF16), earlier)
    carry = jnp.zeros((64, 1), F32)
    ranks = []
    for seg in range(8):
        ranks.append(counts[seg * 64 : seg * 64 + 64] + carry)
        carry = carry + jnp.sum(hits[seg], axis=1, keepdims=True)
    full = jnp.floor((carry + 7.0) * 0.125)
    lower = jnp.where(iota((64, 64), 1) < iota((64, 64), 0), 1.0, 0.0).astype(BF16)
    full_wide = jnp.broadcast_to(full, (64, 128))
    start = fast_dot(lower, full_wide.astype(BF16))
    end = start + full_wide
    start256 = jnp.concatenate([start, start], axis=1)
    selectors, values = [], []
    row = iota((32, ALL_CHUNKS), 0)
    lane = iota((32, ALL_CHUNKS), 1).astype(F32)
    for seg in range(8):
        place = (
            jnp.sum(hits[seg] * (8.0 * start256 + ranks[seg] + 1.0), axis=0, keepdims=True) - 1.0
        )
        chunk = jnp.floor(place * 0.125)
        inside = place - 8.0 * chunk
        selectors.append(
            jnp.where(iota((TABLE, ALL_CHUNKS), 0).astype(F32) == chunk, 1.0, 0.0).astype(BF16)
        )
        kind = jnp.where(
            row < 8, lane, jnp.where(row < 16, float(seg), jnp.where(row < 24, 1.0, 0.0))
        )
        values.append(jnp.where((row % 8).astype(F32) == inside, kind, 0.0).astype(BF16))
    table = fast_dot(
        jnp.concatenate(values, axis=1), jnp.concatenate(selectors, axis=1), NT
    )
    tile = table[0:8] + (1.0 - table[16:24]) * float(ALL_CHUNKS)
    turn = 16.0 * (iota((8, TABLE), 0).astype(F32) - table[8:16])
    turn = jnp.where(turn < 0.0, turn + 128.0, turn)
    place = iota((64, 128), 1).astype(F32)
    real = iota((64, 128), 0) < BRICKS
    owner = [
        jnp.sum(jnp.where((end <= place + 128.0 * k) & real, 1.0, 0.0), axis=0, keepdims=True)
        for k in range(TABLE // 128)
    ]
    owner = jnp.minimum(jnp.concatenate(owner, axis=1), float(BRICKS - 1))
    number = jnp.sum(full_wide, axis=0, keepdims=True)
    number = jnp.concatenate([number] * (TABLE // 128), axis=1)
    last = jnp.where(iota((8, TABLE), 0) == 0, owner, number)
    return jnp.concatenate([tile, turn, last], axis=0).astype(I32)


def gradient_kernel(
    tiles_hbm, grads_ref, out_ref,
    tiles_ref, table_vmem, table_smem, slot_ref, total_ref, sems,
):
    load = pltpu.make_async_copy(tiles_hbm, tiles_ref.at[pl.ds(0, ALL_CHUNKS * 8)], sems.at[0])
    load.start()
    tiles_ref[pl.ds(ALL_CHUNKS * 8, 8), :] = jnp.zeros((8, 128), F32)
    row, lane = iota((128, 128), 0), iota((128, 128), 1)
    for part in range(4):
        for v in range(4):
            spread = jnp.where(row == part * 32 + (lane // 16) * 4 + v, 1.0, 0.0)
            wide = exact_dot(grads_ref[...], spread)
            for g in range(GROUPS):
                slot_ref[v, pl.ds(g * CHUNKS + part * 8, 8), :] = wide[g * 8 : g * 8 + 8]
    total_ref[...] = jnp.zeros_like(total_ref)
    load.wait()

    extra = tiles_ref[pl.ds(7, ALL_CHUNKS, stride=8), :]
    table_vmem[...] = plan_chunks(extra)
    plan = pltpu.make_async_copy(table_vmem, table_smem, sems.at[1])
    plan.start()

    density = tiles_ref[pl.ds(3, ALL_CHUNKS, stride=8), :]
    optical, through, opaque, (step, remains) = march(density, extra)
    light = through * opaque
    mixed = jnp.zeros((ALL_CHUNKS, 128), F32)
    for v in range(3):
        radiance = sigmoid(tiles_ref[pl.ds(4 + v, ALL_CHUNKS, stride=8), :])
        grad_colour = slot_ref[v]
        mixed += grad_colour * radiance
        tiles_ref[pl.ds(4 + v, ALL_CHUNKS, stride=8), :] = (
            grad_colour * light * radiance * (1.0 - radiance)
        )
    later = jnp.where((row // 16 == lane // 16) & (row > lane), 1.0, 0.0)
    grad_optical = through * remains * mixed - exact_dot(light * mixed, later) + slot_ref[3]
    tiles_ref[pl.ds(3, ALL_CHUNKS, stride=8), :] = grad_optical * step * sigmoid(density)
    plan.wait()

    group_sum = lane_group_sum().astype(BF16)
    lane_group = iota((8, 128), 1) // 16
    c32 = iota((32, 128), 0)

    def one(chunk):
        tile = jnp.zeros((8, 128), F32)
        for p in range(8):
            start = pl.multiple_of(table_smem[p, chunk] * 8, 8)
            part = pltpu.roll(tiles_ref[pl.ds(start, 8), :], table_smem[8 + p, chunk], 1)
            tile = jnp.where(lane_group == p, part, tile)
        hat_x, hat_y, hat_z = hat(tile[0:1]), hat(tile[1:2]), hat(tile[2:3])
        plane = jnp.concatenate([hat_y[y : y + 1] * hat_z for y in range(8)], axis=0)
        grad = jnp.where(
            c32 == 0,
            tile[3:4],
            jnp.where(c32 < 10, tile[4:5], jnp.where(c32 < 19, tile[5:6], tile[6:7])),
        )
        grad = grad * basis_rows(tile[7:8], group_sum)
        left = jnp.concatenate(
            [
                jnp.concatenate([grad * hat_x[2 * x + k : 2 * x + k + 1] for x in range(4)], axis=0)
                for k in range(2)
            ],
            axis=1,
        )
        left_high, left_low = split(left)
        high, low = split(plane)
        none = jnp.zeros((64, 128), BF16)

        def both(value):
            return jnp.concatenate(
                [
                    jnp.concatenate([value, none], axis=1),
                    jnp.concatenate([none, value], axis=1),
                ],
                axis=0,
            )

        high, low = both(high), both(low)
        return fast_dot(
            jnp.concatenate([left_high, left_high, left_low], axis=1),
            jnp.concatenate([high, low, high], axis=1),
            NT,
        )

    def several(turn, carry):
        parts = [one(turn * UNROLL + k) for k in range(UNROLL)]
        for k in range(UNROLL):
            b = table_smem[16, turn * UNROLL + k]
            rows = pl.ds(pl.multiple_of(b * 128, 128), 128)
            total_ref[rows, :] += parts[k]
        return carry

    lax.fori_loop(0, (table_smem[17, 0] + UNROLL - 1) // UNROLL, several, 0)

    for c in range(COEF):
        for x in range(4):
            out_ref[c, :, x * 128 : x * 128 + 128] = total_ref[
                pl.ds(x * 32 + c, BRICKS, stride=128), :
            ]


def gradient(tiles, grads):
    return pl.pallas_call(
        gradient_kernel,
        out_shape=jax.ShapeDtypeStruct((COEF, BRICKS, VOXELS), F32),
        in_specs=[ANY, VMEM],
        out_specs=VMEM,
        scratch_shapes=[
            pltpu.VMEM((ALL_CHUNKS * 8 + 8, 128), F32),
            pltpu.VMEM((24, TABLE), I32),
            pltpu.SMEM((24, TABLE), I32),
            pltpu.VMEM((4, ALL_CHUNKS, 128), F32),
            pltpu.VMEM((BRICKS * 128, 128), F32),
            pltpu.SemaphoreType.DMA((2,)),
        ],
        compiler_params=pltpu.CompilerParams(vmem_limit_bytes=48 << 20),
        name="gradient",
    )(tiles, grads)


def local(
    bricks, requests, seg_owner, seg_slot, sample_cells, sample_fracs,
    ray_angles, ray_step, pixel_target,
):
    got, choice = dispatch(
        seg_owner.reshape(1, RAYS),
        seg_slot.reshape(1, RAYS),
        requests.reshape(OWNERS, 2),
        sample_cells.reshape(SAMP, RAYS),
        sample_fracs.reshape(3 * SAMP, RAYS),
        ray_angles,
        ray_step.reshape(1, RAYS),
    )
    tiles, sums = forward(bricks, got)
    colour, tiles, grads = exchange(sums, tiles, choice, pixel_target)
    gradients = gradient(
        tiles.reshape(ALL_CHUNKS * 8, 128), grads.reshape(GROUPS * 8, 128)
    )
    return gradients, colour


def solution(mesh):
    return jax.shard_map(
        local,
        mesh=mesh,
        in_specs=(
            P(None, "seg", None),
            P("seg", "grp", None, None),
            P("seg", "grp", None),
            P("seg", "grp"),
            P(None, "seg", "grp"),
            P(None, None, "seg", "grp"),
            P(None, "grp"),
            P("grp"),
            P(None, "grp"),
        ),
        out_specs=(P(None, "seg", None), P(None, "grp")),
        check_vma=False,
    )
```

```python
import functools

import jax
import jax.numpy as jnp
from jax import lax
from jax.experimental import pallas as pl
from jax.experimental.pallas import tpu as pltpu
from jax.sharding import PartitionSpec as P

COEF = 28
VOXELS = 512
SAMP = 16
OWNERS = 64
GROUPS = 8
SLOTS = 4
BRICKS = 48
RAYS = 128
CHUNKS = OWNERS * SLOTS // 8
ALL_CHUNKS = GROUPS * CHUNKS
TABLE = 384
UNROLL = 16
FUNROLL = 8
LOSS_SCALE = 1024.0
BASIS_0 = 0.28209479
ROW_OF = [24] + [
    25 + ch if k == 0 else ch * 8 + k - 1 for ch in range(3) for k in range(9)
]
F32 = jnp.float32
BF16 = jnp.bfloat16
I32 = jnp.int32
VMEM = pl.BlockSpec(memory_space=pltpu.VMEM)
ANY = pl.BlockSpec(memory_space=pl.ANY)
MESH = pl.DeviceIdType.MESH
NN = (((1,), (0,)), ((), ()))
NT = (((1,), (1,)), ((), ()))


def iota(shape, dim):
    return lax.broadcasted_iota(I32, shape, dim)


def exact_dot(a, b, dims=NN):
    return lax.dot_general(
        a, b, dims, precision=lax.Precision.HIGHEST, preferred_element_type=F32
    )


def fast_dot(a, b, dims=NN):
    return lax.dot_general(a, b, dims, preferred_element_type=F32)


def split(value):
    high = value.astype(BF16)
    return high, (value - high.astype(F32)).astype(BF16)


def hat(place):
    return jnp.maximum(1.0 - jnp.abs(place - iota((8, 128), 0).astype(F32)), 0.0)


def softplus(value):
    return jnp.maximum(value, 0.0) + jnp.log1p(jnp.exp(-jnp.abs(value)))


def sigmoid(value):
    return 1.0 / (1.0 + jnp.exp(-value))


def ray_basis(angles):
    polar = angles[0:1]
    azimuth = angles[1:2]
    x = jnp.sin(polar) * jnp.cos(azimuth)
    y = jnp.sin(polar) * jnp.sin(azimuth)
    z = jnp.cos(polar)
    return [
        BASIS_0 * jnp.ones_like(x),
        -0.48860251 * y,
        0.48860251 * z,
        -0.48860251 * x,
        1.09254843 * x * y,
        -1.09254843 * y * z,
        0.31539157 * (2.0 * z * z - x * x - y * y),
        -1.09254843 * x * z,
        0.54627422 * (x * x - y * y),
    ]


def pack(owner, slot, wanted, cells, fracs, basis, step):
    mine = owner == iota((OWNERS, RAYS), 0)
    across = jnp.broadcast_to(owner, (RAYS, RAYS))
    ahead = iota((RAYS, RAYS), 0) < iota((RAYS, RAYS), 1)
    rank = jnp.sum(
        jnp.where((jnp.transpose(across) == across) & ahead, 1, 0), axis=0, keepdims=True
    )
    columns = jnp.transpose(wanted)
    brick = jnp.sum(
        jnp.where(mine, jnp.where(slot == 0, columns[:, 0:1], columns[:, 1:2]), 0),
        axis=0, keepdims=True,
    )
    chosen = [mine & (rank == j) for j in range(SLOTS)]
    choice = jnp.concatenate([jnp.where(one, 1.0, 0.0) for one in chosen], axis=1)
    lane = iota((OWNERS, RAYS), 1)
    bricks = jnp.zeros((OWNERS, RAYS), I32)
    for j in range(SLOTS):
        named = jnp.sum(jnp.where(chosen[j], brick, 0), axis=1, keepdims=True)
        bricks = jnp.where(lane == j, named, bricks)
    cell_x = (cells * 1338) >> 16
    rest = cells - cell_x * 49
    cell_y = (rest * 9363) >> 16
    cell_z = rest - cell_y * 7
    place_x = cell_x.astype(F32) + fracs[0:16]
    place_y = cell_y.astype(F32) + fracs[16:32]
    place_z = cell_z.astype(F32) + fracs[32:48]
    row = iota((SAMP, RAYS), 0)
    extra = jnp.where(row == 11, 1.0, 0.0)
    for k, value in enumerate(basis + [step, brick.astype(F32) + 1.0]):
        extra = jnp.where(row == k, value, extra)
    none = jnp.zeros((SAMP, RAYS), F32)

    def placed(first, second):
        parts = []
        for j in range(SLOTS):
            rows = [none] * 8
            rows[j] = first
            rows[4 + j] = second
            parts.append(jnp.concatenate(rows, axis=0))
        return jnp.concatenate(parts, axis=1)

    return (
        choice,
        bricks,
        exact_dot(choice, placed(place_x, place_y), NT),
        exact_dot(choice, placed(place_z, extra), NT),
    )


def greet(axes):
    barrier = pltpu.get_barrier_semaphore()
    total = 0
    for axis, count in axes:
        me = lax.axis_index(axis)

        def hail(turn, carry, axis=axis, count=count, me=me):
            pl.semaphore_signal(
                barrier,
                inc=1,
                device_id={axis: lax.rem(me + turn, count)},
                device_id_type=MESH,
            )
            return carry

        lax.fori_loop(1, count, hail, 0)
        total += count - 1
    return lambda: pl.semaphore_wait(barrier, total)


def send_all(axis, count, source, target, send_sem, recv_sem):
    me = lax.axis_index(axis)

    def one(turn, carry):
        peer = lax.rem(me + turn, count)
        pltpu.make_async_remote_copy(
            src_ref=source(peer),
            dst_ref=target.at[me],
            send_sem=send_sem,
            recv_sem=recv_sem,
            device_id={axis: peer},
            device_id_type=MESH,
        ).start()
        return carry

    lax.fori_loop(1, count, one, 0)


def wait_all(target, count, sem):
    part = target.at[pl.ds(0, count - 1)]
    pltpu.make_async_copy(part, part, sem).wait()


def lay_out_bricks(bricks_ref, wide_ref, brick_ref):
    for c in range(COEF, 32):
        for x in range(4):
            wide_ref[x, pl.ds(c, BRICKS, stride=32), :] = jnp.zeros((BRICKS, 128), F32)
    for c in range(COEF):
        for x in range(4):
            wide_ref[x, pl.ds(ROW_OF[c], BRICKS, stride=32), :] = bricks_ref[
                c, :, x * 128 : x * 128 + 128
            ].astype(F32)

    def narrow(turn, carry):
        for k in range(8):
            rows = pl.ds(pl.multiple_of(turn * 256 + k * 32, 32), 32)
            for x in range(4):
                brick_ref[turn * 8 + k, :, x * 128 : x * 128 + 128] = wide_ref[
                    x, rows, :
                ].astype(BF16)
        return carry

    lax.fori_loop(0, BRICKS // 8, narrow, 0)


def unpack(got_ref, half_ref, place_ref, basis_ref):
    left = iota((CHUNKS, 128), 1) < 64
    for half in range(2):
        half_ref[...] = got_ref[:, half, :]
        even = half_ref[pl.ds(0, CHUNKS, stride=2), :]
        odd = half_ref[pl.ds(1, CHUNKS, stride=2), :]
        place_ref[2 * half] = jnp.where(left, even, pltpu.roll(odd, 64, 1))
        place_ref[2 * half + 1] = jnp.where(left, pltpu.roll(even, 64, 1), odd)
    row, lane = iota((128, 1024), 0), iota((128, 1024), 1)
    spread = jnp.where(row == ((lane % 128) // 16) * 16 + lane // 128 + 1, 1.0, 0.0)
    basis = exact_dot(place_ref[3], spread)
    for k in range(8):
        basis_ref[pl.ds(k, CHUNKS, stride=8), :] = basis[:, k * 128 : k * 128 + 128]


def interpolate(brick_ref, place_ref, basis_ref, id_smem, raw_ref):
    lane_group = iota((32, 128), 1) // 16

    def one(chunk):
        hat_x = hat(place_ref[0, pl.ds(chunk, 1), :])
        hat_y = hat(place_ref[1, pl.ds(chunk, 1), :])
        hat_z = hat(place_ref[2, pl.ds(chunk, 1), :])
        plane = jnp.concatenate([hat_y[y : y + 1] * hat_z for y in range(8)], axis=0)
        weights = jnp.concatenate([hat_x[x : x + 1] * plane for x in range(8)], axis=0)
        high, low = split(weights)
        rows = []
        for seg in range(8):
            b = id_smem[chunk * 2 + seg // 4, 0, seg % 4]
            rows.append(brick_ref[b])
        values = fast_dot(
            jnp.concatenate(rows, axis=0), jnp.concatenate([high, low], axis=1)
        )
        coef = jnp.zeros((32, 128), F32)
        for seg in range(8):
            part = values[seg * 32 : seg * 32 + 32]
            coef = jnp.where(lane_group == seg, part[:, 0:128] + part[:, 128:256], coef)
        basis = basis_ref[pl.ds(pl.multiple_of(chunk * 8, 8), 8), :]
        raw_ref[0, pl.ds(chunk, 1), :] = coef[24:25]
        for ch in range(3):
            raw_ref[1 + ch, pl.ds(chunk, 1), :] = coef[25 + ch : 26 + ch] * BASIS_0 + jnp.sum(
                coef[8 * ch : 8 * ch + 8] * basis, axis=0, keepdims=True
            )

    def several(turn, carry):
        for k in range(FUNROLL):
            one(turn * FUNROLL + k)
        return carry

    lax.fori_loop(0, CHUNKS // FUNROLL, several, 0)


def segment_sums(raw_ref, extra):
    optical, through, opaque, _ = march(raw_ref[0], extra)
    light = through * opaque
    total = jnp.zeros((CHUNKS, 128), F32)
    row, lane = iota((128, 128), 0), iota((128, 128), 1)
    for v in range(4):
        part = optical if v == 3 else light * sigmoid(raw_ref[1 + v])
        total += exact_dot(part, jnp.where(lane == (row // 16) * 8 + v, 1.0, 0.0))
    return total


def march(density, extra):
    row, lane = iota((128, 128), 0), iota((128, 128), 1)
    same = row // 16 == lane // 16
    step = exact_dot(extra, jnp.where(same & (row % 16 == 9), 1.0, 0.0))
    optical = softplus(density) * step
    before = exact_dot(optical, jnp.where(same & (row < lane), 1.0, 0.0))
    through = jnp.exp(-before)
    remains = jnp.exp(-optical)
    return optical, through, 1.0 - remains, (step, remains)


def to_rays(sums, choice):
    half = lax.rem(lax.axis_index("seg"), 2)
    turned = pltpu.roll(sums, lax.rem(128 - half * 32, 128), 1)
    found = exact_dot(jnp.transpose(turned)[0:32], choice)
    total = jnp.zeros((8, RAYS), F32)
    for j in range(SLOTS):
        total += found[8 * j : 8 * j + 8, RAYS * j : RAYS * j + RAYS]
    return total


def composite(colours, taus, target):
    me = lax.axis_index("seg")
    lower = jnp.where(iota((OWNERS, OWNERS), 1) < iota((OWNERS, OWNERS), 0), 1.0, 0.0)
    through = jnp.exp(-exact_dot(lower, taus))
    depth = iota((OWNERS, RAYS), 0)
    here = jnp.sum(jnp.where(depth == me, through, 0.0), axis=0, keepdims=True)
    colour, grad_colour = [], []
    grad_tau = jnp.zeros((1, RAYS), F32)
    for v in range(3):
        contrib = through * colours[v]
        colour.append(jnp.sum(contrib, axis=0, keepdims=True))
        behind = jnp.sum(jnp.where(depth > me, contrib, 0.0), axis=0, keepdims=True)
        misfit = LOSS_SCALE * (colour[v] - target[v : v + 1])
        grad_colour.append(here * misfit)
        grad_tau -= misfit * behind
    return colour, grad_colour + [grad_tau]


def to_slots(grads, choice):
    me = lax.axis_index("seg")
    row = iota((SLOTS * 4, RAYS), 0)
    block = jnp.zeros((SLOTS * 4, RAYS), F32)
    for v in range(4):
        block = jnp.where(row % 4 == v, grads[v], block)
    wide = jnp.concatenate(
        [jnp.where(row // 4 == j, block, 0.0) for j in range(SLOTS)], axis=1
    )
    wide = jnp.concatenate([wide, jnp.zeros((112, SLOTS * RAYS), F32)], axis=0)
    placed = exact_dot(choice, wide, NT)
    return pltpu.roll(placed, (me // 16) * 32 + lax.rem(me, 2) * 16, 1)


def render_kernel(
    owner_hbm, slot_hbm, wanted_hbm, cells_hbm, fracs_hbm, angles_hbm, step_hbm, target_hbm,
    bricks_hbm,
    colour_ref, places_ref, raws_ref, all_grads_ref,
    owner_ref, slot_ref, wanted_ref, cells_ref, fracs_ref, angles_ref, step_ref, target_ref,
    bricks_ref,
    choice_ref, out_ref, got_ref, wide_ref, brick_ref, half_ref, numbers_ref, ids_ref, id_smem,
    place_ref, raw_ref, basis_ref,
    sums_ref, back_ref, ray_ref, rays_ref, slot_out_ref, slots_ref, grads_ref,
    load_sems, send_sems, recv_sems, own_sems,
):
    loads = [
        pltpu.make_async_copy(source, target, load_sems.at[k])
        for k, (source, target) in enumerate(
            [
                (owner_hbm, owner_ref), (slot_hbm, slot_ref), (wanted_hbm, wanted_ref),
                (cells_hbm, cells_ref), (fracs_hbm, fracs_ref), (angles_hbm, angles_ref),
                (step_hbm, step_ref), (target_hbm, target_ref), (bricks_hbm, bricks_ref),
            ]
        )
    ]
    for load in loads:
        load.start()
    met = greet([("seg", OWNERS), ("grp", GROUPS)])
    for load in loads[:8]:
        load.wait()
    me = lax.axis_index("seg")
    group = lax.axis_index("grp")

    choice, numbers, first, second = pack(
        owner_ref[...], slot_ref[...], wanted_ref[...], cells_ref[...], fracs_ref[...],
        ray_basis(angles_ref[...]), step_ref[...],
    )
    choice_ref[...] = choice
    out_ref[:, 0, :] = first
    out_ref[:, 1, :] = second
    numbers_ref[:, 0, :] = numbers
    met()
    send_all(
        "seg", OWNERS, lambda peer: numbers_ref.at[peer], ids_ref, send_sems.at[7], recv_sems.at[7]
    )
    ids_ref[me] = numbers_ref[me]
    send_all(
        "seg", OWNERS, lambda peer: out_ref.at[peer], got_ref, send_sems.at[0], recv_sems.at[0]
    )
    got_ref[me] = out_ref[me]
    loads[8].wait()
    lay_out_bricks(bricks_ref, wide_ref, brick_ref)
    wait_all(got_ref, OWNERS, recv_sems.at[0])

    unpack(got_ref, half_ref, place_ref, basis_ref)
    extra = place_ref[3]
    send_all(
        "grp", GROUPS, lambda peer: place_ref, places_ref, send_sems.at[1], recv_sems.at[1]
    )
    own_places = pltpu.make_async_copy(place_ref, places_ref.at[group], own_sems.at[0])
    own_places.start()
    wait_all(ids_ref, OWNERS, recv_sems.at[7])
    ids = pltpu.make_async_copy(ids_ref, id_smem, own_sems.at[2])
    ids.start()
    ids.wait()
    interpolate(brick_ref, place_ref, basis_ref, id_smem, raw_ref)
    sums_ref[:, 0, :] = segment_sums(raw_ref, extra)

    send_all(
        "seg", OWNERS, lambda peer: sums_ref.at[peer // 2], back_ref,
        send_sems.at[2], recv_sems.at[2],
    )
    back_ref[me] = sums_ref[me // 2]
    send_all("grp", GROUPS, lambda peer: raw_ref, raws_ref, send_sems.at[3], recv_sems.at[3])
    own_raws = pltpu.make_async_copy(raw_ref, raws_ref.at[group], own_sems.at[1])
    own_raws.start()
    wait_all(back_ref, OWNERS, recv_sems.at[2])
    choice = choice_ref[...]
    ray_ref[...] = to_rays(back_ref[:, 0, :], choice)[0:4]

    send_all("seg", OWNERS, lambda peer: ray_ref, rays_ref, send_sems.at[4], recv_sems.at[4])
    rays_ref[me] = ray_ref[...]
    wait_all(rays_ref, OWNERS, recv_sems.at[4])
    colour, grads = composite(
        [rays_ref[:, v, :] for v in range(3)], rays_ref[:, 3, :], target_ref[...]
    )
    for v in range(3):
        colour_ref[v : v + 1, :] = colour[v]
    slot_out_ref[:, 0, :] = to_slots(grads, choice)

    send_all(
        "seg", OWNERS, lambda peer: slot_out_ref.at[peer], slots_ref,
        send_sems.at[5], recv_sems.at[5],
    )
    slots_ref[me] = slot_out_ref[me]
    wait_all(slots_ref, OWNERS, recv_sems.at[5])
    pick = jnp.where((iota((8, OWNERS), 1) // 2) % 8 == iota((8, OWNERS), 0), 1.0, 0.0)
    grads_ref[...] = exact_dot(pick, slots_ref[:, 0, :])
    send_all(
        "grp", GROUPS, lambda peer: grads_ref, all_grads_ref, send_sems.at[6], recv_sems.at[6]
    )
    all_grads_ref[group] = grads_ref[...]
    wait_all(all_grads_ref, GROUPS, recv_sems.at[6])
    own_places.wait()
    own_raws.wait()
    wait_all(places_ref, GROUPS, recv_sems.at[1])
    wait_all(raws_ref, GROUPS, recv_sems.at[3])
    wait_all(got_ref, OWNERS, send_sems.at[0])
    wait_all(ids_ref, OWNERS, send_sems.at[7])
    wait_all(places_ref, GROUPS, send_sems.at[1])
    wait_all(back_ref, OWNERS, send_sems.at[2])
    wait_all(raws_ref, GROUPS, send_sems.at[3])
    wait_all(rays_ref, OWNERS, send_sems.at[4])
    wait_all(slots_ref, OWNERS, send_sems.at[5])
    wait_all(all_grads_ref, GROUPS, send_sems.at[6])


def render(*operands):
    return pl.pallas_call(
        render_kernel,
        out_shape=(
            jax.ShapeDtypeStruct((3, RAYS), F32),
            jax.ShapeDtypeStruct((GROUPS, 4, CHUNKS, 128), F32),
            jax.ShapeDtypeStruct((GROUPS, 4, CHUNKS, 128), F32),
            jax.ShapeDtypeStruct((GROUPS, 8, 128), F32),
        ),
        in_specs=[ANY] * 9,
        out_specs=(VMEM, ANY, ANY, VMEM),
        scratch_shapes=[pltpu.VMEM(x.shape, x.dtype) for x in operands]
        + [
            pltpu.VMEM((OWNERS, SLOTS * RAYS), F32),
            pltpu.VMEM((OWNERS, 2, 128), F32),
            pltpu.VMEM((OWNERS, 2, 128), F32),
            pltpu.VMEM((4, BRICKS * 32, 128), F32),
            pltpu.VMEM((BRICKS, 32, VOXELS), BF16),
            pltpu.VMEM((OWNERS, 128), F32),
            pltpu.VMEM((OWNERS, 1, 128), I32),
            pltpu.VMEM((OWNERS, 1, 128), I32),
            pltpu.SMEM((OWNERS, 1, 128), I32),
            pltpu.VMEM((4, CHUNKS, 128), F32),
            pltpu.VMEM((4, CHUNKS, 128), F32),
            pltpu.VMEM((CHUNKS * 8, 128), F32),
            pltpu.VMEM((CHUNKS, 1, 128), F32),
            pltpu.VMEM((OWNERS, 1, 128), F32),
            pltpu.VMEM((4, RAYS), F32),
            pltpu.VMEM((OWNERS, 4, RAYS), F32),
            pltpu.VMEM((OWNERS, 1, 128), F32),
            pltpu.VMEM((OWNERS, 1, 128), F32),
            pltpu.VMEM((8, 128), F32),
            pltpu.SemaphoreType.DMA((9,)),
            pltpu.SemaphoreType.DMA((8,)),
            pltpu.SemaphoreType.DMA((8,)),
            pltpu.SemaphoreType.DMA((3,)),
        ],
        compiler_params=pltpu.CompilerParams(
            collective_id=0, has_side_effects=True, vmem_limit_bytes=64 << 20
        ),
        name="render",
    )(*operands)


def plan_chunks(extra):
    across = jnp.transpose(extra)
    named = iota((64, ALL_CHUNKS), 0).astype(F32) + 1.0
    hits = [
        jnp.where(across[seg * 16 + 10 : seg * 16 + 11] == named, 1.0, 0.0) for seg in range(8)
    ]
    earlier = jnp.where(
        iota((ALL_CHUNKS, ALL_CHUNKS), 0) < iota((ALL_CHUNKS, ALL_CHUNKS), 1), 1.0, 0.0
    ).astype(BF16)
    counts = fast_dot(jnp.concatenate(hits, axis=0).astype(BF16), earlier)
    carry = jnp.zeros((64, 1), F32)
    ranks = []
    for seg in range(8):
        ranks.append(counts[seg * 64 : seg * 64 + 64] + carry)
        carry = carry + jnp.sum(hits[seg], axis=1, keepdims=True)
    full = jnp.floor((carry + 7.0) * 0.125)
    lower = jnp.where(iota((64, 64), 1) < iota((64, 64), 0), 1.0, 0.0).astype(BF16)
    full_wide = jnp.broadcast_to(full, (64, 128))
    start = fast_dot(lower, full_wide.astype(BF16))
    end = start + full_wide
    start256 = jnp.concatenate([start, start], axis=1)
    selectors, values = [], []
    row = iota((32, ALL_CHUNKS), 0)
    lane = iota((32, ALL_CHUNKS), 1).astype(F32)
    for seg in range(8):
        place = (
            jnp.sum(hits[seg] * (8.0 * start256 + ranks[seg] + 1.0), axis=0, keepdims=True) - 1.0
        )
        chunk = jnp.floor(place * 0.125)
        inside = place - 8.0 * chunk
        selectors.append(
            jnp.where(iota((TABLE, ALL_CHUNKS), 0).astype(F32) == chunk, 1.0, 0.0).astype(BF16)
        )
        kind = jnp.where(
            row < 8, lane, jnp.where(row < 16, float(seg), jnp.where(row < 24, 1.0, 0.0))
        )
        values.append(jnp.where((row % 8).astype(F32) == inside, kind, 0.0).astype(BF16))
    table = fast_dot(
        jnp.concatenate(values, axis=1), jnp.concatenate(selectors, axis=1), NT
    )
    tile = table[0:8] + (1.0 - table[16:24]) * float(ALL_CHUNKS)
    turn = 16.0 * (iota((8, TABLE), 0).astype(F32) - table[8:16])
    turn = jnp.where(turn < 0.0, turn + 128.0, turn)
    place = iota((64, 128), 1).astype(F32)
    real = iota((64, 128), 0) < BRICKS
    owner = [
        jnp.sum(jnp.where((end <= place + 128.0 * k) & real, 1.0, 0.0), axis=0, keepdims=True)
        for k in range(TABLE // 128)
    ]
    owner = jnp.minimum(jnp.concatenate(owner, axis=1), float(BRICKS - 1))
    number = jnp.sum(full_wide, axis=0, keepdims=True)
    number = jnp.concatenate([number] * (TABLE // 128), axis=1)
    last = jnp.where(iota((8, TABLE), 0) == 0, owner, number)
    return jnp.concatenate([tile, turn, last], axis=0).astype(I32)


def gradient_kernel(
    places_hbm, raws_hbm, grads_hbm, colour_hbm, out_ref, colour_ref,
    places_ref, raws_ref, grads_ref, tiles_ref, table_vmem, table_smem, slot_ref, total_ref, sems,
):
    load_places = pltpu.make_async_copy(places_hbm, places_ref, sems.at[0])
    load_raws = pltpu.make_async_copy(raws_hbm, raws_ref, sems.at[2])
    load_places.start()
    load_raws.start()
    load_grads = pltpu.make_async_copy(grads_hbm, grads_ref, sems.at[3])
    load_grads.start()
    load_colour = pltpu.make_async_copy(colour_hbm, colour_ref, sems.at[4])
    load_colour.start()
    tiles_ref[pl.ds(ALL_CHUNKS * 8, 8), :] = jnp.zeros((8, 128), F32)
    total_ref[...] = jnp.zeros_like(total_ref)
    load_places.wait()
    extra = jnp.concatenate([places_ref[g, 3] for g in range(GROUPS)], axis=0)
    table_vmem[...] = plan_chunks(extra)
    plan = pltpu.make_async_copy(table_vmem, table_smem, sems.at[1])
    plan.start()
    for g in range(GROUPS):
        for q in range(4):
            tiles_ref[pl.ds(g * CHUNKS * 8 + 4 + q, CHUNKS, stride=8), :] = places_ref[g, q]

    load_grads.wait()
    load_colour.wait()
    row, lane = iota((128, 128), 0), iota((128, 128), 1)
    for part in range(4):
        for v in range(4):
            spread = jnp.where(row == part * 32 + (lane // 16) * 4 + v, 1.0, 0.0)
            wide = exact_dot(grads_ref[...], spread)
            for g in range(GROUPS):
                slot_ref[v, pl.ds(g * CHUNKS + part * 8, 8), :] = wide[g * 8 : g * 8 + 8]
    load_raws.wait()

    def raw(v):
        return jnp.concatenate([raws_ref[g, v] for g in range(GROUPS)], axis=0)

    density = raw(0)
    optical, through, opaque, (step, remains) = march(density, extra)
    light = through * opaque
    mixed = jnp.zeros((ALL_CHUNKS, 128), F32)
    for v in range(3):
        radiance = sigmoid(raw(1 + v))
        grad_colour = slot_ref[v]
        mixed += grad_colour * radiance
        tiles_ref[pl.ds(1 + v, ALL_CHUNKS, stride=8), :] = (
            grad_colour * light * radiance * (1.0 - radiance)
        )
    later = jnp.where((row // 16 == lane // 16) & (row > lane), 1.0, 0.0)
    grad_optical = through * remains * mixed - exact_dot(light * mixed, later) + slot_ref[3]
    tiles_ref[pl.ds(0, ALL_CHUNKS, stride=8), :] = grad_optical * step * sigmoid(density)
    plan.wait()

    lane_group = iota((8, 128), 1) // 16
    pick = lane_group * 16 + iota((8, 128), 0) + 1
    row8 = iota((8, 128), 0)
    first = jnp.where(row8 == 0, 1.0, jnp.where(row8 < 4, BASIS_0, 0.0))

    def one(chunk):
        tile = jnp.zeros((8, 128), F32)
        for p in range(8):
            start = pl.multiple_of(table_smem[p, chunk] * 8, 8)
            part = pltpu.roll(tiles_ref[pl.ds(start, 8), :], table_smem[8 + p, chunk], 1)
            tile = jnp.where(lane_group == p, part, tile)
        hat_x, hat_y, hat_z = hat(tile[4:5]), hat(tile[5:6]), hat(tile[6:7])
        plane = jnp.concatenate([hat_y[y : y + 1] * hat_z for y in range(8)], axis=0)
        basis = jnp.take_along_axis(jnp.broadcast_to(tile[7:8], (8, 128)), pick, axis=1)
        grad = jnp.concatenate([basis * tile[ch : ch + 1] for ch in (1, 2, 3)] + [tile * first], axis=0)
        left = jnp.concatenate(
            [
                jnp.concatenate([grad * hat_x[2 * x + k : 2 * x + k + 1] for x in range(4)], axis=0)
                for k in range(2)
            ],
            axis=1,
        )
        left_high, left_low = split(left)
        high, low = split(plane)
        none = jnp.zeros((64, 128), BF16)

        def both(value):
            return jnp.concatenate(
                [
                    jnp.concatenate([value, none], axis=1),
                    jnp.concatenate([none, value], axis=1),
                ],
                axis=0,
            )

        high, low = both(high), both(low)
        return fast_dot(
            jnp.concatenate([left_high, left_high, left_low], axis=1),
            jnp.concatenate([high, low, high], axis=1),
            NT,
        )

    def several(turn, carry):
        parts = [one(turn * UNROLL + k) for k in range(UNROLL)]
        for k in range(UNROLL):
            b = table_smem[16, turn * UNROLL + k]
            rows = pl.ds(pl.multiple_of(b * 128, 128), 128)
            total_ref[rows, :] += parts[k]
        return carry

    lax.fori_loop(0, (table_smem[17, 0] + UNROLL - 1) // UNROLL, several, 0)

    for c in range(COEF):
        for x in range(4):
            out_ref[c, :, x * 128 : x * 128 + 128] = total_ref[
                pl.ds(x * 32 + ROW_OF[c], BRICKS, stride=128), :
            ]


def gradient(places, raws, grads, colour):
    return pl.pallas_call(
        gradient_kernel,
        out_shape=(
            jax.ShapeDtypeStruct((COEF, BRICKS, VOXELS), F32),
            jax.ShapeDtypeStruct((3, RAYS), F32),
        ),
        in_specs=[ANY] * 4,
        out_specs=(VMEM, VMEM),
        scratch_shapes=[
            pltpu.VMEM((GROUPS, 4, CHUNKS, 128), F32),
            pltpu.VMEM((GROUPS, 4, CHUNKS, 128), F32),
            pltpu.VMEM((GROUPS * 8, 128), F32),
            pltpu.VMEM((ALL_CHUNKS * 8 + 8, 128), F32),
            pltpu.VMEM((24, TABLE), I32),
            pltpu.SMEM((24, TABLE), I32),
            pltpu.VMEM((4, ALL_CHUNKS, 128), F32),
            pltpu.VMEM((BRICKS * 128, 128), F32),
            pltpu.SemaphoreType.DMA((5,)),
        ],
        compiler_params=pltpu.CompilerParams(vmem_limit_bytes=64 << 20),
        name="gradient",
    )(places, raws, grads, colour)


def local(
    bricks, requests, seg_owner, seg_slot, sample_cells, sample_fracs,
    ray_angles, ray_step, pixel_target,
):
    colour, places, raws, grads = render(
        seg_owner.reshape(1, RAYS),
        seg_slot.reshape(1, RAYS),
        jnp.transpose(requests.reshape(OWNERS, 2)),
        sample_cells.reshape(SAMP, RAYS),
        sample_fracs.reshape(3 * SAMP, RAYS),
        ray_angles,
        ray_step.reshape(1, RAYS),
        pixel_target,
        bricks,
    )
    return gradient(places, raws, grads.reshape(GROUPS * 8, 128), colour)


def solution(mesh):
    return jax.shard_map(
        local,
        mesh=mesh,
        in_specs=(
            P(None, "seg", None),
            P("seg", "grp", None, None),
            P("seg", "grp", None),
            P("seg", "grp"),
            P(None, "seg", "grp"),
            P(None, None, "seg", "grp"),
            P(None, "grp"),
            P("grp"),
            P(None, "grp"),
        ),
        out_specs=(P(None, "seg", None), P(None, "grp")),
        check_vma=False,
    )
```

```python
import functools

import jax
import jax.numpy as jnp
from jax import lax
from jax.experimental import pallas as pl
from jax.experimental.pallas import tpu as pltpu
from jax.sharding import PartitionSpec as P

COEF = 28
VOXELS = 512
SAMP = 16
OWNERS = 64
GROUPS = 8
SLOTS = 4
BRICKS = 48
RAYS = 128
CHUNKS = OWNERS * SLOTS // 8
ALL_CHUNKS = GROUPS * CHUNKS
TABLE = 384
UNROLL = 32
BRICK_ROWS = 136
FUNROLL = 8
LOSS_SCALE = 1024.0
BASIS_0 = 0.28209479
ROW_OF = [24] + [
    25 + ch if k == 0 else ch * 8 + k - 1 for ch in range(3) for k in range(9)
]
F32 = jnp.float32
BF16 = jnp.bfloat16
I32 = jnp.int32
VMEM = pl.BlockSpec(memory_space=pltpu.VMEM)
ANY = pl.BlockSpec(memory_space=pl.ANY)
MESH = pl.DeviceIdType.MESH
NN = (((1,), (0,)), ((), ()))
NT = (((1,), (1,)), ((), ()))


def iota(shape, dim):
    return lax.broadcasted_iota(I32, shape, dim)


def exact_dot(a, b, dims=NN):
    return lax.dot_general(
        a, b, dims, precision=lax.Precision.HIGHEST, preferred_element_type=F32
    )


def fast_dot(a, b, dims=NN):
    return lax.dot_general(a, b, dims, preferred_element_type=F32)


def split(value):
    high = value.astype(BF16)
    return high, (value - high.astype(F32)).astype(BF16)


def hat(place):
    return jnp.maximum(1.0 - jnp.abs(place - iota((8, 128), 0).astype(F32)), 0.0)


def softplus(value):
    return jnp.maximum(value, 0.0) + jnp.log1p(jnp.exp(-jnp.abs(value)))


def sigmoid(value):
    return 1.0 / (1.0 + jnp.exp(-value))


def ray_basis(angles):
    polar = angles[0:1]
    azimuth = angles[1:2]
    x = jnp.sin(polar) * jnp.cos(azimuth)
    y = jnp.sin(polar) * jnp.sin(azimuth)
    z = jnp.cos(polar)
    return [
        BASIS_0 * jnp.ones_like(x),
        -0.48860251 * y,
        0.48860251 * z,
        -0.48860251 * x,
        1.09254843 * x * y,
        -1.09254843 * y * z,
        0.31539157 * (2.0 * z * z - x * x - y * y),
        -1.09254843 * x * z,
        0.54627422 * (x * x - y * y),
    ]


def pack(owner, slot, wanted, cells, fracs, basis, step):
    mine = owner == iota((OWNERS, RAYS), 0)
    across = jnp.broadcast_to(owner, (RAYS, RAYS))
    ahead = iota((RAYS, RAYS), 0) < iota((RAYS, RAYS), 1)
    rank = jnp.sum(
        jnp.where((jnp.transpose(across) == across) & ahead, 1, 0), axis=0, keepdims=True
    )
    columns = jnp.transpose(wanted)
    brick = jnp.sum(
        jnp.where(mine, jnp.where(slot == 0, columns[:, 0:1], columns[:, 1:2]), 0),
        axis=0, keepdims=True,
    )
    chosen = [mine & (rank == j) for j in range(SLOTS)]
    choice = jnp.concatenate([jnp.where(one, 1.0, 0.0) for one in chosen], axis=1)
    lane = iota((OWNERS, RAYS), 1) - lax.rem(lax.axis_index("seg"), 32) * SLOTS
    bricks = jnp.zeros((OWNERS, RAYS), I32)
    for j in range(SLOTS):
        named = jnp.sum(jnp.where(chosen[j], brick, 0), axis=1, keepdims=True)
        bricks = jnp.where(lane == j, named, bricks)
    cell_x = (cells * 1338) >> 16
    rest = cells - cell_x * 49
    cell_y = (rest * 9363) >> 16
    cell_z = rest - cell_y * 7
    place_x = cell_x.astype(F32) + fracs[0:16]
    place_y = cell_y.astype(F32) + fracs[16:32]
    place_z = cell_z.astype(F32) + fracs[32:48]
    row = iota((SAMP, RAYS), 0)
    extra = jnp.where(row == 11, 1.0, 0.0)
    for k, value in enumerate(basis + [step, brick.astype(F32) + 1.0]):
        extra = jnp.where(row == k, value, extra)
    none = jnp.zeros((SAMP, RAYS), F32)

    def placed(first, second):
        parts = []
        for j in range(SLOTS):
            rows = [none] * 8
            rows[j] = first
            rows[4 + j] = second
            parts.append(jnp.concatenate(rows, axis=0))
        return jnp.concatenate(parts, axis=1)

    return (
        choice,
        bricks,
        exact_dot(choice, placed(place_x, place_y), NT),
        exact_dot(choice, placed(place_z, extra), NT),
    )


def greet(axes):
    barrier = pltpu.get_barrier_semaphore()
    total = 0
    for axis, count in axes:
        me = lax.axis_index(axis)

        def hail(turn, carry, axis=axis, count=count, me=me):
            pl.semaphore_signal(
                barrier,
                inc=1,
                device_id={axis: lax.rem(me + turn, count)},
                device_id_type=MESH,
            )
            return carry

        lax.fori_loop(1, count, hail, 0, unroll=9 if count == OWNERS else 7)
        total += count - 1
    return lambda: pl.semaphore_wait(barrier, total)


def send_all(axis, count, source, target, send_sem, recv_sem):
    me = lax.axis_index(axis)

    def one(turn, carry):
        peer = lax.rem(me + turn, count)
        pltpu.make_async_remote_copy(
            src_ref=source(peer),
            dst_ref=target.at[me],
            send_sem=send_sem,
            recv_sem=recv_sem,
            device_id={axis: peer},
            device_id_type=MESH,
        ).start()
        return carry

    lax.fori_loop(1, count, one, 0, unroll=9 if count == OWNERS else 7)


def ring_start(ref, step, send_sems, recv_sems):
    me = lax.axis_index("grp")
    for way in range(2 if step < 4 else 1):
        block = lax.rem(me + GROUPS + (step - 1) * (2 * way - 1), GROUPS)
        pltpu.make_async_remote_copy(
            src_ref=ref.at[block],
            dst_ref=ref.at[block],
            send_sem=send_sems.at[way, step - 1],
            recv_sem=recv_sems.at[way, step - 1],
            device_id={"grp": lax.rem(me + GROUPS + 1 - 2 * way, GROUPS)},
            device_id_type=MESH,
        ).start()


def ring_wait(ref, step, sems, arriving):
    me = lax.axis_index("grp")
    for way in range(2 if step < 4 else 1):
        away = step if arriving else step - 1
        part = ref.at[lax.rem(me + GROUPS + away * (2 * way - 1), GROUPS)]
        pltpu.make_async_copy(part, part, sems.at[way, step - 1]).wait()


def wait_all(target, count, sem):
    part = target.at[pl.ds(0, count - 1)]
    pltpu.make_async_copy(part, part, sem).wait()


def lay_out_bricks(bricks_ref, wide_ref, brick_ref):
    for c in range(COEF, 32):
        for x in range(4):
            wide_ref[x, pl.ds(c, BRICKS, stride=32), :] = jnp.zeros((BRICKS, 128), F32)
    for c in range(COEF):
        for x in range(4):
            wide_ref[x, pl.ds(ROW_OF[c], BRICKS, stride=32), :] = bricks_ref[
                c, :, x * 128 : x * 128 + 128
            ].astype(F32)

    def narrow(turn, carry):
        for k in range(8):
            rows = pl.ds(pl.multiple_of(turn * 256 + k * 32, 32), 32)
            for x in range(4):
                brick_ref[turn * 8 + k, :, x * 128 : x * 128 + 128] = wide_ref[
                    x, rows, :
                ].astype(BF16)
        return carry

    lax.fori_loop(0, BRICKS // 8, narrow, 0)


def unpack(got_ref, half_ref, place_ref, basis_ref):
    left = iota((CHUNKS, 128), 1) < 64
    for half in range(2):
        half_ref[...] = got_ref[:, half, :]
        even = half_ref[pl.ds(0, CHUNKS, stride=2), :]
        odd = half_ref[pl.ds(1, CHUNKS, stride=2), :]
        place_ref[2 * half] = jnp.where(left, even, pltpu.roll(odd, 64, 1))
        place_ref[2 * half + 1] = jnp.where(left, pltpu.roll(even, 64, 1), odd)
    row, lane = iota((128, 1024), 0), iota((128, 1024), 1)
    spread = jnp.where(row == ((lane % 128) // 16) * 16 + lane // 128 + 1, 1.0, 0.0)
    basis = exact_dot(place_ref[3], spread)
    for k in range(8):
        basis_ref[pl.ds(k, CHUNKS, stride=8), :] = basis[:, k * 128 : k * 128 + 128]


def interpolate(brick_ref, place_ref, basis_ref, id_smem, raw_ref):
    lane_group = iota((32, 128), 1) // 16

    def one(chunk):
        hat_x = hat(place_ref[0, pl.ds(chunk, 1), :])
        hat_y = hat(place_ref[1, pl.ds(chunk, 1), :])
        hat_z = hat(place_ref[2, pl.ds(chunk, 1), :])
        plane = jnp.concatenate([hat_y[y : y + 1] * hat_z for y in range(8)], axis=0)
        weights = jnp.concatenate([hat_x[x : x + 1] * plane for x in range(8)], axis=0)
        high, low = split(weights)
        rows = []
        for seg in range(8):
            b = id_smem[chunk // 16, lax.rem(chunk, 16) * 8 + seg]
            rows.append(brick_ref[b])
        values = fast_dot(
            jnp.concatenate(rows, axis=0), jnp.concatenate([high, low], axis=1)
        )
        coef = jnp.zeros((32, 128), F32)
        for seg in range(8):
            part = values[seg * 32 : seg * 32 + 32]
            coef = jnp.where(lane_group == seg, part[:, 0:128] + part[:, 128:256], coef)
        basis = basis_ref[pl.ds(pl.multiple_of(chunk * 8, 8), 8), :]
        raw_ref[0, pl.ds(chunk, 1), :] = coef[24:25]
        for ch in range(3):
            raw_ref[1 + ch, pl.ds(chunk, 1), :] = coef[25 + ch : 26 + ch] * BASIS_0 + jnp.sum(
                coef[8 * ch : 8 * ch + 8] * basis, axis=0, keepdims=True
            )

    def several(turn, carry):
        for k in range(FUNROLL):
            one(turn * FUNROLL + k)
        return carry

    lax.fori_loop(0, CHUNKS // FUNROLL, several, 0)


def segment_sums(raw_ref, extra):
    optical, through, opaque, _ = march(raw_ref[0], extra)
    light = through * opaque
    total = jnp.zeros((CHUNKS, 128), F32)
    row, lane = iota((128, 128), 0), iota((128, 128), 1)
    for v in range(4):
        part = optical if v == 3 else light * sigmoid(raw_ref[1 + v])
        total += exact_dot(part, jnp.where(lane == (row // 16) * 8 + v, 1.0, 0.0))
    return total


def march(density, extra):
    row, lane = iota((128, 128), 0), iota((128, 128), 1)
    same = row // 16 == lane // 16
    step = exact_dot(extra, jnp.where(same & (row % 16 == 9), 1.0, 0.0))
    optical = softplus(density) * step
    before = exact_dot(optical, jnp.where(same & (row < lane), 1.0, 0.0))
    through = jnp.exp(-before)
    remains = jnp.exp(-optical)
    return optical, through, 1.0 - remains, (step, remains)


def plan_chunks(extra):
    across = jnp.transpose(extra)
    named = iota((64, ALL_CHUNKS), 0).astype(F32) + 1.0
    hits = [
        jnp.where(across[seg * 16 + 10 : seg * 16 + 11] == named, 1.0, 0.0) for seg in range(8)
    ]
    earlier = jnp.where(
        iota((ALL_CHUNKS, ALL_CHUNKS), 0) < iota((ALL_CHUNKS, ALL_CHUNKS), 1), 1.0, 0.0
    ).astype(BF16)
    counts = fast_dot(jnp.concatenate(hits, axis=0).astype(BF16), earlier)
    carry = jnp.zeros((64, 1), F32)
    ranks = []
    for seg in range(8):
        ranks.append(counts[seg * 64 : seg * 64 + 64] + carry)
        carry = carry + jnp.sum(hits[seg], axis=1, keepdims=True)
    full = jnp.floor((carry + 7.0) * 0.125)
    lower = jnp.where(iota((64, 64), 1) < iota((64, 64), 0), 1.0, 0.0).astype(BF16)
    full_wide = jnp.broadcast_to(full, (64, 128))
    start = fast_dot(lower, full_wide.astype(BF16))
    end = start + full_wide
    start256 = jnp.concatenate([start, start], axis=1)
    selectors, values = [], []
    row = iota((32, ALL_CHUNKS), 0)
    lane = iota((32, ALL_CHUNKS), 1).astype(F32)
    for seg in range(8):
        place = (
            jnp.sum(hits[seg] * (8.0 * start256 + ranks[seg] + 1.0), axis=0, keepdims=True) - 1.0
        )
        chunk = jnp.floor(place * 0.125)
        inside = place - 8.0 * chunk
        selectors.append(
            jnp.where(iota((TABLE, ALL_CHUNKS), 0).astype(F32) == chunk, 1.0, 0.0).astype(BF16)
        )
        kind = jnp.where(
            row < 8, lane, jnp.where(row < 16, float(seg), jnp.where(row < 24, 1.0, 0.0))
        )
        values.append(jnp.where((row % 8).astype(F32) == inside, kind, 0.0).astype(BF16))
    table = fast_dot(
        jnp.concatenate(values, axis=1), jnp.concatenate(selectors, axis=1), NT
    )
    tile = table[0:8] + (1.0 - table[16:24]) * float(ALL_CHUNKS)
    turn = 16.0 * (iota((8, TABLE), 0).astype(F32) - table[8:16])
    turn = jnp.where(turn < 0.0, turn + 128.0, turn)
    place = iota((64, 128), 1).astype(F32)
    real = iota((64, 128), 0) < BRICKS
    owner = [
        jnp.sum(jnp.where((end <= place + 128.0 * k) & real, 1.0, 0.0), axis=0, keepdims=True)
        for k in range(TABLE // 128)
    ]
    owner = jnp.minimum(jnp.concatenate(owner, axis=1), float(BRICKS - 1))
    number = jnp.sum(full_wide, axis=0, keepdims=True)
    number = jnp.concatenate([number] * (TABLE // 128), axis=1)
    last = jnp.where(iota((8, TABLE), 0) == 0, owner, number)
    return jnp.concatenate([tile, turn, last], axis=0).astype(I32)


def shade_all(raws_ref, extra):
    raw = [
        jnp.concatenate([raws_ref[g, v] for g in range(GROUPS)], axis=0) for v in range(4)
    ]
    _, through, opaque, (step, remains) = march(raw[0], extra)
    light = through * opaque
    radiance = [sigmoid(value) for value in raw[1:]]
    return radiance + [light, through * remains, step * sigmoid(raw[0])]


def sample_gradients(grads_ref, shades_ref, slot_ref, tiles_ref):
    row, lane = iota((128, 128), 0), iota((128, 128), 1)
    grads = jnp.concatenate([grads_ref[g] for g in range(GROUPS)], axis=0)
    for part in range(4):
        for v in range(4):
            spread = jnp.where(row == part * 32 + (lane // 16) * 4 + v, 1.0, 0.0)
            wide = exact_dot(grads, spread)
            for g in range(GROUPS):
                slot_ref[v, pl.ds(g * CHUNKS + part * 8, 8), :] = wide[g * 8 : g * 8 + 8]
    light = shades_ref[3]
    mixed = jnp.zeros((ALL_CHUNKS, 128), F32)
    for v in range(3):
        radiance = shades_ref[v]
        grad_colour = slot_ref[v]
        mixed += grad_colour * radiance
        tiles_ref[pl.ds(1 + v, ALL_CHUNKS, stride=8), :] = (
            grad_colour * light * radiance * (1.0 - radiance)
        )
    later = jnp.where((row // 16 == lane // 16) & (row > lane), 1.0, 0.0)
    grad_optical = shades_ref[4] * mixed - exact_dot(light * mixed, later) + slot_ref[3]
    tiles_ref[pl.ds(0, ALL_CHUNKS, stride=8), :] = grad_optical * shades_ref[5]


def to_rays(sums, choice):
    half = lax.rem(lax.axis_index("seg"), 2)
    turned = pltpu.roll(sums, lax.rem(128 - half * 32, 128), 1)
    found = exact_dot(jnp.transpose(turned)[0:32], choice)
    total = jnp.zeros((8, RAYS), F32)
    for j in range(SLOTS):
        total += found[8 * j : 8 * j + 8, RAYS * j : RAYS * j + RAYS]
    return total


def composite(colours, taus, target):
    me = lax.axis_index("seg")
    lower = jnp.where(iota((OWNERS, OWNERS), 1) < iota((OWNERS, OWNERS), 0), 1.0, 0.0)
    through = jnp.exp(-exact_dot(lower, taus))
    depth = iota((OWNERS, RAYS), 0)
    here = jnp.sum(jnp.where(depth == me, through, 0.0), axis=0, keepdims=True)
    colour, grad_colour = [], []
    grad_tau = jnp.zeros((1, RAYS), F32)
    for v in range(3):
        contrib = through * colours[v]
        colour.append(jnp.sum(contrib, axis=0, keepdims=True))
        behind = jnp.sum(jnp.where(depth > me, contrib, 0.0), axis=0, keepdims=True)
        misfit = LOSS_SCALE * (colour[v] - target[v : v + 1])
        grad_colour.append(here * misfit)
        grad_tau -= misfit * behind
    return colour, grad_colour + [grad_tau]


def to_slots(grads, choice):
    me = lax.axis_index("seg")
    row = iota((SLOTS * 4, RAYS), 0)
    block = jnp.zeros((SLOTS * 4, RAYS), F32)
    for v in range(4):
        block = jnp.where(row % 4 == v, grads[v], block)
    wide = jnp.concatenate(
        [jnp.where(row // 4 == j, block, 0.0) for j in range(SLOTS)], axis=1
    )
    wide = jnp.concatenate([wide, jnp.zeros((112, SLOTS * RAYS), F32)], axis=0)
    placed = exact_dot(choice, wide, NT)
    return pltpu.roll(placed, (me // 16) * 32 + lax.rem(me, 2) * 16, 1)


def render_kernel(
    owner_hbm, slot_hbm, wanted_hbm, cells_hbm, fracs_hbm, angles_hbm, step_hbm, target_hbm,
    bricks_hbm,
    colour_ref, tiles_ref, table_ref,
    owner_ref, slot_ref, wanted_ref, cells_ref, fracs_ref, angles_ref, step_ref, target_ref,
    bricks_ref,
    choice_ref, out_ref, got_ref, wide_ref, brick_ref, half_ref, numbers_ref, ids_ref, id_vmem, id_smem,
    place_ref, raw_ref, basis_ref,
    sums_ref, back_ref, ray_ref, rays_ref, slot_out_ref, slots_ref, grads_ref,
    places_ref, raws_ref, all_grads_ref, shades_ref, slot_grads_ref,
    load_sems, send_sems, recv_sems, ring_sends, ring_recvs, own_sem,
):
    loads = [
        pltpu.make_async_copy(source, target, load_sems.at[k])
        for k, (source, target) in enumerate(
            [
                (owner_hbm, owner_ref), (slot_hbm, slot_ref), (wanted_hbm, wanted_ref),
                (cells_hbm, cells_ref), (fracs_hbm, fracs_ref), (angles_hbm, angles_ref),
                (step_hbm, step_ref), (target_hbm, target_ref), (bricks_hbm, bricks_ref),
            ]
        )
    ]
    for load in loads:
        load.start()
    met = greet([("seg", OWNERS), ("grp", GROUPS)])
    for load in loads[:8]:
        load.wait()
    me = lax.axis_index("seg")
    group = lax.axis_index("grp")

    def pass_places(step):
        ring_start(places_ref, step, ring_sends.at[0], ring_recvs.at[0])

    def take_places(step):
        ring_wait(places_ref, step, ring_recvs.at[0], True)

    def pass_raws(step):
        ring_start(raws_ref, step, ring_sends.at[1], ring_recvs.at[1])

    def take_raws(step):
        ring_wait(raws_ref, step, ring_recvs.at[1], True)

    choice, numbers, first, second = pack(
        owner_ref[...], slot_ref[...], wanted_ref[...], cells_ref[...], fracs_ref[...],
        ray_basis(angles_ref[...]), step_ref[...],
    )
    choice_ref[...] = choice
    out_ref[:, 0, :] = first
    out_ref[:, 1, :] = second
    numbers_ref[:, 0, :] = numbers
    met()
    send_all(
        "seg", OWNERS, lambda peer: numbers_ref.at[peer], ids_ref, send_sems.at[7], recv_sems.at[7]
    )
    ids_ref[me] = numbers_ref[me]
    send_all(
        "seg", OWNERS, lambda peer: out_ref.at[peer], got_ref, send_sems.at[0], recv_sems.at[0]
    )
    got_ref[me] = out_ref[me]
    loads[8].wait()
    lay_out_bricks(bricks_ref, wide_ref, brick_ref)
    wait_all(got_ref, OWNERS, recv_sems.at[0])

    unpack(got_ref, half_ref, place_ref, basis_ref)
    extra = place_ref[3]
    places_ref[group] = place_ref[...]
    pass_places(1)
    wait_all(ids_ref, OWNERS, recv_sems.at[7])
    for half in range(2):
        id_vmem[half : half + 1, :] = jnp.sum(
            ids_ref[32 * half : 32 * half + 32, 0, :], axis=0, keepdims=True
        )
    ids = pltpu.make_async_copy(id_vmem, id_smem, own_sem)
    ids.start()
    ids.wait()
    interpolate(brick_ref, place_ref, basis_ref, id_smem, raw_ref)
    take_places(1)
    pass_places(2)
    raws_ref[group] = raw_ref[...]
    pass_raws(1)
    sums_ref[:, 0, :] = segment_sums(raw_ref, extra)

    send_all(
        "seg", OWNERS, lambda peer: sums_ref.at[peer // 2], back_ref,
        send_sems.at[2], recv_sems.at[2],
    )
    back_ref[me] = sums_ref[me // 2]
    take_places(2)
    pass_places(3)
    take_raws(1)
    pass_raws(2)
    wait_all(back_ref, OWNERS, recv_sems.at[2])
    choice = choice_ref[...]
    ray_ref[...] = to_rays(back_ref[:, 0, :], choice)[0:4]

    send_all("seg", OWNERS, lambda peer: ray_ref, rays_ref, send_sems.at[4], recv_sems.at[4])
    rays_ref[me] = ray_ref[...]
    take_places(3)
    pass_places(4)
    take_raws(2)
    pass_raws(3)
    take_places(4)
    all_extra = jnp.concatenate([places_ref[g, 3] for g in range(GROUPS)], axis=0)
    table_ref[...] = plan_chunks(all_extra)
    wait_all(rays_ref, OWNERS, recv_sems.at[4])
    colour, grads = composite(
        [rays_ref[:, v, :] for v in range(3)], rays_ref[:, 3, :], target_ref[...]
    )
    for v in range(3):
        colour_ref[v : v + 1, :] = colour[v]
    slot_out_ref[:, 0, :] = to_slots(grads, choice)

    send_all(
        "seg", OWNERS, lambda peer: slot_out_ref.at[peer], slots_ref,
        send_sems.at[5], recv_sems.at[5],
    )
    slots_ref[me] = slot_out_ref[me]
    take_raws(3)
    pass_raws(4)
    for g in range(GROUPS):
        for q in range(4):
            tiles_ref[pl.ds(g * CHUNKS * 8 + 4 + q, CHUNKS, stride=8), :] = places_ref[g, q]
    wait_all(slots_ref, OWNERS, recv_sems.at[5])
    pick = jnp.where((iota((8, OWNERS), 1) // 2) % 8 == iota((8, OWNERS), 0), 1.0, 0.0)
    grads_ref[...] = exact_dot(pick, slots_ref[:, 0, :])
    send_all(
        "grp", GROUPS, lambda peer: grads_ref, all_grads_ref, send_sems.at[6], recv_sems.at[6]
    )
    all_grads_ref[group] = grads_ref[...]
    take_raws(4)
    for k, value in enumerate(shade_all(raws_ref, all_extra)):
        shades_ref[k] = value
    wait_all(all_grads_ref, GROUPS, recv_sems.at[6])
    sample_gradients(all_grads_ref, shades_ref, slot_grads_ref, tiles_ref)
    wait_all(got_ref, OWNERS, send_sems.at[0])
    wait_all(ids_ref, OWNERS, send_sems.at[7])
    wait_all(back_ref, OWNERS, send_sems.at[2])
    for step in range(1, 5):
        ring_wait(places_ref, step, ring_sends.at[0], False)
        ring_wait(raws_ref, step, ring_sends.at[1], False)
    wait_all(rays_ref, OWNERS, send_sems.at[4])
    wait_all(slots_ref, OWNERS, send_sems.at[5])
    wait_all(all_grads_ref, GROUPS, send_sems.at[6])


def render(*operands):
    return pl.pallas_call(
        render_kernel,
        out_shape=(
            jax.ShapeDtypeStruct((3, RAYS), F32),
            jax.ShapeDtypeStruct((ALL_CHUNKS * 8, 128), F32),
            jax.ShapeDtypeStruct((24, TABLE), I32),
        ),
        in_specs=[ANY] * 9,
        out_specs=(VMEM, VMEM, VMEM),
        scratch_shapes=[pltpu.VMEM(x.shape, x.dtype) for x in operands]
        + [
            pltpu.VMEM((OWNERS, SLOTS * RAYS), F32),
            pltpu.VMEM((OWNERS, 2, 128), F32),
            pltpu.VMEM((OWNERS, 2, 128), F32),
            pltpu.VMEM((4, BRICKS * 32, 128), F32),
            pltpu.VMEM((BRICKS, 32, VOXELS), BF16),
            pltpu.VMEM((OWNERS, 128), F32),
            pltpu.VMEM((OWNERS, 1, 128), I32),
            pltpu.VMEM((OWNERS, 1, 128), I32),
            pltpu.VMEM((2, 128), I32),
            pltpu.SMEM((2, 128), I32),
            pltpu.VMEM((4, CHUNKS, 128), F32),
            pltpu.VMEM((4, CHUNKS, 128), F32),
            pltpu.VMEM((CHUNKS * 8, 128), F32),
            pltpu.VMEM((CHUNKS, 1, 128), F32),
            pltpu.VMEM((OWNERS, 1, 128), F32),
            pltpu.VMEM((4, RAYS), F32),
            pltpu.VMEM((OWNERS, 4, RAYS), F32),
            pltpu.VMEM((OWNERS, 1, 128), F32),
            pltpu.VMEM((OWNERS, 1, 128), F32),
            pltpu.VMEM((8, 128), F32),
            pltpu.VMEM((GROUPS, 4, CHUNKS, 128), F32),
            pltpu.VMEM((GROUPS, 4, CHUNKS, 128), F32),
            pltpu.VMEM((GROUPS, 8, 128), F32),
            pltpu.VMEM((6, ALL_CHUNKS, 128), F32),
            pltpu.VMEM((4, ALL_CHUNKS, 128), F32),
            pltpu.SemaphoreType.DMA((9,)),
            pltpu.SemaphoreType.DMA((8,)),
            pltpu.SemaphoreType.DMA((8,)),
            pltpu.SemaphoreType.DMA((2, 2, 4)),
            pltpu.SemaphoreType.DMA((2, 2, 4)),
            pltpu.SemaphoreType.DMA,
        ],
        compiler_params=pltpu.CompilerParams(
            collective_id=0, has_side_effects=True, vmem_limit_bytes=64 << 20
        ),
        name="render",
    )(*operands)


def gradient_kernel(
    tiles_hbm, table_hbm, colour_hbm, out_hbm, colour_ref,
    tiles_ref, table_smem, total_ref, out_ref, sems, out_sems,
):
    loads = [
        pltpu.make_async_copy(table_hbm, table_smem, sems.at[0]),
        pltpu.make_async_copy(tiles_hbm, tiles_ref.at[pl.ds(0, ALL_CHUNKS * 8)], sems.at[1]),
        pltpu.make_async_copy(colour_hbm, colour_ref, sems.at[2]),
    ]
    for load in loads:
        load.start()
    tiles_ref[pl.ds(ALL_CHUNKS * 8, 8), :] = jnp.zeros((8, 128), F32)
    total_ref[...] = jnp.zeros_like(total_ref)
    for load in loads:
        load.wait()

    lane_group = iota((8, 128), 1) // 16
    pick = lane_group * 16 + iota((8, 128), 0) + 1
    row8 = iota((8, 128), 0)
    first = jnp.where(row8 == 0, 1.0, jnp.where(row8 < 4, BASIS_0, 0.0))

    def one(chunk):
        tile = jnp.zeros((8, 128), F32)
        for p in range(8):
            start = pl.multiple_of(table_smem[p, chunk] * 8, 8)
            part = pltpu.roll(tiles_ref[pl.ds(start, 8), :], table_smem[8 + p, chunk], 1)
            tile = jnp.where(lane_group == p, part, tile)
        hat_x, hat_y, hat_z = hat(tile[4:5]), hat(tile[5:6]), hat(tile[6:7])
        plane = jnp.concatenate([hat_y[y : y + 1] * hat_z for y in range(8)], axis=0)
        basis = jnp.take_along_axis(jnp.broadcast_to(tile[7:8], (8, 128)), pick, axis=1)
        grad = jnp.concatenate([basis * tile[ch : ch + 1] for ch in (1, 2, 3)] + [tile * first], axis=0)
        left = jnp.concatenate(
            [
                jnp.concatenate([grad * hat_x[2 * x + k : 2 * x + k + 1] for x in range(4)], axis=0)
                for k in range(2)
            ],
            axis=1,
        )
        left_high, left_low = split(left)
        high, low = split(plane)
        none = jnp.zeros((64, 128), BF16)

        def both(value):
            return jnp.concatenate(
                [
                    jnp.concatenate([value, none], axis=1),
                    jnp.concatenate([none, value], axis=1),
                ],
                axis=0,
            )

        high, low = both(high), both(low)
        return fast_dot(
            jnp.concatenate([left_high, left_high, left_low], axis=1),
            jnp.concatenate([high, low, high], axis=1),
            NT,
        )

    def several(turn, carry):
        parts = [one(turn * UNROLL + k) for k in range(UNROLL)]
        for k in range(UNROLL):
            b = table_smem[16, turn * UNROLL + k]
            rows = pl.ds(pl.multiple_of(b * BRICK_ROWS, 8), 128)
            total_ref[rows, :] += parts[k]
        return carry

    lax.fori_loop(0, (table_smem[17, 0] + UNROLL - 1) // UNROLL, several, 0)

    outs = []
    for c in range(COEF):
        for x in range(4):
            out_ref[c, :, x * 128 : x * 128 + 128] = total_ref[
                pl.ds(x * 32 + ROW_OF[c], BRICKS, stride=BRICK_ROWS), :
            ]
        outs.append(pltpu.make_async_copy(out_ref.at[c], out_hbm.at[c], out_sems.at[c]))
        outs[c].start()
    for out in outs:
        out.wait()


def gradient(tiles, table, colour):
    return pl.pallas_call(
        gradient_kernel,
        out_shape=(
            jax.ShapeDtypeStruct((COEF, BRICKS, VOXELS), F32),
            jax.ShapeDtypeStruct((3, RAYS), F32),
        ),
        in_specs=[ANY] * 3,
        out_specs=(ANY, VMEM),
        scratch_shapes=[
            pltpu.VMEM((ALL_CHUNKS * 8 + 8, 128), F32),
            pltpu.SMEM((24, TABLE), I32),
            pltpu.VMEM((BRICKS * BRICK_ROWS, 128), F32),
            pltpu.VMEM((COEF, BRICKS, VOXELS), F32),
            pltpu.SemaphoreType.DMA((3,)),
            pltpu.SemaphoreType.DMA((COEF,)),
        ],
        compiler_params=pltpu.CompilerParams(vmem_limit_bytes=64 << 20),
        name="gradient",
    )(tiles, table, colour)


def local(
    bricks, requests, seg_owner, seg_slot, sample_cells, sample_fracs,
    ray_angles, ray_step, pixel_target,
):
    colour, tiles, table = render(
        seg_owner.reshape(1, RAYS),
        seg_slot.reshape(1, RAYS),
        jnp.transpose(requests.reshape(OWNERS, 2)),
        sample_cells.reshape(SAMP, RAYS),
        sample_fracs.reshape(3 * SAMP, RAYS),
        ray_angles,
        ray_step.reshape(1, RAYS),
        pixel_target,
        bricks,
    )
    return gradient(tiles, table, colour)


def solution(mesh):
    return jax.shard_map(
        local,
        mesh=mesh,
        in_specs=(
            P(None, "seg", None),
            P("seg", "grp", None, None),
            P("seg", "grp", None),
            P("seg", "grp"),
            P(None, "seg", "grp"),
            P(None, None, "seg", "grp"),
            P(None, "grp"),
            P("grp"),
            P(None, "grp"),
        ),
        out_specs=(P(None, "seg", None), P(None, "grp")),
        check_vma=False,
    )
```

```python
import functools

import jax
import jax.numpy as jnp
from jax import lax
from jax.experimental import pallas as pl
from jax.experimental.pallas import tpu as pltpu
from jax.sharding import PartitionSpec as P

COEF = 28
VOXELS = 512
SAMP = 16
OWNERS = 64
GROUPS = 8
SLOTS = 4
BRICKS = 48
RAYS = 128
CHUNKS = OWNERS * SLOTS // 8
ALL_CHUNKS = GROUPS * CHUNKS
TABLE = 384
UNROLL = 32
BRICK_ROWS = 136
FUNROLL = 8
LOSS_SCALE = 1024.0
BASIS_0 = 0.28209479
ROW_OF = [24] + [
    25 + ch if k == 0 else ch * 8 + k - 1 for ch in range(3) for k in range(9)
]
F32 = jnp.float32
BF16 = jnp.bfloat16
I32 = jnp.int32
VMEM = pl.BlockSpec(memory_space=pltpu.VMEM)
ANY = pl.BlockSpec(memory_space=pl.ANY)
MESH = pl.DeviceIdType.MESH
NN = (((1,), (0,)), ((), ()))
NT = (((1,), (1,)), ((), ()))


def iota(shape, dim):
    return lax.broadcasted_iota(I32, shape, dim)


def exact_dot(a, b, dims=NN):
    return lax.dot_general(
        a, b, dims, precision=lax.Precision.HIGHEST, preferred_element_type=F32
    )


def fast_dot(a, b, dims=NN):
    return lax.dot_general(a, b, dims, preferred_element_type=F32)


def split(value):
    high = value.astype(BF16)
    return high, (value - high.astype(F32)).astype(BF16)


def hat(place):
    return jnp.maximum(1.0 - jnp.abs(place - iota((8, 128), 0).astype(F32)), 0.0)


def softplus(value):
    return jnp.maximum(value, 0.0) + jnp.log1p(jnp.exp(-jnp.abs(value)))


def sigmoid(value):
    return 1.0 / (1.0 + jnp.exp(-value))


def ray_basis(angles):
    polar = angles[0:1]
    azimuth = angles[1:2]
    x = jnp.sin(polar) * jnp.cos(azimuth)
    y = jnp.sin(polar) * jnp.sin(azimuth)
    z = jnp.cos(polar)
    return [
        BASIS_0 * jnp.ones_like(x),
        -0.48860251 * y,
        0.48860251 * z,
        -0.48860251 * x,
        1.09254843 * x * y,
        -1.09254843 * y * z,
        0.31539157 * (2.0 * z * z - x * x - y * y),
        -1.09254843 * x * z,
        0.54627422 * (x * x - y * y),
    ]


def pack(owner, slot, wanted, cells, fracs, basis, step):
    mine = owner == iota((OWNERS, RAYS), 0)
    across = jnp.broadcast_to(owner, (RAYS, RAYS))
    ahead = iota((RAYS, RAYS), 0) < iota((RAYS, RAYS), 1)
    rank = jnp.sum(
        jnp.where((jnp.transpose(across) == across) & ahead, 1, 0), axis=0, keepdims=True
    )
    columns = jnp.transpose(wanted)
    brick = jnp.sum(
        jnp.where(mine, jnp.where(slot == 0, columns[:, 0:1], columns[:, 1:2]), 0),
        axis=0, keepdims=True,
    )
    chosen = [mine & (rank == j) for j in range(SLOTS)]
    choice = jnp.concatenate([jnp.where(one, 1.0, 0.0) for one in chosen], axis=1)
    lane = iota((OWNERS, RAYS), 1) - lax.rem(lax.axis_index("seg"), 32) * SLOTS
    spots = owner * SLOTS + rank
    bricks = jnp.zeros((OWNERS, RAYS), I32)
    for j in range(SLOTS):
        named = jnp.sum(jnp.where(chosen[j], brick, 0), axis=1, keepdims=True)
        bricks = jnp.where(lane == j, named, bricks)
    cell_x = (cells * 1338) >> 16
    rest = cells - cell_x * 49
    cell_y = (rest * 9363) >> 16
    cell_z = rest - cell_y * 7
    place_x = cell_x.astype(F32) + fracs[0:16]
    place_y = cell_y.astype(F32) + fracs[16:32]
    place_z = cell_z.astype(F32) + fracs[32:48]
    row = iota((SAMP, RAYS), 0)
    extra = jnp.where(row == 11, 1.0, 0.0)
    for k, value in enumerate(basis + [step, brick.astype(F32) + 1.0]):
        extra = jnp.where(row == k, value, extra)
    none = jnp.zeros((SAMP, RAYS), F32)

    def placed(first, second):
        parts = []
        for j in range(SLOTS):
            rows = [none] * 8
            rows[j] = first
            rows[4 + j] = second
            parts.append(jnp.concatenate(rows, axis=0))
        return jnp.concatenate(parts, axis=1)

    return (
        spots,
        bricks,
        exact_dot(choice, placed(place_x, place_y), NT),
        exact_dot(choice, placed(place_z, extra), NT),
    )


def greet(axes):
    barrier = pltpu.get_barrier_semaphore()
    total = 0
    for axis, count in axes:
        me = lax.axis_index(axis)

        def hail(turn, carry, axis=axis, count=count, me=me):
            pl.semaphore_signal(
                barrier,
                inc=1,
                device_id={axis: lax.rem(me + turn, count)},
                device_id_type=MESH,
            )
            return carry

        lax.fori_loop(1, count, hail, 0, unroll=9 if count == OWNERS else 7)
        total += count - 1
    return lambda: pl.semaphore_wait(barrier, total)


def send_all(axis, count, source, target, send_sem, recv_sem):
    me = lax.axis_index(axis)

    def one(turn, carry):
        peer = lax.rem(me + turn, count)
        pltpu.make_async_remote_copy(
            src_ref=source(peer),
            dst_ref=target.at[me],
            send_sem=send_sem,
            recv_sem=recv_sem,
            device_id={axis: peer},
            device_id_type=MESH,
        ).start()
        return carry

    lax.fori_loop(1, count, one, 0, unroll=9 if count == OWNERS else 7)


def ring_start(ref, step, send_sems, recv_sems):
    me = lax.axis_index("grp")
    for way in range(2 if step < 4 else 1):
        block = lax.rem(me + GROUPS + (step - 1) * (2 * way - 1), GROUPS)
        pltpu.make_async_remote_copy(
            src_ref=ref.at[block],
            dst_ref=ref.at[block],
            send_sem=send_sems.at[way, step - 1],
            recv_sem=recv_sems.at[way, step - 1],
            device_id={"grp": lax.rem(me + GROUPS + 1 - 2 * way, GROUPS)},
            device_id_type=MESH,
        ).start()


def ring_wait(ref, step, sems, arriving):
    me = lax.axis_index("grp")
    for way in range(2 if step < 4 else 1):
        away = step if arriving else step - 1
        part = ref.at[lax.rem(me + GROUPS + away * (2 * way - 1), GROUPS)]
        pltpu.make_async_copy(part, part, sems.at[way, step - 1]).wait()


def wait_all(target, count, sem):
    part = target.at[pl.ds(0, count - 1)]
    pltpu.make_async_copy(part, part, sem).wait()


def lay_out_bricks(bricks_ref, wide_ref, brick_ref):
    for c in range(COEF, 32):
        for x in range(4):
            wide_ref[x, pl.ds(c, BRICKS, stride=40), :] = jnp.zeros((BRICKS, 128), F32)
    for c in range(COEF):
        for x in range(4):
            wide_ref[x, pl.ds(ROW_OF[c], BRICKS, stride=40), :] = bricks_ref[
                c, :, x * 128 : x * 128 + 128
            ].astype(F32)

    def narrow(turn, carry):
        for k in range(8):
            rows = pl.ds(pl.multiple_of(turn * 320 + k * 40, 8), 32)
            for x in range(4):
                brick_ref[turn * 8 + k, :, x * 128 : x * 128 + 128] = wide_ref[
                    x, rows, :
                ].astype(BF16)
        return carry

    lax.fori_loop(0, BRICKS // 8, narrow, 0)


def unpack(got_ref, half_ref, place_ref, basis_ref):
    left = iota((CHUNKS, 128), 1) < 64
    for half in range(2):
        half_ref[...] = got_ref[:, half, :]
        even = half_ref[pl.ds(0, CHUNKS, stride=2), :]
        odd = half_ref[pl.ds(1, CHUNKS, stride=2), :]
        place_ref[2 * half] = jnp.where(left, even, pltpu.roll(odd, 64, 1))
        place_ref[2 * half + 1] = jnp.where(left, pltpu.roll(even, 64, 1), odd)
    row, lane = iota((128, 1024), 0), iota((128, 1024), 1)
    spread = jnp.where(row == ((lane % 128) // 16) * 16 + lane // 128 + 1, 1.0, 0.0)
    basis = exact_dot(place_ref[3], spread)
    for k in range(8):
        basis_ref[pl.ds(k, CHUNKS, stride=8), :] = basis[:, k * 128 : k * 128 + 128]


def interpolate(brick_ref, place_ref, basis_ref, id_smem, raw_ref):
    lane_group = iota((32, 128), 1) // 16

    def one(chunk):
        hat_x = hat(place_ref[0, pl.ds(chunk, 1), :])
        hat_y = hat(place_ref[1, pl.ds(chunk, 1), :])
        hat_z = hat(place_ref[2, pl.ds(chunk, 1), :])
        plane = jnp.concatenate([hat_y[y : y + 1] * hat_z for y in range(8)], axis=0)
        weights = jnp.concatenate([hat_x[x : x + 1] * plane for x in range(8)], axis=0)
        high, low = split(weights)
        rows = []
        for seg in range(8):
            b = id_smem[chunk // 16, lax.rem(chunk, 16) * 8 + seg]
            rows.append(brick_ref[b])
        values = fast_dot(
            jnp.concatenate(rows, axis=0), jnp.concatenate([high, low], axis=1)
        )
        coef = jnp.zeros((32, 128), F32)
        for seg in range(8):
            part = values[seg * 32 : seg * 32 + 32]
            coef = jnp.where(lane_group == seg, part[:, 0:128] + part[:, 128:256], coef)
        basis = basis_ref[pl.ds(pl.multiple_of(chunk * 8, 8), 8), :]
        raw_ref[0, pl.ds(chunk, 1), :] = coef[24:25]
        for ch in range(3):
            raw_ref[1 + ch, pl.ds(chunk, 1), :] = coef[25 + ch : 26 + ch] * BASIS_0 + jnp.sum(
                coef[8 * ch : 8 * ch + 8] * basis, axis=0, keepdims=True
            )

    def several(turn, carry):
        for k in range(FUNROLL):
            one(turn * FUNROLL + k)
        return carry

    lax.fori_loop(0, CHUNKS // FUNROLL, several, 0)


def segment_sums(raw_ref, extra):
    optical, through, opaque, _ = march(raw_ref[0], extra)
    light = through * opaque
    total = jnp.zeros((CHUNKS, 128), F32)
    row, lane = iota((128, 128), 0), iota((128, 128), 1)
    for v in range(4):
        part = optical if v == 3 else light * sigmoid(raw_ref[1 + v])
        total += exact_dot(part, jnp.where(lane == (row // 16) * 4 + v, 1.0, 0.0))
    return sum(pltpu.roll(total[8 * k : 8 * k + 8], 32 * k, 1) if k else total[0:8] for k in range(4))


def march(density, extra):
    row, lane = iota((128, 128), 0), iota((128, 128), 1)
    same = row // 16 == lane // 16
    step = exact_dot(extra, jnp.where(same & (row % 16 == 9), 1.0, 0.0))
    optical = softplus(density) * step
    before = exact_dot(optical, jnp.where(same & (row < lane), 1.0, 0.0))
    through = jnp.exp(-before)
    remains = jnp.exp(-optical)
    return optical, through, 1.0 - remains, (step, remains)


def plan_chunks(extra):
    across = jnp.transpose(extra)
    named = iota((64, ALL_CHUNKS), 0).astype(F32) + 1.0
    hits = [
        jnp.where(across[seg * 16 + 10 : seg * 16 + 11] == named, 1.0, 0.0) for seg in range(8)
    ]
    earlier = jnp.where(
        iota((ALL_CHUNKS, ALL_CHUNKS), 0) < iota((ALL_CHUNKS, ALL_CHUNKS), 1), 1.0, 0.0
    ).astype(BF16)
    counts = fast_dot(jnp.concatenate(hits, axis=0).astype(BF16), earlier)
    carry = jnp.zeros((64, 1), F32)
    ranks = []
    for seg in range(8):
        ranks.append(counts[seg * 64 : seg * 64 + 64] + carry)
        carry = carry + jnp.sum(hits[seg], axis=1, keepdims=True)
    full = jnp.floor((carry + 7.0) * 0.125)
    lower = jnp.where(iota((64, 64), 1) < iota((64, 64), 0), 1.0, 0.0).astype(BF16)
    full_wide = jnp.broadcast_to(full, (64, 128))
    start = fast_dot(lower, full_wide.astype(BF16))
    end = start + full_wide
    start256 = jnp.concatenate([start, start], axis=1)
    selectors, values = [], []
    row = iota((32, ALL_CHUNKS), 0)
    lane = iota((32, ALL_CHUNKS), 1).astype(F32)
    for seg in range(8):
        place = (
            jnp.sum(hits[seg] * (8.0 * start256 + ranks[seg] + 1.0), axis=0, keepdims=True) - 1.0
        )
        chunk = jnp.floor(place * 0.125)
        inside = place - 8.0 * chunk
        selectors.append(
            jnp.where(iota((TABLE, ALL_CHUNKS), 0).astype(F32) == chunk, 1.0, 0.0).astype(BF16)
        )
        kind = jnp.where(
            row < 8, lane, jnp.where(row < 16, float(seg), jnp.where(row < 24, 1.0, 0.0))
        )
        values.append(jnp.where((row % 8).astype(F32) == inside, kind, 0.0).astype(BF16))
    table = fast_dot(
        jnp.concatenate(values, axis=1), jnp.concatenate(selectors, axis=1), NT
    )
    tile = table[0:8] + (1.0 - table[16:24]) * float(ALL_CHUNKS)
    turn = 16.0 * (iota((8, TABLE), 0).astype(F32) - table[8:16])
    turn = jnp.where(turn < 0.0, turn + 128.0, turn)
    place = iota((64, 128), 1).astype(F32)
    real = iota((64, 128), 0) < BRICKS
    owner = [
        jnp.sum(jnp.where((end <= place + 128.0 * k) & real, 1.0, 0.0), axis=0, keepdims=True)
        for k in range(TABLE // 128)
    ]
    owner = jnp.minimum(jnp.concatenate(owner, axis=1), float(BRICKS - 1))
    number = jnp.sum(full_wide, axis=0, keepdims=True)
    number = jnp.concatenate([number] * (TABLE // 128), axis=1)
    last = jnp.where(iota((8, TABLE), 0) == 0, owner, number)
    return jnp.concatenate([tile, turn, last], axis=0).astype(I32)


def shade_all(raws_ref, extra):
    raw = [
        jnp.concatenate([raws_ref[g, v] for g in range(GROUPS)], axis=0) for v in range(4)
    ]
    _, through, opaque, (step, remains) = march(raw[0], extra)
    light = through * opaque
    radiance = [sigmoid(value) for value in raw[1:]]
    return radiance + [light, through * remains, step * sigmoid(raw[0])]


def sample_gradients(grads_ref, shades_ref, slot_ref, tiles_ref):
    row, lane = iota((128, 128), 0), iota((128, 128), 1)
    grads = jnp.concatenate([grads_ref[g] for g in range(GROUPS)], axis=0)
    for part in range(4):
        for v in range(4):
            spread = jnp.where(row == part * 32 + (lane // 16) * 4 + v, 1.0, 0.0)
            wide = exact_dot(grads, spread)
            for g in range(GROUPS):
                slot_ref[v, pl.ds(g * CHUNKS + part * 8, 8), :] = wide[g * 8 : g * 8 + 8]
    light = shades_ref[3]
    mixed = jnp.zeros((ALL_CHUNKS, 128), F32)
    for v in range(3):
        radiance = shades_ref[v]
        grad_colour = slot_ref[v]
        mixed += grad_colour * radiance
        tiles_ref[pl.ds(1 + v, ALL_CHUNKS, stride=8), :] = (
            grad_colour * light * radiance * (1.0 - radiance)
        )
    later = jnp.where((row // 16 == lane // 16) & (row > lane), 1.0, 0.0)
    grad_optical = shades_ref[4] * mixed - exact_dot(light * mixed, later) + slot_ref[3]
    tiles_ref[pl.ds(0, ALL_CHUNKS, stride=8), :] = grad_optical * shades_ref[5]


def to_rays(sums_ref, spots_ref, rays_ref):
    owner = iota((OWNERS, RAYS), 0)
    slot = iota((16, RAYS), 0) // 4
    for row in range(8):
        across = jnp.transpose(sums_ref[:, row, :])
        high, rest = split(across)
        middle, low = split(across - high.astype(F32))
        for part in range(4):
            for half in range(2):
                s = 2 * (part * 8 + row) + half
                rows = slice(part * 32 + half * 16, part * 32 + half * 16 + 16)
                spots = spots_ref[s, 1:2, :]
                hits = jnp.where(spots // SLOTS == owner, 1.0, 0.0).astype(BF16)
                three = fast_dot(
                    jnp.concatenate([high[rows], middle[rows], low[rows]], axis=0), hits
                )
                found = three[0:16] + three[16:32] + three[32:48]
                found = jnp.where(spots % SLOTS == slot, found, 0.0)
                found = found[0:8] + found[8:16]
                rays_ref[s] = found[0:4] + found[4:8]


def composite(colours, taus, target):
    depth, other = iota((OWNERS, OWNERS), 0), iota((OWNERS, OWNERS), 1)
    through = jnp.exp(-exact_dot(jnp.where(other < depth, 1.0, 0.0), taus))
    behind = jnp.where(other > depth, 1.0, 0.0)
    colour, grads = [], []
    grad_tau = jnp.zeros((OWNERS, RAYS), F32)
    for v in range(3):
        contrib = through * colours[v]
        colour.append(jnp.sum(contrib, axis=0, keepdims=True))
        misfit = LOSS_SCALE * (colour[v] - target[v : v + 1])
        grads.append(through * misfit)
        grad_tau -= misfit * exact_dot(behind, contrib)
    return colour, grads + [grad_tau]


def to_slots(grads, spots):
    me = lax.axis_index("seg")
    depth = iota((OWNERS, 128), 0)
    place = iota((OWNERS, 128), 1) - (depth // 16) * 32 - (depth % 2) * 16
    placed = jnp.zeros((OWNERS, 128), F32)
    for j in range(SLOTS):
        here = spots == me * SLOTS + j
        for v in range(4):
            value = jnp.sum(jnp.where(here, grads[v], 0.0), axis=1, keepdims=True)
            placed = jnp.where(place == j * 4 + v, value, placed)
    pick = jnp.where((iota((8, OWNERS), 1) // 2) % 8 == iota((8, OWNERS), 0), 1.0, 0.0)
    return exact_dot(pick, placed)


def render_kernel(
    owner_hbm, slot_hbm, wanted_hbm, cells_hbm, fracs_hbm, angles_hbm, step_hbm, target_hbm,
    bricks_hbm,
    colour_ref, tiles_ref, table_ref,
    owner_ref, slot_ref, wanted_ref, cells_ref, fracs_ref, angles_ref, step_ref, target_ref,
    bricks_ref,
    out_ref, got_ref, wide_ref, brick_ref, half_ref, numbers_ref, ids_ref, id_vmem, id_smem,
    place_ref, raw_ref, basis_ref,
    sums_ref, all_sums_ref, rays_ref, grads_ref,
    places_ref, raws_ref, all_grads_ref, shades_ref, slot_grads_ref,
    load_sems, send_sems, recv_sems, ring_sends, ring_recvs, own_sem,
):
    loads = [
        pltpu.make_async_copy(source, target, load_sems.at[k])
        for k, (source, target) in enumerate(
            [
                (owner_hbm, owner_ref), (slot_hbm, slot_ref), (wanted_hbm, wanted_ref),
                (cells_hbm, cells_ref), (fracs_hbm, fracs_ref), (angles_hbm, angles_ref),
                (step_hbm, step_ref), (target_hbm, target_ref), (bricks_hbm, bricks_ref),
            ]
        )
    ]
    for load in loads:
        load.start()
    met = greet([("seg", OWNERS), ("grp", GROUPS)])
    for load in loads[:8]:
        load.wait()
    me = lax.axis_index("seg")
    group = lax.axis_index("grp")

    def pass_places(step):
        ring_start(places_ref, step, ring_sends.at[0], ring_recvs.at[0])

    def take_places(step):
        ring_wait(places_ref, step, ring_recvs.at[0], True)

    def pass_raws(step):
        ring_start(raws_ref, step, ring_sends.at[1], ring_recvs.at[1])

    def take_raws(step):
        ring_wait(raws_ref, step, ring_recvs.at[1], True)

    spots, numbers, first, second = pack(
        owner_ref[...], slot_ref[...], wanted_ref[...], cells_ref[...], fracs_ref[...],
        ray_basis(angles_ref[...]), step_ref[...],
    )
    out_ref[:, 0, :] = first
    out_ref[:, 1, :] = second
    numbers_ref[:, 0, :] = numbers
    numbers_ref[:, 1, :] = jnp.broadcast_to(spots, (OWNERS, RAYS))
    met()
    send_all(
        "seg", OWNERS, lambda peer: numbers_ref.at[peer], ids_ref, send_sems.at[7], recv_sems.at[7]
    )
    ids_ref[me] = numbers_ref[me]
    send_all(
        "seg", OWNERS, lambda peer: out_ref.at[peer], got_ref, send_sems.at[0], recv_sems.at[0]
    )
    got_ref[me] = out_ref[me]
    loads[8].wait()
    lay_out_bricks(bricks_ref, wide_ref, brick_ref)
    wait_all(got_ref, OWNERS, recv_sems.at[0])

    unpack(got_ref, half_ref, place_ref, basis_ref)
    extra = place_ref[3]
    places_ref[group] = place_ref[...]
    pass_places(1)
    wait_all(ids_ref, OWNERS, recv_sems.at[7])
    for half in range(2):
        id_vmem[half : half + 1, :] = jnp.sum(
            ids_ref[32 * half : 32 * half + 32, 0, :], axis=0, keepdims=True
        )
    ids = pltpu.make_async_copy(id_vmem, id_smem, own_sem)
    ids.start()
    ids.wait()
    interpolate(brick_ref, place_ref, basis_ref, id_smem, raw_ref)
    take_places(1)
    pass_places(2)
    raws_ref[group] = raw_ref[...]
    pass_raws(1)
    sums_ref[...] = segment_sums(raw_ref, extra)

    send_all(
        "seg", OWNERS, lambda peer: sums_ref, all_sums_ref, send_sems.at[2], recv_sems.at[2]
    )
    all_sums_ref[me] = sums_ref[...]
    take_places(2)
    pass_places(3)
    take_raws(1)
    pass_raws(2)
    take_places(3)
    pass_places(4)
    take_raws(2)
    pass_raws(3)
    wait_all(all_sums_ref, OWNERS, recv_sems.at[2])
    to_rays(all_sums_ref, ids_ref, rays_ref)
    take_raws(3)
    pass_raws(4)
    colour, grads = composite(
        [rays_ref[:, v, :] for v in range(3)], rays_ref[:, 3, :], target_ref[...]
    )
    for v in range(3):
        colour_ref[v : v + 1, :] = colour[v]
    grads_ref[...] = to_slots(grads, ids_ref[:, 1, :])

    send_all(
        "grp", GROUPS, lambda peer: grads_ref, all_grads_ref, send_sems.at[6], recv_sems.at[6]
    )
    all_grads_ref[group] = grads_ref[...]
    take_places(4)
    all_extra = jnp.concatenate([places_ref[g, 3] for g in range(GROUPS)], axis=0)
    table_ref[...] = plan_chunks(all_extra)
    for g in range(GROUPS):
        for q in range(4):
            tiles_ref[pl.ds(g * CHUNKS * 8 + 4 + q, CHUNKS, stride=8), :] = places_ref[g, q]
    take_raws(4)
    for k, value in enumerate(shade_all(raws_ref, all_extra)):
        shades_ref[k] = value
    wait_all(all_grads_ref, GROUPS, recv_sems.at[6])
    sample_gradients(all_grads_ref, shades_ref, slot_grads_ref, tiles_ref)
    wait_all(got_ref, OWNERS, send_sems.at[0])
    wait_all(ids_ref, OWNERS, send_sems.at[7])
    wait_all(all_sums_ref, OWNERS, send_sems.at[2])
    for step in range(1, 5):
        ring_wait(places_ref, step, ring_sends.at[0], False)
        ring_wait(raws_ref, step, ring_sends.at[1], False)
    wait_all(all_grads_ref, GROUPS, send_sems.at[6])


def render(*operands):
    return pl.pallas_call(
        render_kernel,
        out_shape=(
            jax.ShapeDtypeStruct((3, RAYS), F32),
            jax.ShapeDtypeStruct((ALL_CHUNKS * 8, 128), F32),
            jax.ShapeDtypeStruct((24, TABLE), I32),
        ),
        in_specs=[ANY] * 9,
        out_specs=(VMEM, VMEM, VMEM),
        scratch_shapes=[pltpu.VMEM(x.shape, x.dtype) for x in operands]
        + [
            pltpu.VMEM((OWNERS, 2, 128), F32),
            pltpu.VMEM((OWNERS, 2, 128), F32),
            pltpu.VMEM((4, BRICKS * 40, 128), F32),
            pltpu.VMEM((BRICKS, 32, VOXELS), BF16),
            pltpu.VMEM((OWNERS, 128), F32),
            pltpu.VMEM((OWNERS, 2, 128), I32),
            pltpu.VMEM((OWNERS, 2, 128), I32),
            pltpu.VMEM((2, 128), I32),
            pltpu.SMEM((2, 128), I32),
            pltpu.VMEM((4, CHUNKS, 128), F32),
            pltpu.VMEM((4, CHUNKS, 128), F32),
            pltpu.VMEM((CHUNKS * 8, 128), F32),
            pltpu.VMEM((8, 128), F32),
            pltpu.VMEM((OWNERS, 8, 128), F32),
            pltpu.VMEM((OWNERS, 4, RAYS), F32),
            pltpu.VMEM((8, 128), F32),
            pltpu.VMEM((GROUPS, 4, CHUNKS, 128), F32),
            pltpu.VMEM((GROUPS, 4, CHUNKS, 128), F32),
            pltpu.VMEM((GROUPS, 8, 128), F32),
            pltpu.VMEM((6, ALL_CHUNKS, 128), F32),
            pltpu.VMEM((4, ALL_CHUNKS, 128), F32),
            pltpu.SemaphoreType.DMA((9,)),
            pltpu.SemaphoreType.DMA((8,)),
            pltpu.SemaphoreType.DMA((8,)),
            pltpu.SemaphoreType.DMA((2, 2, 4)),
            pltpu.SemaphoreType.DMA((2, 2, 4)),
            pltpu.SemaphoreType.DMA,
        ],
        compiler_params=pltpu.CompilerParams(
            collective_id=0, has_side_effects=True, vmem_limit_bytes=64 << 20
        ),
        name="render",
    )(*operands)


def gradient_kernel(
    tiles_hbm, table_hbm, colour_hbm, out_hbm, colour_ref,
    tiles_ref, table_smem, total_ref, out_ref, sems, out_sems,
):
    loads = [
        pltpu.make_async_copy(table_hbm, table_smem, sems.at[0]),
        pltpu.make_async_copy(tiles_hbm, tiles_ref.at[pl.ds(0, ALL_CHUNKS * 8)], sems.at[1]),
        pltpu.make_async_copy(colour_hbm, colour_ref, sems.at[2]),
    ]
    for load in loads:
        load.start()
    tiles_ref[pl.ds(ALL_CHUNKS * 8, 8), :] = jnp.zeros((8, 128), F32)
    total_ref[...] = jnp.zeros_like(total_ref)
    for load in loads:
        load.wait()

    lane_group = iota((8, 128), 1) // 16
    pick = lane_group * 16 + iota((8, 128), 0) + 1
    row8 = iota((8, 128), 0)
    first = jnp.where(row8 == 0, 1.0, jnp.where(row8 < 4, BASIS_0, 0.0))

    def one(chunk):
        tile = jnp.zeros((8, 128), F32)
        for p in range(8):
            start = pl.multiple_of(table_smem[p, chunk] * 8, 8)
            part = pltpu.roll(tiles_ref[pl.ds(start, 8), :], table_smem[8 + p, chunk], 1)
            tile = jnp.where(lane_group == p, part, tile)
        hat_x, hat_y, hat_z = hat(tile[4:5]), hat(tile[5:6]), hat(tile[6:7])
        plane = jnp.concatenate([hat_y[y : y + 1] * hat_z for y in range(8)], axis=0)
        basis = jnp.take_along_axis(jnp.broadcast_to(tile[7:8], (8, 128)), pick, axis=1)
        grad = jnp.concatenate([basis * tile[ch : ch + 1] for ch in (1, 2, 3)] + [tile * first], axis=0)
        left = jnp.concatenate(
            [
                jnp.concatenate([grad * hat_x[2 * x + k : 2 * x + k + 1] for x in range(4)], axis=0)
                for k in range(2)
            ],
            axis=1,
        )
        left_high, left_low = split(left)
        high, low = split(plane)
        none = jnp.zeros((64, 128), BF16)

        def both(value):
            return jnp.concatenate(
                [
                    jnp.concatenate([value, none], axis=1),
                    jnp.concatenate([none, value], axis=1),
                ],
                axis=0,
            )

        high, low = both(high), both(low)
        four = fast_dot(
            jnp.concatenate([left_high, left_low], axis=0),
            jnp.concatenate([high, low], axis=0),
            NT,
        )
        return four[0:128, 0:128] + four[0:128, 128:256] + four[128:256, 0:128]

    def several(turn, carry):
        parts = [one(turn * UNROLL + k) for k in range(UNROLL)]
        for k in range(UNROLL):
            b = table_smem[16, turn * UNROLL + k]
            rows = pl.ds(pl.multiple_of(b * BRICK_ROWS, 8), 128)
            total_ref[rows, :] += parts[k]
        return carry

    lax.fori_loop(0, (table_smem[17, 0] + UNROLL - 1) // UNROLL, several, 0)

    outs = []
    for c in range(COEF):
        for x in range(4):
            out_ref[c, :, x * 128 : x * 128 + 128] = total_ref[
                pl.ds(x * 32 + ROW_OF[c], BRICKS, stride=BRICK_ROWS), :
            ]
        outs.append(pltpu.make_async_copy(out_ref.at[c], out_hbm.at[c], out_sems.at[c]))
        outs[c].start()
    for out in outs:
        out.wait()


def gradient(tiles, table, colour):
    return pl.pallas_call(
        gradient_kernel,
        out_shape=(
            jax.ShapeDtypeStruct((COEF, BRICKS, VOXELS), F32),
            jax.ShapeDtypeStruct((3, RAYS), F32),
        ),
        in_specs=[ANY] * 3,
        out_specs=(ANY, VMEM),
        scratch_shapes=[
            pltpu.VMEM((ALL_CHUNKS * 8 + 8, 128), F32),
            pltpu.SMEM((24, TABLE), I32),
            pltpu.VMEM((BRICKS * BRICK_ROWS, 128), F32),
            pltpu.VMEM((COEF, BRICKS, VOXELS), F32),
            pltpu.SemaphoreType.DMA((3,)),
            pltpu.SemaphoreType.DMA((COEF,)),
        ],
        compiler_params=pltpu.CompilerParams(vmem_limit_bytes=64 << 20),
        name="gradient",
    )(tiles, table, colour)


def local(
    bricks, requests, seg_owner, seg_slot, sample_cells, sample_fracs,
    ray_angles, ray_step, pixel_target,
):
    colour, tiles, table = render(
        seg_owner.reshape(1, RAYS),
        seg_slot.reshape(1, RAYS),
        jnp.transpose(requests.reshape(OWNERS, 2)),
        sample_cells.reshape(SAMP, RAYS),
        sample_fracs.reshape(3 * SAMP, RAYS),
        ray_angles,
        ray_step.reshape(1, RAYS),
        pixel_target,
        bricks,
    )
    return gradient(tiles, table, colour)


def solution(mesh):
    return jax.shard_map(
        local,
        mesh=mesh,
        in_specs=(
            P(None, "seg", None),
            P("seg", "grp", None, None),
            P("seg", "grp", None),
            P("seg", "grp"),
            P(None, "seg", "grp"),
            P(None, None, "seg", "grp"),
            P(None, "grp"),
            P("grp"),
            P(None, "grp"),
        ),
        out_specs=(P(None, "seg", None), P(None, "grp")),
        check_vma=False,
    )
```

```python
import functools

import jax
import jax.numpy as jnp
from jax import lax
from jax.experimental import pallas as pl
from jax.experimental.pallas import tpu as pltpu
from jax.sharding import PartitionSpec as P

COEF = 28
VOXELS = 512
SAMP = 16
OWNERS = 64
CHIPS = OWNERS // 2
GROUPS = 8
SLOTS = 4
BRICKS = 48
RAYS = 128
CHUNKS = OWNERS * SLOTS // 8
ALL_CHUNKS = GROUPS * CHUNKS
TABLE = 384
UNROLL = 32
BRICK_ROWS = 136
FUNROLL = 8
LOSS_SCALE = 1024.0
BASIS_0 = 0.28209479
ROW_OF = [24] + [
    25 + ch if k == 0 else ch * 8 + k - 1 for ch in range(3) for k in range(9)
]
F32 = jnp.float32
BF16 = jnp.bfloat16
I32 = jnp.int32
VMEM = pl.BlockSpec(memory_space=pltpu.VMEM)
ANY = pl.BlockSpec(memory_space=pl.ANY)
MESH = pl.DeviceIdType.MESH
NN = (((1,), (0,)), ((), ()))
NT = (((1,), (1,)), ((), ()))


def iota(shape, dim):
    return lax.broadcasted_iota(I32, shape, dim)


def exact_dot(a, b, dims=NN):
    return lax.dot_general(
        a, b, dims, precision=lax.Precision.HIGHEST, preferred_element_type=F32
    )


def fast_dot(a, b, dims=NN):
    return lax.dot_general(a, b, dims, preferred_element_type=F32)


def split(value):
    high = value.astype(BF16)
    return high, (value - high.astype(F32)).astype(BF16)


def hat(place):
    return jnp.maximum(1.0 - jnp.abs(place - iota((8, 128), 0).astype(F32)), 0.0)


def softplus(value):
    return jnp.maximum(value, 0.0) + jnp.log1p(jnp.exp(-jnp.abs(value)))


def sigmoid(value):
    return 1.0 / (1.0 + jnp.exp(-value))


def ray_basis(angles):
    polar = angles[0:1]
    azimuth = angles[1:2]
    x = jnp.sin(polar) * jnp.cos(azimuth)
    y = jnp.sin(polar) * jnp.sin(azimuth)
    z = jnp.cos(polar)
    return [
        BASIS_0 * jnp.ones_like(x),
        -0.48860251 * y,
        0.48860251 * z,
        -0.48860251 * x,
        1.09254843 * x * y,
        -1.09254843 * y * z,
        0.31539157 * (2.0 * z * z - x * x - y * y),
        -1.09254843 * x * z,
        0.54627422 * (x * x - y * y),
    ]


def pack(owner, slot, wanted, cells, fracs, basis, step):
    mine = owner == iota((OWNERS, RAYS), 0)
    across = jnp.broadcast_to(owner, (RAYS, RAYS))
    ahead = iota((RAYS, RAYS), 0) < iota((RAYS, RAYS), 1)
    rank = jnp.sum(
        jnp.where((jnp.transpose(across) == across) & ahead, 1, 0), axis=0, keepdims=True
    )
    columns = jnp.transpose(wanted)
    brick = jnp.sum(
        jnp.where(mine, jnp.where(slot == 0, columns[:, 0:1], columns[:, 1:2]), 0),
        axis=0, keepdims=True,
    )
    chosen = [mine & (rank == j) for j in range(SLOTS)]
    choice = jnp.concatenate([jnp.where(one, 1.0, 0.0) for one in chosen], axis=1)
    lane = iota((OWNERS, RAYS), 1) - lax.rem(lax.axis_index("seg"), 32) * SLOTS
    spots = owner * SLOTS + rank
    bricks = jnp.zeros((OWNERS, RAYS), I32)
    for j in range(SLOTS):
        named = jnp.sum(jnp.where(chosen[j], brick, 0), axis=1, keepdims=True)
        bricks = jnp.where(lane == j, named, bricks)
    cell_x = (cells * 1338) >> 16
    rest = cells - cell_x * 49
    cell_y = (rest * 9363) >> 16
    cell_z = rest - cell_y * 7
    place_x = cell_x.astype(F32) + fracs[0:16]
    place_y = cell_y.astype(F32) + fracs[16:32]
    place_z = cell_z.astype(F32) + fracs[32:48]
    row = iota((SAMP, RAYS), 0)
    extra = jnp.where(row == 11, 1.0, 0.0)
    for k, value in enumerate(basis + [step, brick.astype(F32) + 1.0]):
        extra = jnp.where(row == k, value, extra)
    none = jnp.zeros((SAMP, RAYS), F32)

    def placed(first, second):
        parts = []
        for j in range(SLOTS):
            rows = [none] * 8
            rows[j] = first
            rows[4 + j] = second
            parts.append(jnp.concatenate(rows, axis=0))
        return jnp.concatenate(parts, axis=1)

    return (
        bricks * 256 + spots,
        exact_dot(choice, placed(place_x, place_y), NT),
        exact_dot(choice, placed(place_z, extra), NT),
    )


def greet(axes):
    barrier = pltpu.get_barrier_semaphore()
    total = 0
    for axis, count in axes:
        me = lax.axis_index(axis)

        def hail(turn, carry, axis=axis, count=count, me=me):
            pl.semaphore_signal(
                barrier,
                inc=1,
                device_id={axis: lax.rem(me + turn, count)},
                device_id_type=MESH,
            )
            return carry

        lax.fori_loop(1, count, hail, 0, unroll=9 if count == OWNERS else 7)
        total += count - 1
    return lambda: pl.semaphore_wait(barrier, total)


def send_all(axis, count, source, target, send_sem, recv_sem):
    me = lax.axis_index(axis)

    def one(turn, carry):
        peer = lax.rem(me + turn, count)
        pltpu.make_async_remote_copy(
            src_ref=source(peer),
            dst_ref=target.at[me],
            send_sem=send_sem,
            recv_sem=recv_sem,
            device_id={axis: peer},
            device_id_type=MESH,
        ).start()
        return carry

    lax.fori_loop(1, count, one, 0, unroll=9 if count == OWNERS else 7)


def ring_start(ref, step, send_sems, recv_sems):
    me = lax.axis_index("grp")
    for way in range(2 if step < 4 else 1):
        block = lax.rem(me + GROUPS + (step - 1) * (2 * way - 1), GROUPS)
        pltpu.make_async_remote_copy(
            src_ref=ref.at[block],
            dst_ref=ref.at[block],
            send_sem=send_sems.at[way, step - 1],
            recv_sem=recv_sems.at[way, step - 1],
            device_id={"grp": lax.rem(me + GROUPS + 1 - 2 * way, GROUPS)},
            device_id_type=MESH,
        ).start()


def ring_wait(ref, step, sems, arriving):
    me = lax.axis_index("grp")
    for way in range(2 if step < 4 else 1):
        away = step if arriving else step - 1
        part = ref.at[lax.rem(me + GROUPS + away * (2 * way - 1), GROUPS)]
        pltpu.make_async_copy(part, part, sems.at[way, step - 1]).wait()


def wait_all(target, count, sem):
    part = target.at[pl.ds(0, count - 1)]
    pltpu.make_async_copy(part, part, sem).wait()


def lay_out_bricks(bricks_ref, wide_ref, brick_ref):
    for c in range(COEF, 32):
        for x in range(4):
            wide_ref[x, pl.ds(c, BRICKS, stride=40), :] = jnp.zeros((BRICKS, 128), F32)
    for c in range(COEF):
        for x in range(4):
            wide_ref[x, pl.ds(ROW_OF[c], BRICKS, stride=40), :] = bricks_ref[
                c, :, x * 128 : x * 128 + 128
            ].astype(F32)

    def narrow(turn, carry):
        for k in range(8):
            rows = pl.ds(pl.multiple_of(turn * 320 + k * 40, 8), 32)
            for x in range(4):
                brick_ref[turn * 8 + k, :, x * 128 : x * 128 + 128] = wide_ref[
                    x, rows, :
                ].astype(BF16)
        return carry

    lax.fori_loop(0, BRICKS // 8, narrow, 0)


def unpack(got_ref, half_ref, place_ref, basis_ref):
    left = iota((CHUNKS, 128), 1) < 64
    for half in range(2):
        half_ref[...] = got_ref[:, half, :]
        even = half_ref[pl.ds(0, CHUNKS, stride=2), :]
        odd = half_ref[pl.ds(1, CHUNKS, stride=2), :]
        place_ref[2 * half] = jnp.where(left, even, pltpu.roll(odd, 64, 1))
        place_ref[2 * half + 1] = jnp.where(left, pltpu.roll(even, 64, 1), odd)
    row, lane = iota((128, 1024), 0), iota((128, 1024), 1)
    spread = jnp.where(row == ((lane % 128) // 16) * 16 + lane // 128 + 1, 1.0, 0.0)
    basis = exact_dot(place_ref[3], spread)
    for k in range(8):
        basis_ref[pl.ds(k, CHUNKS, stride=8), :] = basis[:, k * 128 : k * 128 + 128]


def interpolate(brick_ref, place_ref, basis_ref, id_smem, raw_ref, half):
    lane_group = iota((32, 128), 1) // 16

    def one(chunk):
        hat_x = hat(place_ref[0, pl.ds(chunk, 1), :])
        hat_y = hat(place_ref[1, pl.ds(chunk, 1), :])
        hat_z = hat(place_ref[2, pl.ds(chunk, 1), :])
        plane = jnp.concatenate([hat_y[y : y + 1] * hat_z for y in range(8)], axis=0)
        weights = jnp.concatenate([hat_x[x : x + 1] * plane for x in range(8)], axis=0)
        high, low = split(weights)
        rows = []
        for seg in range(8):
            b = id_smem[chunk // 16, lax.rem(chunk, 16) * 8 + seg]
            rows.append(brick_ref[b])
        values = fast_dot(
            jnp.concatenate(rows, axis=0), jnp.concatenate([high, low], axis=1)
        )
        coef = jnp.zeros((32, 128), F32)
        for seg in range(8):
            part = values[seg * 32 : seg * 32 + 32]
            coef = jnp.where(lane_group == seg, part[:, 0:128] + part[:, 128:256], coef)
        basis = basis_ref[pl.ds(pl.multiple_of(chunk * 8, 8), 8), :]
        raw_ref[0, pl.ds(chunk, 1), :] = coef[24:25]
        for ch in range(3):
            raw_ref[1 + ch, pl.ds(chunk, 1), :] = coef[25 + ch : 26 + ch] * BASIS_0 + jnp.sum(
                coef[8 * ch : 8 * ch + 8] * basis, axis=0, keepdims=True
            )

    def several(turn, carry):
        for k in range(FUNROLL):
            one(turn * FUNROLL + k)
        return carry

    turns = CHUNKS // FUNROLL // 2
    lax.fori_loop(half * turns, (half + 1) * turns, several, 0)


def segment_sums(raw_ref, extra):
    optical, through, opaque, _ = march(raw_ref[0], extra)
    light = through * opaque
    total = jnp.zeros((CHUNKS, 128), F32)
    row, lane = iota((128, 128), 0), iota((128, 128), 1)
    for v in range(4):
        part = optical if v == 3 else light * sigmoid(raw_ref[1 + v])
        total += exact_dot(part, jnp.where(lane == (row // 16) * 4 + v, 1.0, 0.0))
    return sum(pltpu.roll(total[8 * k : 8 * k + 8], 32 * k, 1) if k else total[0:8] for k in range(4))


def march(density, extra):
    row, lane = iota((128, 128), 0), iota((128, 128), 1)
    same = row // 16 == lane // 16
    step = exact_dot(extra, jnp.where(same & (row % 16 == 9), 1.0, 0.0))
    optical = softplus(density) * step
    before = exact_dot(optical, jnp.where(same & (row < lane), 1.0, 0.0))
    through = jnp.exp(-before)
    remains = jnp.exp(-optical)
    return optical, through, 1.0 - remains, (step, remains)


def plan_chunks(extra):
    across = jnp.transpose(extra)
    named = iota((64, ALL_CHUNKS), 0).astype(F32) + 1.0
    hits = [
        jnp.where(across[seg * 16 + 10 : seg * 16 + 11] == named, 1.0, 0.0) for seg in range(8)
    ]
    earlier = jnp.where(
        iota((ALL_CHUNKS, ALL_CHUNKS), 0) < iota((ALL_CHUNKS, ALL_CHUNKS), 1), 1.0, 0.0
    ).astype(BF16)
    counts = fast_dot(jnp.concatenate(hits, axis=0).astype(BF16), earlier)
    carry = jnp.zeros((64, 1), F32)
    ranks = []
    for seg in range(8):
        ranks.append(counts[seg * 64 : seg * 64 + 64] + carry)
        carry = carry + jnp.sum(hits[seg], axis=1, keepdims=True)
    full = jnp.floor((carry + 7.0) * 0.125)
    lower = jnp.where(iota((64, 64), 1) < iota((64, 64), 0), 1.0, 0.0).astype(BF16)
    full_wide = jnp.broadcast_to(full, (64, 128))
    start = fast_dot(lower, full_wide.astype(BF16))
    end = start + full_wide
    start256 = jnp.concatenate([start, start], axis=1)
    selectors, values = [], []
    row = iota((32, ALL_CHUNKS), 0)
    lane = iota((32, ALL_CHUNKS), 1).astype(F32)
    for seg in range(8):
        place = (
            jnp.sum(hits[seg] * (8.0 * start256 + ranks[seg] + 1.0), axis=0, keepdims=True) - 1.0
        )
        chunk = jnp.floor(place * 0.125)
        inside = place - 8.0 * chunk
        selectors.append(
            jnp.where(iota((TABLE, ALL_CHUNKS), 0).astype(F32) == chunk, 1.0, 0.0).astype(BF16)
        )
        kind = jnp.where(
            row < 8, lane, jnp.where(row < 16, float(seg), jnp.where(row < 24, 1.0, 0.0))
        )
        values.append(jnp.where((row % 8).astype(F32) == inside, kind, 0.0).astype(BF16))
    table = fast_dot(
        jnp.concatenate(values, axis=1), jnp.concatenate(selectors, axis=1), NT
    )
    tile = table[0:8] + (1.0 - table[16:24]) * float(ALL_CHUNKS)
    turn = 16.0 * (iota((8, TABLE), 0).astype(F32) - table[8:16])
    turn = jnp.where(turn < 0.0, turn + 128.0, turn)
    place = iota((64, 128), 1).astype(F32)
    real = iota((64, 128), 0) < BRICKS
    owner = [
        jnp.sum(jnp.where((end <= place + 128.0 * k) & real, 1.0, 0.0), axis=0, keepdims=True)
        for k in range(TABLE // 128)
    ]
    owner = jnp.minimum(jnp.concatenate(owner, axis=1), float(BRICKS - 1))
    number = jnp.sum(full_wide, axis=0, keepdims=True)
    number = jnp.concatenate([number] * (TABLE // 128), axis=1)
    last = jnp.where(iota((8, TABLE), 0) == 0, owner, number)
    return jnp.concatenate([tile, turn, last], axis=0).astype(I32)


def shade_all(raws_ref, extra):
    raw = [
        jnp.concatenate([raws_ref[g, v] for g in range(GROUPS)], axis=0) for v in range(4)
    ]
    _, through, opaque, (step, remains) = march(raw[0], extra)
    light = through * opaque
    radiance = [sigmoid(value) for value in raw[1:]]
    return radiance + [light, through * remains, step * sigmoid(raw[0])]


def sample_gradients(grads_ref, shades_ref, slot_ref, tiles_ref):
    row, lane = iota((128, 128), 0), iota((128, 128), 1)
    grads = jnp.concatenate([grads_ref[g] for g in range(GROUPS)], axis=0)
    for part in range(4):
        for v in range(4):
            spread = jnp.where(row == part * 32 + (lane // 16) * 4 + v, 1.0, 0.0)
            wide = exact_dot(grads, spread)
            for g in range(GROUPS):
                slot_ref[v, pl.ds(g * CHUNKS + part * 8, 8), :] = wide[g * 8 : g * 8 + 8]
    light = shades_ref[3]
    mixed = jnp.zeros((ALL_CHUNKS, 128), F32)
    for v in range(3):
        radiance = shades_ref[v]
        grad_colour = slot_ref[v]
        mixed += grad_colour * radiance
        tiles_ref[pl.ds(1 + v, ALL_CHUNKS, stride=8), :] = (
            grad_colour * light * radiance * (1.0 - radiance)
        )
    later = jnp.where((row // 16 == lane // 16) & (row > lane), 1.0, 0.0)
    grad_optical = shades_ref[4] * mixed - exact_dot(light * mixed, later) + slot_ref[3]
    tiles_ref[pl.ds(0, ALL_CHUNKS, stride=8), :] = grad_optical * shades_ref[5]


def to_rays(sums_ref, spots_ref, rays_ref):
    spot = iota((OWNERS, RAYS), 0)
    owner = lax.rem(spot, CHIPS) * 2 + spot // CHIPS
    slot = iota((16, RAYS), 0) // 4
    for row in range(8):
        across = jnp.transpose(sums_ref[:, :, row, :].reshape(OWNERS, 128))
        high, rest = split(across)
        middle, low = split(across - high.astype(F32))
        for part in range(4):
            for half in range(2):
                s = 2 * (part * 8 + row) + half
                rows = slice(part * 32 + half * 16, part * 32 + half * 16 + 16)
                spots = spots_ref[s]
                hits = jnp.where(spots // SLOTS == owner, 1.0, 0.0).astype(BF16)
                three = fast_dot(
                    jnp.concatenate([high[rows], middle[rows], low[rows]], axis=0), hits
                )
                found = three[0:16] + three[16:32] + three[32:48]
                found = jnp.where(spots % SLOTS == slot, found, 0.0)
                found = found[0:8] + found[8:16]
                rays_ref[s] = found[0:4] + found[4:8]


def composite(colours, taus, target):
    depth, other = iota((OWNERS, OWNERS), 0), iota((OWNERS, OWNERS), 1)
    through = jnp.exp(-exact_dot(jnp.where(other < depth, 1.0, 0.0), taus))
    behind = jnp.where(other > depth, 1.0, 0.0)
    colour, grads = [], []
    grad_tau = jnp.zeros((OWNERS, RAYS), F32)
    for v in range(3):
        contrib = through * colours[v]
        colour.append(jnp.sum(contrib, axis=0, keepdims=True))
        misfit = LOSS_SCALE * (colour[v] - target[v : v + 1])
        grads.append(through * misfit)
        grad_tau -= misfit * exact_dot(behind, contrib)
    return colour, grads + [grad_tau]


def to_slots(grads, spots):
    me = lax.axis_index("seg")
    depth = iota((OWNERS, 128), 0)
    place = iota((OWNERS, 128), 1) - (depth // 16) * 32 - (depth % 2) * 16
    placed = jnp.zeros((OWNERS, 128), F32)
    for j in range(SLOTS):
        here = spots == me * SLOTS + j
        for v in range(4):
            value = jnp.sum(jnp.where(here, grads[v], 0.0), axis=1, keepdims=True)
            placed = jnp.where(place == j * 4 + v, value, placed)
    pick = jnp.where((iota((8, OWNERS), 1) // 2) % 8 == iota((8, OWNERS), 0), 1.0, 0.0)
    return exact_dot(pick, placed)


def render_kernel(
    owner_hbm, slot_hbm, wanted_hbm, cells_hbm, fracs_hbm, angles_hbm, step_hbm, target_hbm,
    bricks_hbm,
    colour_ref, tiles_ref, table_ref,
    owner_ref, slot_ref, wanted_ref, cells_ref, fracs_ref, angles_ref, step_ref, target_ref,
    bricks_ref,
    out_ref, got_ref, wide_ref, brick_ref, half_ref, numbers_ref, ids_ref, spots_ref, id_vmem, id_smem,
    place_ref, raw_ref, basis_ref,
    sums_ref, all_sums_ref, rays_ref, grads_ref,
    places_ref, raws_ref, all_grads_ref, shades_ref, slot_grads_ref,
    load_sems, send_sems, recv_sems, ring_sends, ring_recvs, own_sem,
):
    loads = [
        pltpu.make_async_copy(source, target, load_sems.at[k])
        for k, (source, target) in enumerate(
            [
                (owner_hbm, owner_ref), (slot_hbm, slot_ref), (wanted_hbm, wanted_ref),
                (cells_hbm, cells_ref), (fracs_hbm, fracs_ref), (angles_hbm, angles_ref),
                (step_hbm, step_ref), (target_hbm, target_ref), (bricks_hbm, bricks_ref),
            ]
        )
    ]
    for load in loads:
        load.start()
    met = greet([("seg", OWNERS), ("grp", GROUPS)])
    for load in loads[:8]:
        load.wait()
    me = lax.axis_index("seg")
    group = lax.axis_index("grp")

    def pass_places(step):
        ring_start(places_ref, step, ring_sends.at[0], ring_recvs.at[0])

    def take_places(step):
        ring_wait(places_ref, step, ring_recvs.at[0], True)

    def pass_raws(step):
        ring_start(raws_ref, step, ring_sends.at[1], ring_recvs.at[1])

    def take_raws(step):
        ring_wait(raws_ref, step, ring_recvs.at[1], True)

    numbers, first, second = pack(
        owner_ref[...], slot_ref[...], wanted_ref[...], cells_ref[...], fracs_ref[...],
        ray_basis(angles_ref[...]), step_ref[...],
    )
    out_ref[:, 0, :] = first
    out_ref[:, 1, :] = second
    numbers_ref[:, 0, :] = numbers
    met()
    send_all(
        "seg", OWNERS, lambda peer: numbers_ref.at[peer], ids_ref, send_sems.at[7], recv_sems.at[7]
    )
    ids_ref[me] = numbers_ref[me]
    send_all(
        "seg", OWNERS, lambda peer: out_ref.at[peer], got_ref, send_sems.at[0], recv_sems.at[0]
    )
    got_ref[me] = out_ref[me]
    loads[8].wait()
    lay_out_bricks(bricks_ref, wide_ref, brick_ref)
    wait_all(got_ref, OWNERS, recv_sems.at[0])

    unpack(got_ref, half_ref, place_ref, basis_ref)
    extra = place_ref[3]
    places_ref[group] = place_ref[...]
    pass_places(1)
    wait_all(ids_ref, OWNERS, recv_sems.at[7])
    for half in range(2):
        id_vmem[half : half + 1, :] = jnp.sum(
            ids_ref[32 * half : 32 * half + 32, 0, :] // 256, axis=0, keepdims=True
        )
    ids = pltpu.make_async_copy(id_vmem, id_smem, own_sem)
    ids.start()
    spots_ref[:, 0, :] = lax.rem(ids_ref[:, 0, :], 256)
    ids.wait()
    interpolate(brick_ref, place_ref, basis_ref, id_smem, raw_ref, 0)
    take_places(1)
    pass_places(2)
    interpolate(brick_ref, place_ref, basis_ref, id_smem, raw_ref, 1)
    take_places(2)
    pass_places(3)
    raws_ref[group] = raw_ref[...]
    pass_raws(1)
    sums_ref[...] = segment_sums(raw_ref, extra)

    chip, core = me // 2, lax.rem(me, 2)

    def to_chip(turn, carry):
        pltpu.make_async_remote_copy(
            src_ref=sums_ref,
            dst_ref=all_sums_ref.at[core, chip],
            send_sem=send_sems.at[2],
            recv_sem=recv_sems.at[2],
            device_id={"seg": lax.rem(chip + turn, CHIPS) * 2 + core},
            device_id_type=MESH,
        ).start()
        return carry

    lax.fori_loop(1, CHIPS, to_chip, 0, unroll=31)
    all_sums_ref[core, chip] = sums_ref[...]
    take_places(3)
    pass_places(4)
    take_raws(1)
    pass_raws(2)
    wait_all(all_sums_ref.at[core], CHIPS, recv_sems.at[2])
    across = pltpu.make_async_remote_copy(
        src_ref=all_sums_ref.at[core],
        dst_ref=all_sums_ref.at[core],
        send_sem=send_sems.at[4],
        recv_sem=recv_sems.at[4],
        device_id={"seg": me + 1 - 2 * core},
        device_id_type=MESH,
    )
    across.start()
    take_raws(2)
    pass_raws(3)
    take_places(4)
    all_extra = jnp.concatenate([places_ref[g, 3] for g in range(GROUPS)], axis=0)
    table_ref[...] = plan_chunks(all_extra)
    other = all_sums_ref.at[1 - core]
    pltpu.make_async_copy(other, other, recv_sems.at[4]).wait()
    to_rays(all_sums_ref, spots_ref, rays_ref)
    take_raws(3)
    pass_raws(4)
    colour, grads = composite(
        [rays_ref[:, v, :] for v in range(3)], rays_ref[:, 3, :], target_ref[...]
    )
    for v in range(3):
        colour_ref[v : v + 1, :] = colour[v]
    grads_ref[...] = to_slots(grads, spots_ref[:, 0, :])

    send_all(
        "grp", GROUPS, lambda peer: grads_ref, all_grads_ref, send_sems.at[6], recv_sems.at[6]
    )
    all_grads_ref[group] = grads_ref[...]
    for g in range(GROUPS):
        for q in range(4):
            tiles_ref[pl.ds(g * CHUNKS * 8 + 4 + q, CHUNKS, stride=8), :] = places_ref[g, q]
    take_raws(4)
    for k, value in enumerate(shade_all(raws_ref, all_extra)):
        shades_ref[k] = value
    wait_all(all_grads_ref, GROUPS, recv_sems.at[6])
    sample_gradients(all_grads_ref, shades_ref, slot_grads_ref, tiles_ref)
    wait_all(got_ref, OWNERS, send_sems.at[0])
    wait_all(ids_ref, OWNERS, send_sems.at[7])
    wait_all(all_sums_ref.at[core], CHIPS, send_sems.at[2])
    across.wait_send()
    for step in range(1, 5):
        ring_wait(places_ref, step, ring_sends.at[0], False)
        ring_wait(raws_ref, step, ring_sends.at[1], False)
    wait_all(all_grads_ref, GROUPS, send_sems.at[6])


def render(*operands):
    return pl.pallas_call(
        render_kernel,
        out_shape=(
            jax.ShapeDtypeStruct((3, RAYS), F32),
            jax.ShapeDtypeStruct((ALL_CHUNKS * 8, 128), F32),
            jax.ShapeDtypeStruct((24, TABLE), I32),
        ),
        in_specs=[ANY] * 9,
        out_specs=(VMEM, VMEM, VMEM),
        scratch_shapes=[pltpu.VMEM(x.shape, x.dtype) for x in operands]
        + [
            pltpu.VMEM((OWNERS, 2, 128), F32),
            pltpu.VMEM((OWNERS, 2, 128), F32),
            pltpu.VMEM((4, BRICKS * 40, 128), F32),
            pltpu.VMEM((BRICKS, 32, VOXELS), BF16),
            pltpu.VMEM((OWNERS, 128), F32),
            pltpu.VMEM((OWNERS, 1, 128), I32),
            pltpu.VMEM((OWNERS, 1, 128), I32),
            pltpu.VMEM((OWNERS, 1, 128), I32),
            pltpu.VMEM((2, 128), I32),
            pltpu.SMEM((2, 128), I32),
            pltpu.VMEM((4, CHUNKS, 128), F32),
            pltpu.VMEM((4, CHUNKS, 128), F32),
            pltpu.VMEM((CHUNKS * 8, 128), F32),
            pltpu.VMEM((8, 128), F32),
            pltpu.VMEM((2, CHIPS, 8, 128), F32),
            pltpu.VMEM((OWNERS, 4, RAYS), F32),
            pltpu.VMEM((8, 128), F32),
            pltpu.VMEM((GROUPS, 4, CHUNKS, 128), F32),
            pltpu.VMEM((GROUPS, 4, CHUNKS, 128), F32),
            pltpu.VMEM((GROUPS, 8, 128), F32),
            pltpu.VMEM((6, ALL_CHUNKS, 128), F32),
            pltpu.VMEM((4, ALL_CHUNKS, 128), F32),
            pltpu.SemaphoreType.DMA((9,)),
            pltpu.SemaphoreType.DMA((8,)),
            pltpu.SemaphoreType.DMA((8,)),
            pltpu.SemaphoreType.DMA((2, 2, 4)),
            pltpu.SemaphoreType.DMA((2, 2, 4)),
            pltpu.SemaphoreType.DMA,
        ],
        compiler_params=pltpu.CompilerParams(
            collective_id=0, has_side_effects=True, vmem_limit_bytes=64 << 20
        ),
        name="render",
    )(*operands)


def gradient_kernel(
    tiles_hbm, table_hbm, colour_hbm, out_hbm, colour_ref,
    tiles_ref, table_smem, total_ref, out_ref, sems, out_sems,
):
    loads = [
        pltpu.make_async_copy(table_hbm, table_smem, sems.at[0]),
        pltpu.make_async_copy(tiles_hbm, tiles_ref.at[pl.ds(0, ALL_CHUNKS * 8)], sems.at[1]),
        pltpu.make_async_copy(colour_hbm, colour_ref, sems.at[2]),
    ]
    for load in loads:
        load.start()
    tiles_ref[pl.ds(ALL_CHUNKS * 8, 8), :] = jnp.zeros((8, 128), F32)
    total_ref[...] = jnp.zeros_like(total_ref)
    for load in loads:
        load.wait()

    lane_group = iota((8, 128), 1) // 16
    pick = lane_group * 16 + iota((8, 128), 0) + 1
    row8 = iota((8, 128), 0)
    first = jnp.where(row8 == 0, 1.0, jnp.where(row8 < 4, BASIS_0, 0.0))

    def one(chunk):
        tile = jnp.zeros((8, 128), F32)
        for p in range(8):
            start = pl.multiple_of(table_smem[p, chunk] * 8, 8)
            part = pltpu.roll(tiles_ref[pl.ds(start, 8), :], table_smem[8 + p, chunk], 1)
            tile = jnp.where(lane_group == p, part, tile)
        hat_x, hat_y, hat_z = hat(tile[4:5]), hat(tile[5:6]), hat(tile[6:7])
        plane = jnp.concatenate([hat_y[y : y + 1] * hat_z for y in range(8)], axis=0)
        basis = jnp.take_along_axis(jnp.broadcast_to(tile[7:8], (8, 128)), pick, axis=1)
        grad = jnp.concatenate([basis * tile[ch : ch + 1] for ch in (1, 2, 3)] + [tile * first], axis=0)
        left = jnp.concatenate(
            [
                jnp.concatenate([grad * hat_x[2 * x + k : 2 * x + k + 1] for x in range(4)], axis=0)
                for k in range(2)
            ],
            axis=1,
        )
        left_high, left_low = split(left)
        high, low = split(plane)
        none = jnp.zeros((64, 128), BF16)

        def both(value):
            return jnp.concatenate(
                [
                    jnp.concatenate([value, none], axis=1),
                    jnp.concatenate([none, value], axis=1),
                ],
                axis=0,
            )

        high, low = both(high), both(low)
        four = fast_dot(
            jnp.concatenate([left_high, left_low], axis=0),
            jnp.concatenate([high, low], axis=0),
            NT,
        )
        return four[0:128, 0:128] + four[0:128, 128:256] + four[128:256, 0:128]

    def several(turn, carry):
        parts = [one(turn * UNROLL + k) for k in range(UNROLL)]
        for k in range(UNROLL):
            b = table_smem[16, turn * UNROLL + k]
            rows = pl.ds(pl.multiple_of(b * BRICK_ROWS, 8), 128)
            total_ref[rows, :] += parts[k]
        return carry

    lax.fori_loop(0, (table_smem[17, 0] + UNROLL - 1) // UNROLL, several, 0)

    outs = []
    for c in range(COEF):
        for x in range(4):
            out_ref[c, :, x * 128 : x * 128 + 128] = total_ref[
                pl.ds(x * 32 + ROW_OF[c], BRICKS, stride=BRICK_ROWS), :
            ]
        outs.append(pltpu.make_async_copy(out_ref.at[c], out_hbm.at[c], out_sems.at[c]))
        outs[c].start()
    for out in outs:
        out.wait()


def gradient(tiles, table, colour):
    return pl.pallas_call(
        gradient_kernel,
        out_shape=(
            jax.ShapeDtypeStruct((COEF, BRICKS, VOXELS), F32),
            jax.ShapeDtypeStruct((3, RAYS), F32),
        ),
        in_specs=[ANY] * 3,
        out_specs=(ANY, VMEM),
        scratch_shapes=[
            pltpu.VMEM((ALL_CHUNKS * 8 + 8, 128), F32),
            pltpu.SMEM((24, TABLE), I32),
            pltpu.VMEM((BRICKS * BRICK_ROWS, 128), F32),
            pltpu.VMEM((COEF, BRICKS, VOXELS), F32),
            pltpu.SemaphoreType.DMA((3,)),
            pltpu.SemaphoreType.DMA((COEF,)),
        ],
        compiler_params=pltpu.CompilerParams(vmem_limit_bytes=64 << 20),
        name="gradient",
    )(tiles, table, colour)


def local(
    bricks, requests, seg_owner, seg_slot, sample_cells, sample_fracs,
    ray_angles, ray_step, pixel_target,
):
    colour, tiles, table = render(
        seg_owner.reshape(1, RAYS),
        seg_slot.reshape(1, RAYS),
        jnp.transpose(requests.reshape(OWNERS, 2)),
        sample_cells.reshape(SAMP, RAYS),
        sample_fracs.reshape(3 * SAMP, RAYS),
        ray_angles,
        ray_step.reshape(1, RAYS),
        pixel_target,
        bricks,
    )
    return gradient(tiles, table, colour)


def solution(mesh):
    return jax.shard_map(
        local,
        mesh=mesh,
        in_specs=(
            P(None, "seg", None),
            P("seg", "grp", None, None),
            P("seg", "grp", None),
            P("seg", "grp"),
            P(None, "seg", "grp"),
            P(None, None, "seg", "grp"),
            P(None, "grp"),
            P("grp"),
            P(None, "grp"),
        ),
        out_specs=(P(None, "seg", None), P(None, "grp")),
        check_vma=False,
    )
```

```python
import functools

import jax
import jax.numpy as jnp
from jax import lax
from jax.experimental import pallas as pl
from jax.experimental.pallas import tpu as pltpu
from jax.sharding import PartitionSpec as P

COEF = 28
VOXELS = 512
SAMP = 16
OWNERS = 64
GROUPS = 8
SLOTS = 4
BRICKS = 48
RAYS = 128
CHUNKS = OWNERS * SLOTS // 8
ALL_CHUNKS = GROUPS * CHUNKS
TABLE = 384
UNROLL = 48
BRICK_ROWS = 136
FUNROLL = 16
LOSS_SCALE = 1024.0
BASIS_0 = 0.28209479
ROW_OF = [24] + [
    25 + ch if k == 0 else ch * 8 + k - 1 for ch in range(3) for k in range(9)
]
F32 = jnp.float32
BF16 = jnp.bfloat16
I32 = jnp.int32
VMEM = pl.BlockSpec(memory_space=pltpu.VMEM)
ANY = pl.BlockSpec(memory_space=pl.ANY)
MESH = pl.DeviceIdType.MESH
NN = (((1,), (0,)), ((), ()))
NT = (((1,), (1,)), ((), ()))


def iota(shape, dim):
    return lax.broadcasted_iota(I32, shape, dim)


def exact_dot(a, b, dims=NN):
    return lax.dot_general(
        a, b, dims, precision=lax.Precision.HIGHEST, preferred_element_type=F32
    )


def fast_dot(a, b, dims=NN):
    return lax.dot_general(a, b, dims, preferred_element_type=F32)


def split(value):
    high = value.astype(BF16)
    return high, (value - high.astype(F32)).astype(BF16)


def hat(place):
    return jnp.maximum(1.0 - jnp.abs(place - iota((8, 128), 0).astype(F32)), 0.0)


def softplus(value):
    return jnp.maximum(value, 0.0) + jnp.log1p(jnp.exp(-jnp.abs(value)))


def sigmoid(value):
    return 1.0 / (1.0 + jnp.exp(-value))


def ray_basis(angles):
    polar = angles[0:1]
    azimuth = angles[1:2]
    x = jnp.sin(polar) * jnp.cos(azimuth)
    y = jnp.sin(polar) * jnp.sin(azimuth)
    z = jnp.cos(polar)
    return [
        BASIS_0 * jnp.ones_like(x),
        -0.48860251 * y,
        0.48860251 * z,
        -0.48860251 * x,
        1.09254843 * x * y,
        -1.09254843 * y * z,
        0.31539157 * (2.0 * z * z - x * x - y * y),
        -1.09254843 * x * z,
        0.54627422 * (x * x - y * y),
    ]


def pack(owner, slot, wanted, cells, fracs, basis, step):
    mine = owner == iota((OWNERS, RAYS), 0)
    across = jnp.broadcast_to(owner, (RAYS, RAYS))
    ahead = iota((RAYS, RAYS), 0) < iota((RAYS, RAYS), 1)
    rank = jnp.sum(
        jnp.where((jnp.transpose(across) == across) & ahead, 1, 0), axis=0, keepdims=True
    )
    columns = jnp.transpose(wanted)
    brick = jnp.sum(
        jnp.where(mine, jnp.where(slot == 0, columns[:, 0:1], columns[:, 1:2]), 0),
        axis=0, keepdims=True,
    )
    chosen = [mine & (rank == j) for j in range(SLOTS)]
    choice = jnp.concatenate([jnp.where(one, 1.0, 0.0) for one in chosen], axis=1)
    lane = iota((OWNERS, RAYS), 1) - lax.rem(lax.axis_index("seg"), 32) * SLOTS
    spots = owner * SLOTS + rank
    bricks = jnp.zeros((OWNERS, RAYS), I32)
    for j in range(SLOTS):
        named = jnp.sum(jnp.where(chosen[j], brick, 0), axis=1, keepdims=True)
        bricks = jnp.where(lane == j, named, bricks)
    cell_x = (cells * 1338) >> 16
    rest = cells - cell_x * 49
    cell_y = (rest * 9363) >> 16
    cell_z = rest - cell_y * 7
    place_x = cell_x.astype(F32) + fracs[0:16]
    place_y = cell_y.astype(F32) + fracs[16:32]
    place_z = cell_z.astype(F32) + fracs[32:48]
    row = iota((SAMP, RAYS), 0)
    extra = jnp.where(row == 11, 1.0, 0.0)
    for k, value in enumerate(basis + [step, brick.astype(F32) + 1.0]):
        extra = jnp.where(row == k, value, extra)
    none = jnp.zeros((SAMP, RAYS), F32)

    def placed(first, second):
        parts = []
        for j in range(SLOTS):
            rows = [none] * 8
            rows[j] = first
            rows[4 + j] = second
            parts.append(jnp.concatenate(rows, axis=0))
        return jnp.concatenate(parts, axis=1)

    return (
        bricks * 256 + spots,
        exact_dot(choice, placed(place_x, place_y), NT),
        exact_dot(choice, placed(place_z, extra), NT),
    )


def greet(axes):
    barrier = pltpu.get_barrier_semaphore()
    total = 0
    for axis, count in axes:
        me = lax.axis_index(axis)

        def hail(turn, carry, axis=axis, count=count, me=me):
            pl.semaphore_signal(
                barrier,
                inc=1,
                device_id={axis: lax.rem(me + turn, count)},
                device_id_type=MESH,
            )
            return carry

        lax.fori_loop(1, count, hail, 0, unroll=9 if count == OWNERS else 7)
        total += count - 1
    return lambda: pl.semaphore_wait(barrier, total)


def send_all(axis, count, source, target, send_sem, recv_sem):
    me = lax.axis_index(axis)

    def one(turn, carry):
        peer = lax.rem(me + turn, count)
        pltpu.make_async_remote_copy(
            src_ref=source(peer),
            dst_ref=target.at[me],
            send_sem=send_sem,
            recv_sem=recv_sem,
            device_id={axis: peer},
            device_id_type=MESH,
        ).start()
        return carry

    lax.fori_loop(1, count, one, 0, unroll=9 if count == OWNERS else 7)


def ring_start(ref, step, send_sems, recv_sems):
    me = lax.axis_index("grp")
    for way in range(2 if step < 4 else 1):
        block = lax.rem(me + GROUPS + (step - 1) * (2 * way - 1), GROUPS)
        pltpu.make_async_remote_copy(
            src_ref=ref.at[block],
            dst_ref=ref.at[block],
            send_sem=send_sems.at[way, step - 1],
            recv_sem=recv_sems.at[way, step - 1],
            device_id={"grp": lax.rem(me + GROUPS + 1 - 2 * way, GROUPS)},
            device_id_type=MESH,
        ).start()


def ring_wait(ref, step, sems, arriving):
    me = lax.axis_index("grp")
    for way in range(2 if step < 4 else 1):
        away = step if arriving else step - 1
        part = ref.at[lax.rem(me + GROUPS + away * (2 * way - 1), GROUPS)]
        pltpu.make_async_copy(part, part, sems.at[way, step - 1]).wait()


def wait_all(target, count, sem):
    part = target.at[pl.ds(0, count - 1)]
    pltpu.make_async_copy(part, part, sem).wait()


def lay_out_bricks(bricks_ref, wide_ref, brick_ref):
    for c in range(COEF, 32):
        for x in range(4):
            wide_ref[x, pl.ds(c, BRICKS, stride=40), :] = jnp.zeros((BRICKS, 128), F32)
    for c in range(COEF):
        for x in range(4):
            wide_ref[x, pl.ds(ROW_OF[c], BRICKS, stride=40), :] = bricks_ref[
                c, :, x * 128 : x * 128 + 128
            ].astype(F32)

    def narrow(turn, carry):
        for k in range(8):
            rows = pl.ds(pl.multiple_of(turn * 320 + k * 40, 8), 32)
            for x in range(4):
                brick_ref[turn * 8 + k, :, x * 128 : x * 128 + 128] = wide_ref[
                    x, rows, :
                ].astype(BF16)
        return carry

    lax.fori_loop(0, BRICKS // 8, narrow, 0)


def unpack(got_ref, half_ref, place_ref, basis_ref):
    left = iota((CHUNKS, 128), 1) < 64
    for half in range(2):
        half_ref[...] = got_ref[:, half, :]
        even = half_ref[pl.ds(0, CHUNKS, stride=2), :]
        odd = half_ref[pl.ds(1, CHUNKS, stride=2), :]
        place_ref[2 * half] = jnp.where(left, even, pltpu.roll(odd, 64, 1))
        place_ref[2 * half + 1] = jnp.where(left, pltpu.roll(even, 64, 1), odd)
    row, lane = iota((128, 1024), 0), iota((128, 1024), 1)
    spread = jnp.where(row == ((lane % 128) // 16) * 16 + lane // 128 + 1, 1.0, 0.0)
    basis = exact_dot(place_ref[3], spread)
    for k in range(8):
        basis_ref[pl.ds(k, CHUNKS, stride=8), :] = basis[:, k * 128 : k * 128 + 128]


def interpolate(brick_ref, place_ref, basis_ref, id_smem, raw_ref):
    lane_group = iota((32, 128), 1) // 16

    def one(chunk):
        hat_x = hat(place_ref[0, pl.ds(chunk, 1), :])
        hat_y = hat(place_ref[1, pl.ds(chunk, 1), :])
        hat_z = hat(place_ref[2, pl.ds(chunk, 1), :])
        plane = jnp.concatenate([hat_y[y : y + 1] * hat_z for y in range(8)], axis=0)
        weights = jnp.concatenate([hat_x[x : x + 1] * plane for x in range(8)], axis=0)
        high, low = split(weights)
        rows = []
        for seg in range(8):
            b = id_smem[chunk // 16, lax.rem(chunk, 16) * 8 + seg]
            rows.append(brick_ref[b])
        values = fast_dot(
            jnp.concatenate(rows, axis=0), jnp.concatenate([high, low], axis=1)
        )
        coef = jnp.zeros((32, 128), F32)
        for seg in range(8):
            part = values[seg * 32 : seg * 32 + 32]
            coef = jnp.where(lane_group == seg, part[:, 0:128] + part[:, 128:256], coef)
        basis = basis_ref[pl.ds(pl.multiple_of(chunk * 8, 8), 8), :]
        raw_ref[0, pl.ds(chunk, 1), :] = coef[24:25]
        for ch in range(3):
            raw_ref[1 + ch, pl.ds(chunk, 1), :] = coef[25 + ch : 26 + ch] * BASIS_0 + jnp.sum(
                coef[8 * ch : 8 * ch + 8] * basis, axis=0, keepdims=True
            )

    def several(turn, carry):
        for k in range(FUNROLL):
            one(turn * FUNROLL + k)
        return carry

    lax.fori_loop(0, CHUNKS // FUNROLL, several, 0)


def segment_sums(raw_ref, extra):
    optical, through, opaque, _ = march(raw_ref[0], extra)
    light = through * opaque
    total = jnp.zeros((CHUNKS, 128), F32)
    row, lane = iota((128, 128), 0), iota((128, 128), 1)
    for v in range(4):
        part = optical if v == 3 else light * sigmoid(raw_ref[1 + v])
        total += exact_dot(part, jnp.where(lane == (row // 16) * 4 + v, 1.0, 0.0))
    return sum(pltpu.roll(total[8 * k : 8 * k + 8], 32 * k, 1) if k else total[0:8] for k in range(4))


def march(density, extra):
    row, lane = iota((128, 128), 0), iota((128, 128), 1)
    same = row // 16 == lane // 16
    step = exact_dot(extra, jnp.where(same & (row % 16 == 9), 1.0, 0.0))
    optical = softplus(density) * step
    before = exact_dot(optical, jnp.where(same & (row < lane), 1.0, 0.0))
    through = jnp.exp(-before)
    remains = jnp.exp(-optical)
    return optical, through, 1.0 - remains, (step, remains)


def plan_chunks(extra):
    across = jnp.transpose(extra)
    named = iota((64, ALL_CHUNKS), 0).astype(F32) + 1.0
    hits = [
        jnp.where(across[seg * 16 + 10 : seg * 16 + 11] == named, 1.0, 0.0) for seg in range(8)
    ]
    earlier = jnp.where(
        iota((ALL_CHUNKS, ALL_CHUNKS), 0) < iota((ALL_CHUNKS, ALL_CHUNKS), 1), 1.0, 0.0
    ).astype(BF16)
    counts = fast_dot(jnp.concatenate(hits, axis=0).astype(BF16), earlier)
    carry = jnp.zeros((64, 1), F32)
    ranks = []
    for seg in range(8):
        ranks.append(counts[seg * 64 : seg * 64 + 64] + carry)
        carry = carry + jnp.sum(hits[seg], axis=1, keepdims=True)
    full = jnp.floor((carry + 7.0) * 0.125)
    lower = jnp.where(iota((64, 64), 1) < iota((64, 64), 0), 1.0, 0.0).astype(BF16)
    full_wide = jnp.broadcast_to(full, (64, 128))
    start = fast_dot(lower, full_wide.astype(BF16))
    end = start + full_wide
    start256 = jnp.concatenate([start, start], axis=1)
    selectors, values = [], []
    row = iota((32, ALL_CHUNKS), 0)
    lane = iota((32, ALL_CHUNKS), 1).astype(F32)
    for seg in range(8):
        place = (
            jnp.sum(hits[seg] * (8.0 * start256 + ranks[seg] + 1.0), axis=0, keepdims=True) - 1.0
        )
        chunk = jnp.floor(place * 0.125)
        inside = place - 8.0 * chunk
        selectors.append(
            jnp.where(iota((TABLE, ALL_CHUNKS), 0).astype(F32) == chunk, 1.0, 0.0).astype(BF16)
        )
        kind = jnp.where(
            row < 8, lane, jnp.where(row < 16, float(seg), jnp.where(row < 24, 1.0, 0.0))
        )
        values.append(jnp.where((row % 8).astype(F32) == inside, kind, 0.0).astype(BF16))
    table = fast_dot(
        jnp.concatenate(values, axis=1), jnp.concatenate(selectors, axis=1), NT
    )
    tile = table[0:8] + (1.0 - table[16:24]) * float(ALL_CHUNKS)
    turn = 16.0 * (iota((8, TABLE), 0).astype(F32) - table[8:16])
    turn = jnp.where(turn < 0.0, turn + 128.0, turn)
    place = iota((64, 128), 1).astype(F32)
    real = iota((64, 128), 0) < BRICKS
    owner = [
        jnp.sum(jnp.where((end <= place + 128.0 * k) & real, 1.0, 0.0), axis=0, keepdims=True)
        for k in range(TABLE // 128)
    ]
    owner = jnp.minimum(jnp.concatenate(owner, axis=1), float(BRICKS - 1))
    number = jnp.sum(full_wide, axis=0, keepdims=True)
    number = jnp.concatenate([number] * (TABLE // 128), axis=1)
    last = jnp.where(iota((8, TABLE), 0) == 0, owner, number)
    return jnp.concatenate([tile, turn, last], axis=0).astype(I32)


def shade_all(raws_ref, extra):
    raw = [
        jnp.concatenate([raws_ref[g, v] for g in range(GROUPS)], axis=0) for v in range(4)
    ]
    _, through, opaque, (step, remains) = march(raw[0], extra)
    light = through * opaque
    radiance = [sigmoid(value) for value in raw[1:]]
    return radiance + [light, through * remains, step * sigmoid(raw[0])]


def sample_gradients(grads_ref, shades_ref, slot_ref, tiles_ref):
    row, lane = iota((128, 128), 0), iota((128, 128), 1)
    grads = jnp.concatenate([grads_ref[g] for g in range(GROUPS)], axis=0)
    for part in range(4):
        for v in range(4):
            spread = jnp.where(row == part * 32 + (lane // 16) * 4 + v, 1.0, 0.0)
            wide = exact_dot(grads, spread)
            for g in range(GROUPS):
                slot_ref[v, pl.ds(g * CHUNKS + part * 8, 8), :] = wide[g * 8 : g * 8 + 8]
    light = shades_ref[3]
    mixed = jnp.zeros((ALL_CHUNKS, 128), F32)
    for v in range(3):
        radiance = shades_ref[v]
        grad_colour = slot_ref[v]
        mixed += grad_colour * radiance
        tiles_ref[pl.ds(1 + v, ALL_CHUNKS, stride=8), :] = (
            grad_colour * light * radiance * (1.0 - radiance)
        )
    later = jnp.where((row // 16 == lane // 16) & (row > lane), 1.0, 0.0)
    grad_optical = shades_ref[4] * mixed - exact_dot(light * mixed, later) + slot_ref[3]
    tiles_ref[pl.ds(0, ALL_CHUNKS, stride=8), :] = grad_optical * shades_ref[5]


def to_rays(sums_ref, spots_ref, rays_ref):
    owner = iota((OWNERS, RAYS), 0)
    slot = iota((16, RAYS), 0) // 4
    for row in range(8):
        across = jnp.transpose(sums_ref[:, row, :])
        high, rest = split(across)
        middle, low = split(across - high.astype(F32))
        for part in range(4):
            for half in range(2):
                s = 2 * (part * 8 + row) + half
                rows = slice(part * 32 + half * 16, part * 32 + half * 16 + 16)
                spots = spots_ref[s]
                hits = jnp.where(spots // SLOTS == owner, 1.0, 0.0).astype(BF16)
                three = fast_dot(
                    jnp.concatenate([high[rows], middle[rows], low[rows]], axis=0), hits
                )
                found = three[0:16] + three[16:32] + three[32:48]
                found = jnp.where(spots % SLOTS == slot, found, 0.0)
                found = found[0:8] + found[8:16]
                rays_ref[s] = found[0:4] + found[4:8]


def composite(colours, taus, target):
    depth, other = iota((OWNERS, OWNERS), 0), iota((OWNERS, OWNERS), 1)
    through = jnp.exp(-exact_dot(jnp.where(other < depth, 1.0, 0.0), taus))
    behind = jnp.where(other > depth, 1.0, 0.0)
    colour, grads = [], []
    grad_tau = jnp.zeros((OWNERS, RAYS), F32)
    for v in range(3):
        contrib = through * colours[v]
        colour.append(jnp.sum(contrib, axis=0, keepdims=True))
        misfit = LOSS_SCALE * (colour[v] - target[v : v + 1])
        grads.append(through * misfit)
        grad_tau -= misfit * exact_dot(behind, contrib)
    return colour, grads + [grad_tau]


def to_slots(grads, spots):
    me = lax.axis_index("seg")
    depth = iota((OWNERS, 128), 0)
    place = iota((OWNERS, 128), 1) - (depth // 16) * 32 - (depth % 2) * 16
    placed = jnp.zeros((OWNERS, 128), F32)
    for j in range(SLOTS):
        here = spots == me * SLOTS + j
        for v in range(4):
            value = jnp.sum(jnp.where(here, grads[v], 0.0), axis=1, keepdims=True)
            placed = jnp.where(place == j * 4 + v, value, placed)
    pick = jnp.where((iota((8, OWNERS), 1) // 2) % 8 == iota((8, OWNERS), 0), 1.0, 0.0)
    return exact_dot(pick, placed)


def render_kernel(
    owner_hbm, slot_hbm, wanted_hbm, cells_hbm, fracs_hbm, angles_hbm, step_hbm, target_hbm,
    bricks_hbm,
    colour_ref, tiles_ref, table_ref,
    owner_ref, slot_ref, wanted_ref, cells_ref, fracs_ref, angles_ref, step_ref, target_ref,
    bricks_ref,
    out_ref, got_ref, wide_ref, brick_ref, half_ref, numbers_ref, ids_ref, spots_ref, id_vmem, id_smem,
    place_ref, raw_ref, basis_ref,
    sums_ref, all_sums_ref, rays_ref, grads_ref,
    places_ref, raws_ref, all_grads_ref, shades_ref, slot_grads_ref,
    load_sems, send_sems, recv_sems, ring_sends, ring_recvs, own_sem,
):
    loads = [
        pltpu.make_async_copy(source, target, load_sems.at[k])
        for k, (source, target) in enumerate(
            [
                (owner_hbm, owner_ref), (slot_hbm, slot_ref), (wanted_hbm, wanted_ref),
                (cells_hbm, cells_ref), (fracs_hbm, fracs_ref), (angles_hbm, angles_ref),
                (step_hbm, step_ref), (target_hbm, target_ref), (bricks_hbm, bricks_ref),
            ]
        )
    ]
    for load in loads:
        load.start()
    met = greet([("seg", OWNERS), ("grp", GROUPS)])
    for load in loads[:8]:
        load.wait()
    me = lax.axis_index("seg")
    group = lax.axis_index("grp")

    def pass_places(step):
        ring_start(places_ref, step, ring_sends.at[0], ring_recvs.at[0])

    def take_places(step):
        ring_wait(places_ref, step, ring_recvs.at[0], True)

    def pass_raws(step):
        ring_start(raws_ref, step, ring_sends.at[1], ring_recvs.at[1])

    def take_raws(step):
        ring_wait(raws_ref, step, ring_recvs.at[1], True)

    numbers, first, second = pack(
        owner_ref[...], slot_ref[...], wanted_ref[...], cells_ref[...], fracs_ref[...],
        ray_basis(angles_ref[...]), step_ref[...],
    )
    out_ref[:, 0, :] = first
    out_ref[:, 1, :] = second
    numbers_ref[:, 0, :] = numbers
    met()
    send_all(
        "seg", OWNERS, lambda peer: numbers_ref.at[peer], ids_ref, send_sems.at[7], recv_sems.at[7]
    )
    ids_ref[me] = numbers_ref[me]
    send_all(
        "seg", OWNERS, lambda peer: out_ref.at[peer], got_ref, send_sems.at[0], recv_sems.at[0]
    )
    got_ref[me] = out_ref[me]
    loads[8].wait()
    lay_out_bricks(bricks_ref, wide_ref, brick_ref)
    wait_all(got_ref, OWNERS, recv_sems.at[0])

    unpack(got_ref, half_ref, place_ref, basis_ref)
    extra = place_ref[3]
    places_ref[group] = place_ref[...]
    pass_places(1)
    wait_all(ids_ref, OWNERS, recv_sems.at[7])
    for half in range(2):
        id_vmem[half : half + 1, :] = jnp.sum(
            ids_ref[32 * half : 32 * half + 32, 0, :] // 256, axis=0, keepdims=True
        )
    ids = pltpu.make_async_copy(id_vmem, id_smem, own_sem)
    ids.start()
    spots_ref[:, 0, :] = lax.rem(ids_ref[:, 0, :], 256)
    ids.wait()
    interpolate(brick_ref, place_ref, basis_ref, id_smem, raw_ref)
    take_places(1)
    pass_places(2)
    raws_ref[group] = raw_ref[...]
    pass_raws(1)
    sums_ref[...] = segment_sums(raw_ref, extra)

    send_all(
        "seg", OWNERS, lambda peer: sums_ref, all_sums_ref, send_sems.at[2], recv_sems.at[2]
    )
    all_sums_ref[me] = sums_ref[...]
    take_places(2)
    pass_places(3)
    take_raws(1)
    pass_raws(2)
    take_places(3)
    pass_places(4)
    take_raws(2)
    pass_raws(3)
    wait_all(all_sums_ref, OWNERS, recv_sems.at[2])
    to_rays(all_sums_ref, spots_ref, rays_ref)
    take_raws(3)
    pass_raws(4)
    colour, grads = composite(
        [rays_ref[:, v, :] for v in range(3)], rays_ref[:, 3, :], target_ref[...]
    )
    for v in range(3):
        colour_ref[v : v + 1, :] = colour[v]
    grads_ref[...] = to_slots(grads, spots_ref[:, 0, :])

    send_all(
        "grp", GROUPS, lambda peer: grads_ref, all_grads_ref, send_sems.at[6], recv_sems.at[6]
    )
    all_grads_ref[group] = grads_ref[...]
    take_places(4)
    all_extra = jnp.concatenate([places_ref[g, 3] for g in range(GROUPS)], axis=0)
    table_ref[...] = plan_chunks(all_extra)
    for g in range(GROUPS):
        for q in range(4):
            tiles_ref[pl.ds(g * CHUNKS * 8 + 4 + q, CHUNKS, stride=8), :] = places_ref[g, q]
    take_raws(4)
    for k, value in enumerate(shade_all(raws_ref, all_extra)):
        shades_ref[k] = value
    wait_all(all_grads_ref, GROUPS, recv_sems.at[6])
    sample_gradients(all_grads_ref, shades_ref, slot_grads_ref, tiles_ref)
    wait_all(got_ref, OWNERS, send_sems.at[0])
    wait_all(ids_ref, OWNERS, send_sems.at[7])
    wait_all(all_sums_ref, OWNERS, send_sems.at[2])
    for step in range(1, 5):
        ring_wait(places_ref, step, ring_sends.at[0], False)
        ring_wait(raws_ref, step, ring_sends.at[1], False)
    wait_all(all_grads_ref, GROUPS, send_sems.at[6])


def render(*operands):
    return pl.pallas_call(
        render_kernel,
        out_shape=(
            jax.ShapeDtypeStruct((3, RAYS), F32),
            jax.ShapeDtypeStruct((ALL_CHUNKS * 8, 128), F32),
            jax.ShapeDtypeStruct((24, TABLE), I32),
        ),
        in_specs=[ANY] * 9,
        out_specs=(VMEM, VMEM, VMEM),
        scratch_shapes=[pltpu.VMEM(x.shape, x.dtype) for x in operands]
        + [
            pltpu.VMEM((OWNERS, 2, 128), F32),
            pltpu.VMEM((OWNERS, 2, 128), F32),
            pltpu.VMEM((4, BRICKS * 40, 128), F32),
            pltpu.VMEM((BRICKS, 32, VOXELS), BF16),
            pltpu.VMEM((OWNERS, 128), F32),
            pltpu.VMEM((OWNERS, 1, 128), I32),
            pltpu.VMEM((OWNERS, 1, 128), I32),
            pltpu.VMEM((OWNERS, 1, 128), I32),
            pltpu.VMEM((2, 128), I32),
            pltpu.SMEM((2, 128), I32),
            pltpu.VMEM((4, CHUNKS, 128), F32),
            pltpu.VMEM((4, CHUNKS, 128), F32),
            pltpu.VMEM((CHUNKS * 8, 128), F32),
            pltpu.VMEM((8, 128), F32),
            pltpu.VMEM((OWNERS, 8, 128), F32),
            pltpu.VMEM((OWNERS, 4, RAYS), F32),
            pltpu.VMEM((8, 128), F32),
            pltpu.VMEM((GROUPS, 4, CHUNKS, 128), F32),
            pltpu.VMEM((GROUPS, 4, CHUNKS, 128), F32),
            pltpu.VMEM((GROUPS, 8, 128), F32),
            pltpu.VMEM((6, ALL_CHUNKS, 128), F32),
            pltpu.VMEM((4, ALL_CHUNKS, 128), F32),
            pltpu.SemaphoreType.DMA((9,)),
            pltpu.SemaphoreType.DMA((8,)),
            pltpu.SemaphoreType.DMA((8,)),
            pltpu.SemaphoreType.DMA((2, 2, 4)),
            pltpu.SemaphoreType.DMA((2, 2, 4)),
            pltpu.SemaphoreType.DMA,
        ],
        compiler_params=pltpu.CompilerParams(
            collective_id=0, has_side_effects=True, vmem_limit_bytes=64 << 20
        ),
        name="render",
    )(*operands)


def gradient_kernel(
    tiles_hbm, table_hbm, colour_hbm, out_hbm, colour_ref,
    tiles_ref, table_smem, total_ref, out_ref, sems, out_sems,
):
    loads = [
        pltpu.make_async_copy(table_hbm, table_smem, sems.at[0]),
        pltpu.make_async_copy(tiles_hbm, tiles_ref.at[pl.ds(0, ALL_CHUNKS * 8)], sems.at[1]),
        pltpu.make_async_copy(colour_hbm, colour_ref, sems.at[2]),
    ]
    for load in loads:
        load.start()
    tiles_ref[pl.ds(ALL_CHUNKS * 8, 8), :] = jnp.zeros((8, 128), F32)
    total_ref[...] = jnp.zeros_like(total_ref)
    for load in loads:
        load.wait()

    lane_group = iota((8, 128), 1) // 16
    pick = lane_group * 16 + iota((8, 128), 0) + 1
    row8 = iota((8, 128), 0)
    first = jnp.where(row8 == 0, 1.0, jnp.where(row8 < 4, BASIS_0, 0.0))

    def one(chunk):
        tile = jnp.zeros((8, 128), F32)
        for p in range(8):
            start = pl.multiple_of(table_smem[p, chunk] * 8, 8)
            part = pltpu.roll(tiles_ref[pl.ds(start, 8), :], table_smem[8 + p, chunk], 1)
            tile = jnp.where(lane_group == p, part, tile)
        hat_x, hat_y, hat_z = hat(tile[4:5]), hat(tile[5:6]), hat(tile[6:7])
        plane = jnp.concatenate([hat_y[y : y + 1] * hat_z for y in range(8)], axis=0)
        basis = jnp.take_along_axis(jnp.broadcast_to(tile[7:8], (8, 128)), pick, axis=1)
        grad = jnp.concatenate([basis * tile[ch : ch + 1] for ch in (1, 2, 3)] + [tile * first], axis=0)
        left = jnp.concatenate(
            [
                jnp.concatenate([grad * hat_x[2 * x + k : 2 * x + k + 1] for x in range(4)], axis=0)
                for k in range(2)
            ],
            axis=1,
        )
        left_high, left_low = split(left)
        high, low = split(plane)
        none = jnp.zeros((64, 128), BF16)

        def both(value):
            return jnp.concatenate(
                [
                    jnp.concatenate([value, none], axis=1),
                    jnp.concatenate([none, value], axis=1),
                ],
                axis=0,
            )

        high, low = both(high), both(low)
        four = fast_dot(
            jnp.concatenate([left_high, left_low], axis=0),
            jnp.concatenate([high, low], axis=0),
            NT,
        )
        return four[0:128, 0:128] + four[0:128, 128:256] + four[128:256, 0:128]

    def several(turn, carry):
        parts = [one(turn * UNROLL + k) for k in range(UNROLL)]
        for k in range(UNROLL):
            b = table_smem[16, turn * UNROLL + k]
            rows = pl.ds(pl.multiple_of(b * BRICK_ROWS, 8), 128)
            total_ref[rows, :] += parts[k]
        return carry

    lax.fori_loop(0, (table_smem[17, 0] + UNROLL - 1) // UNROLL, several, 0)

    outs = []
    for c in range(COEF):
        for x in range(4):
            out_ref[c, :, x * 128 : x * 128 + 128] = total_ref[
                pl.ds(x * 32 + ROW_OF[c], BRICKS, stride=BRICK_ROWS), :
            ]
        outs.append(pltpu.make_async_copy(out_ref.at[c], out_hbm.at[c], out_sems.at[c]))
        outs[c].start()
    for out in outs:
        out.wait()


def gradient(tiles, table, colour):
    return pl.pallas_call(
        gradient_kernel,
        out_shape=(
            jax.ShapeDtypeStruct((COEF, BRICKS, VOXELS), F32),
            jax.ShapeDtypeStruct((3, RAYS), F32),
        ),
        in_specs=[ANY] * 3,
        out_specs=(ANY, VMEM),
        scratch_shapes=[
            pltpu.VMEM((ALL_CHUNKS * 8 + 8, 128), F32),
            pltpu.SMEM((24, TABLE), I32),
            pltpu.VMEM((BRICKS * BRICK_ROWS, 128), F32),
            pltpu.VMEM((COEF, BRICKS, VOXELS), F32),
            pltpu.SemaphoreType.DMA((3,)),
            pltpu.SemaphoreType.DMA((COEF,)),
        ],
        compiler_params=pltpu.CompilerParams(vmem_limit_bytes=64 << 20),
        name="gradient",
    )(tiles, table, colour)


def local(
    bricks, requests, seg_owner, seg_slot, sample_cells, sample_fracs,
    ray_angles, ray_step, pixel_target,
):
    colour, tiles, table = render(
        seg_owner.reshape(1, RAYS),
        seg_slot.reshape(1, RAYS),
        jnp.transpose(requests.reshape(OWNERS, 2)),
        sample_cells.reshape(SAMP, RAYS),
        sample_fracs.reshape(3 * SAMP, RAYS),
        ray_angles,
        ray_step.reshape(1, RAYS),
        pixel_target,
        bricks,
    )
    return gradient(tiles, table, colour)


def solution(mesh):
    return jax.shard_map(
        local,
        mesh=mesh,
        in_specs=(
            P(None, "seg", None),
            P("seg", "grp", None, None),
            P("seg", "grp", None),
            P("seg", "grp"),
            P(None, "seg", "grp"),
            P(None, None, "seg", "grp"),
            P(None, "grp"),
            P("grp"),
            P(None, "grp"),
        ),
        out_specs=(P(None, "seg", None), P(None, "grp")),
        check_vma=False,
    )
```
